32 devices in a mesh: section: 2 (over x), seq: 8 (over z, core), rep: 2 (over y).
Axes of the slice: x: 2, y: 2, z: 4, core: 2. Of those that a mesh axis runs over, the one named last changes fastest.
Arguments:
- signal: bfloat16 [2, 64, 4, 4096], P(None, 'seq', None, 'rep'), may hold values from -200 to 200, as said below
- head_proj: bfloat16 [2, 32, 128, 384], P('section', 'rep'), may hold values from -2 to 6, as said below
- record_start: int32 [2, 4], replicated, may hold values from 0 to 15
- record_pad: int32 [2, 4], replicated, may hold values from 0 to 15
Outputs:
- layer_out: bfloat16 [2, 2, 64, 4, 4096], P('section', None, 'seq', None, 'rep')
The draws below stay inside these ranges and needn't reach their ends.
Inputs may be any that keep to these rules, and one draw needn't show every extreme that they name: `signal`: finite. `head_proj`: finite.
All inputs are finite; a program needn't handle non-finite values.
Results may differ from the reference program's by a relative error of at most 0.015.
The reference program's roundings to bfloat16 on the way count: a program that leaves them out, or rounds other values in their place, can miss the bound.
Values may be sent and summed in bfloat16 or wider, within the bound.
No kernel may reach another device: no remote copies, remote signals or barrier semaphores. Data moves between devices by JAX's collectives and lax.ppermute only.
A program may use at most 64 MiB of HBM per device.

```python
import math
import jax
import jax.numpy as jnp
from jax import lax

HEADS = 32
HEAD = 128
MB = 2
STATIONS = 4
WIN = 4
TIMES = 64
LAYERS = 2


def draw_signal(key, part):
    streams = jax.random.split(jax.random.fold_in(key, 11), 4)
    shape_heads = (MB, TIMES, STATIONS, HEADS, HEAD)
    base_draw = jnp.clip(jax.random.normal(streams[0], shape_heads, jnp.float32), -6.0, 6.0)
    row_scale = jnp.exp(jax.random.uniform(streams[1], (MB, TIMES, STATIONS, 1, 1), jnp.float32, math.log(0.03), math.log(0.3)))
    slope = jax.random.uniform(streams[2], (MB, TIMES, STATIONS, 1, 1), jnp.float32, -math.log(16.0), math.log(16.0))
    position = (jnp.arange(HEADS, dtype=jnp.float32) + 0.5) / HEADS - 0.5
    tilt = jnp.exp(slope * position[None, None, None, :, None])
    head_scale = jnp.exp(jax.random.uniform(streams[3], (MB, TIMES, STATIONS, HEADS, 1), jnp.float32, 0.0, math.log(3.0)))
    shaped = base_draw * row_scale * tilt * head_scale
    return shaped.reshape(MB, TIMES, STATIONS, HEADS * HEAD).astype(jnp.bfloat16)


def draw_head_proj(key, part):
    streams = jax.random.split(jax.random.fold_in(key, 23), 3)
    base_draw = jnp.clip(jax.random.normal(streams[0], (LAYERS, HEADS, HEAD, 3 * HEAD), jnp.float32), -6.0, 6.0) / math.sqrt(HEAD)
    value_gain = jnp.exp(jax.random.uniform(streams[2], (LAYERS, HEADS, 1, 1), jnp.float32, -math.log(3.0), math.log(3.0)))
    is_value = (jnp.arange(3 * HEAD) >= 2 * HEAD)[None, None, None, :]
    column_gain = jnp.where(is_value, value_gain, 1.0)
    scaled = base_draw * column_gain
    return scaled.astype(jnp.bfloat16)


def touch_ends(array, stream_key, smallest, top_value):
    longest = array.shape.index(max(array.shape))
    spots = []
    for shift in (0, 1):
        where = [jax.random.randint(jax.random.fold_in(stream_key, axis), (), 0, length) for axis, length in enumerate(array.shape)]
        where[longest] = (where[longest] + shift) % array.shape[longest]
        spots.append(tuple(where))
    return array.at[spots[0]].set(smallest).at[spots[1]].set(top_value)


def setup_inputs(seed: int = 0) -> dict:
    key_of = jax.random.split(jax.random.key(seed), 5)
    return {
        "signal": draw_signal(jax.random.fold_in(key_of[4], 71), 0),
        "head_proj": draw_head_proj(jax.random.fold_in(key_of[4], 71), 0),
        "record_start": touch_ends(jax.random.randint(key_of[2], (MB, STATIONS), 0, TIMES // 4), jax.random.fold_in(key_of[2], 1), 0, (TIMES // 4) - 1).astype(jnp.int32),
        "record_pad": touch_ends(jax.random.randint(key_of[3], (MB, STATIONS), 0, TIMES // 4), jax.random.fold_in(key_of[3], 1), 0, (TIMES // 4) - 1).astype(jnp.int32),
    }


def masked_softmax(scores, allowed):
    scores = jnp.where(allowed, scores, -1e+30)
    row_top = lax.optimization_barrier(jnp.max(scores, axis=-1, keepdims=True))
    weights = jnp.where(allowed, jnp.exp(scores - row_top), 0.0)
    return (weights / lax.optimization_barrier(jnp.sum(weights, axis=-1, keepdims=True))).astype(jnp.bfloat16)

def one_layer(hidden, weights, first_step, pad_steps):
    widened = hidden.astype(jnp.float32)
    squares = lax.optimization_barrier(jnp.sum(widened * widened, axis=-1, keepdims=True))
    normed = (widened * lax.rsqrt(squares / (HEADS * HEAD) + 1e-06)).astype(jnp.bfloat16)
    heads_split = normed.reshape(TIMES, STATIONS, HEADS, HEAD).astype(jnp.float32)
    projected = jnp.einsum('tshd,hde->tshe', heads_split, weights.astype(jnp.float32)).astype(jnp.bfloat16)
    time_steps = jnp.arange(TIMES, dtype=jnp.int32)
    is_valid = (time_steps[None, :] >= first_step[:, None]) & (time_steps[None, :] < TIMES - pad_steps[:, None])
    blocks = TIMES // WIN
    offset = jnp.arange(3 * WIN)[None, :] - jnp.arange(WIN)[:, None]
    in_band = (offset >= 0) & (offset <= 2 * WIN)
    centre = offset == WIN
    padded_valid = jnp.pad(is_valid, ((0, 0), (WIN, WIN))).reshape(STATIONS, blocks + 2, WIN).transpose(1, 0, 2)
    key_valid = jnp.concatenate([padded_valid[:-2], padded_valid[1:-1], padded_valid[2:]], axis=2)
    time_allowed = in_band[None, None] & key_valid[:, :, None, :] | centre[None, None]
    station_allowed = is_valid.T[:, None, :] | jnp.eye(STATIONS, dtype=bool)[None]

    def per_head(per_column):
        queries = per_column[..., :HEAD]
        key_rows = per_column[..., HEAD:2 * HEAD]
        value_rows = per_column[..., 2 * HEAD:]
        key_pad = jnp.pad(key_rows, ((WIN, WIN), (0, 0), (0, 0))).reshape(blocks + 2, WIN, STATIONS, HEAD)
        value_pad = jnp.pad(value_rows, ((WIN, WIN), (0, 0), (0, 0))).reshape(blocks + 2, WIN, STATIONS, HEAD)
        key_blocks = jnp.concatenate([key_pad[:-2], key_pad[1:-1], key_pad[2:]], axis=1)
        value_blocks = jnp.concatenate([value_pad[:-2], value_pad[1:-1], value_pad[2:]], axis=1)
        query_blocks = queries.reshape(blocks, WIN, STATIONS, HEAD)
        scores = jnp.einsum('nasd,nbsd->nsab', query_blocks.astype(jnp.float32), key_blocks.astype(jnp.float32)) / math.sqrt(HEAD)
        time_weights = masked_softmax(scores, time_allowed)
        along_time = jnp.einsum('nsab,nbsd->nasd', time_weights.astype(jnp.float32), value_blocks.astype(jnp.float32)).reshape(TIMES, STATIONS, HEAD)
        station_scores = jnp.einsum('tsd,tzd->tsz', queries.astype(jnp.float32), key_rows.astype(jnp.float32)) / math.sqrt(HEAD)
        station_weights = masked_softmax(station_scores, station_allowed)
        across = jnp.einsum('tsz,tzd->tsd', station_weights.astype(jnp.float32), value_rows.astype(jnp.float32))
        return along_time + across
    head_outs = lax.map(per_head, projected.transpose(2, 0, 1, 3))
    updates = head_outs.transpose(1, 2, 0, 3).reshape(TIMES, STATIONS, HEADS * HEAD)
    return (widened + updates).astype(jnp.bfloat16)

def reference(signal, head_proj, record_start, record_pad):
    results = []
    for micro_index in range(MB):
        hidden = signal[micro_index]
        stacked = []
        for layer_index in range(LAYERS):
            hidden = one_layer(hidden, head_proj[layer_index], record_start[micro_index], record_pad[micro_index])
            stacked.append(hidden)
        results.append(jnp.stack(stacked))
    return jnp.stack(results, axis=1)
```

```python
import math

import jax
import jax.numpy as jnp
from jax import lax
from jax.experimental import pallas as pl
from jax.experimental.pallas import tpu as pltpu
from jax.sharding import PartitionSpec as P

HEADS = 32
HEAD = 128
WIN = 4
GROUP = 4
EPS = 1e-06
BIG = 1e30

VMEM = pl.BlockSpec(memory_space=pltpu.VMEM)
SMEM = pl.BlockSpec(memory_space=pltpu.SMEM)
PARAMS = pltpu.CompilerParams(vmem_limit_bytes=48 * 1024 * 1024)


def cost(flops, moved):
    return pl.CostEstimate(flops=flops, bytes_accessed=moved, transcendentals=0)


def eye(rows):
    return (
        lax.broadcasted_iota(jnp.int32, (rows, rows), 0)
        == lax.broadcasted_iota(jnp.int32, (rows, rows), 1)
    ).astype(jnp.float32)


def squares_row(rows):
    gram = lax.dot_general(
        rows, rows, (((1,), (1,)), ((), ())), preferred_element_type=jnp.float32
    )
    return jnp.sum(gram * eye(rows.shape[0]), axis=0, keepdims=True)


def first_kernel(signal_ref, own_ref, squares_ref):
    micro, steps, stations, _ = signal_ref.shape
    rows_micro = steps * stations
    for m in range(micro):
        for t in range(0, steps, 2):
            own_ref[pl.ds(m * rows_micro + t * stations, 2 * stations), :] = jnp.concatenate(
                [signal_ref[m, t].astype(jnp.float32), signal_ref[m, t + 1].astype(jnp.float32)],
                axis=0,
            ).astype(jnp.bfloat16)
    squares_ref[...] = jnp.zeros(squares_ref.shape, jnp.float32)
    rows = own_ref[...]
    squares_ref[0:1, 0 : rows.shape[0]] = squares_row(rows)


def norm_kernel(own_ref, partner_ref, normed_ref, head_ref, tail_ref, *, micro, edge):
    rows = own_ref[...]
    count = rows.shape[0]
    total = squares_row(rows) + partner_ref[0:1, 0:count]
    factor = lax.rsqrt(total / (HEADS * HEAD) + EPS)
    column = jnp.sum(eye(count) * factor, axis=1, keepdims=True)
    normed = (rows.astype(jnp.float32) * column).astype(jnp.bfloat16)
    normed_ref[...] = normed
    rows_micro = count // micro
    for m in range(micro):
        base = m * rows_micro
        head_ref[m * edge : (m + 1) * edge, :] = normed[base : base + edge]
        tail_ref[m * edge : (m + 1) * edge, :] = normed[base + rows_micro - edge : base + rows_micro]


def masks(first_step_ref, pad_ref, m, time_base, total_steps, steps, stations):
    keys = (steps + 2 * WIN) * stations
    columns = GROUP * steps * stations
    key = lax.broadcasted_iota(jnp.int32, (keys, columns), 0)
    query = lax.broadcasted_iota(jnp.int32, (keys, columns), 1) % (steps * stations)
    key_station, query_station = key % stations, query % stations
    key_time, query_time = key // stations - WIN, query // stations
    first = jnp.zeros((keys, columns), jnp.int32)
    last = jnp.zeros((keys, columns), jnp.int32)
    for s in range(stations):
        first = jnp.where(key_station == s, first_step_ref[m, s], first)
        last = jnp.where(key_station == s, total_steps - pad_ref[m, s], last)
    step = time_base + key_time
    recorded = (step >= first) & (step < last)
    same_station = key_station == query_station
    same_time = key_time == query_time
    near = jnp.abs(key_time - query_time) <= WIN
    time_bias = jnp.where(same_station & near & (recorded | same_time), 0.0, -BIG)
    station_bias = jnp.where(same_time & (recorded | same_station), 0.0, -BIG)
    own = slice(WIN * stations, (WIN + steps) * stations)
    return time_bias, station_bias[own]


def softmax_columns(scores):
    grown = jnp.exp(scores - jnp.max(scores, axis=0, keepdims=True))
    return (grown * (1.0 / jnp.sum(grown, axis=0, keepdims=True))).astype(jnp.bfloat16)


def layer_kernel(
    place_ref, first_ref, pad_ref, hidden_ref, normed_ref, left_ref, right_ref, weights_ref,
    kept_ref, out_ref, squares_ref, *, tick, micro, steps, stations, total_steps, last,
):
    rows_micro = steps * stations
    edge = WIN * stations
    own_rows = micro * rows_micro
    heads_dev = weights_ref.shape[1]

    def write(m, head, values):
        lanes = slice(head * HEAD, (head + 1) * HEAD)
        if last:
            for t in range(steps):
                out_ref[0, m, t, :, lanes] = values[t * stations : (t + 1) * stations].astype(jnp.bfloat16)
        else:
            out_ref[m * rows_micro : (m + 1) * rows_micro, lanes] = values.astype(jnp.bfloat16)

    @pl.when(place_ref[0] == tick)
    def _():
        time_base = place_ref[1]
        bias = [
            masks(first_ref, pad_ref, m, time_base, total_steps, steps, stations)
            for m in range(micro)
        ]
        sums = [jnp.zeros((rows_micro, HEAD), jnp.float32) for _ in range(micro)]
        for group in range(heads_dev // GROUP):
            queries, keys, values = [], [], []
            for j in range(GROUP):
                head = group * GROUP + j
                lanes = slice(head * HEAD, (head + 1) * HEAD)
                tokens = jnp.concatenate(
                    [normed_ref[:, lanes], left_ref[:, lanes], right_ref[:, lanes]], axis=0
                )
                projected = jnp.dot(
                    tokens, weights_ref[0, head], preferred_element_type=jnp.float32
                ).astype(jnp.bfloat16)
                queries.append(projected[:own_rows, :HEAD])
                keys.append(projected[:, HEAD : 2 * HEAD])
                values.append(projected[:, 2 * HEAD :])
            for m in range(micro):
                time_bias, station_bias = bias[m]
                own = slice(m * rows_micro, (m + 1) * rows_micro)
                left = slice(own_rows + m * edge, own_rows + (m + 1) * edge)
                right = slice(own_rows + (micro + m) * edge, own_rows + (micro + m + 1) * edge)
                blank = jnp.zeros((rows_micro, HEAD), jnp.bfloat16)
                spread = jnp.concatenate(
                    [
                        jnp.concatenate(
                            [queries[j][own] if i == j else blank for i in range(GROUP)], axis=1
                        )
                        for j in range(GROUP)
                    ],
                    axis=0,
                )
                all_keys = jnp.concatenate(
                    [
                        jnp.concatenate([k[left], k[own], k[right]], axis=0) for k in keys
                    ],
                    axis=1,
                )
                scores = lax.dot_general(
                    all_keys, spread, (((1,), (1,)), ((), ())), preferred_element_type=jnp.float32
                ) * (1.0 / math.sqrt(HEAD))
                time_weights = softmax_columns(scores + time_bias)
                station_weights = softmax_columns(scores[edge : edge + rows_micro] + station_bias)
                both = jnp.concatenate([time_weights, station_weights], axis=0).T
                for j in range(GROUP):
                    head = group * GROUP + j
                    v = values[j]
                    mixed = jnp.dot(
                        both[j * rows_micro : (j + 1) * rows_micro],
                        jnp.concatenate([v[left], v[own], v[right], v[own]], axis=0),
                        preferred_element_type=jnp.float32,
                    )
                    lanes = slice(head * HEAD, (head + 1) * HEAD)
                    result = hidden_ref[own, lanes].astype(jnp.float32) + mixed
                    write(m, head, result)
                    if not last:
                        rounded = result.astype(jnp.bfloat16).astype(jnp.float32)
                        sums[m] = sums[m] + rounded * rounded
        if not last:
            column = jnp.sum(jnp.concatenate(sums, axis=0), axis=1, keepdims=True)
            squares_ref[...] = jnp.zeros(squares_ref.shape, jnp.float32)
            squares_ref[0:1, 0:own_rows] = jnp.sum(eye(own_rows) * column, axis=0, keepdims=True)

    @pl.when(place_ref[0] != tick)
    def _():
        for m in range(micro):
            for head in range(heads_dev):
                lanes = slice(head * HEAD, (head + 1) * HEAD)
                write(m, head, kept_ref[m * rows_micro : (m + 1) * rows_micro, lanes].astype(jnp.float32))
        if not last:
            squares_ref[...] = jnp.zeros(squares_ref.shape, jnp.float32)


def body(signal, head_proj, record_start, record_pad):
    section_count = lax.axis_size("section")
    seq_count = lax.axis_size("seq")
    rep_count = lax.axis_size("rep")
    section_index = lax.axis_index("section")
    micro, steps, stations, features = signal.shape
    total_steps = steps * seq_count
    own_rows = micro * steps * stations
    edge = WIN * stations
    place = jnp.stack([section_index, lax.axis_index("seq") * steps]).astype(jnp.int32)
    bf16, f32 = jnp.bfloat16, jnp.float32
    own_shape = jax.ShapeDtypeStruct((own_rows, features), bf16)
    edge_shape = jax.ShapeDtypeStruct((micro * edge, features), bf16)
    squares_shape = jax.ShapeDtypeStruct((8, 128), f32)
    own_bytes = own_rows * features * 2

    own, squares = pl.pallas_call(
        first_kernel,
        in_specs=[VMEM],
        out_specs=[VMEM, VMEM],
        out_shape=[own_shape, squares_shape],
        compiler_params=PARAMS,
        cost_estimate=cost(2 * own_rows * own_rows * features, 2 * own_bytes),
        name="first",
    )(signal)
    kept = own
    partner = lax.ppermute(
        squares, ("section", "rep"), [(r, (r + 1) % rep_count) for r in range(rep_count)]
    )
    for tick in range(section_count):
        last = tick + 1 == section_count
        normed, head_rows, tail_rows = pl.pallas_call(
            lambda *refs: norm_kernel(*refs, micro=micro, edge=edge),
            in_specs=[VMEM, VMEM],
            out_specs=[VMEM] * 3,
            out_shape=[own_shape, edge_shape, edge_shape],
            compiler_params=PARAMS,
            cost_estimate=cost(2 * own_rows * own_rows * features, 3 * own_bytes),
            name="norm",
        )(own, partner)
        base = tick * seq_count
        left = lax.ppermute(
            tail_rows, ("section", "seq"), [(base + i, base + i + 1) for i in range(seq_count - 1)]
        )
        right = lax.ppermute(
            head_rows, ("section", "seq"), [(base + i + 1, base + i) for i in range(seq_count - 1)]
        )
        out_shape = (
            [jax.ShapeDtypeStruct((1,) + signal.shape, bf16)] if last else [own_shape]
        ) + [squares_shape]

        def kernel(*refs, tick=tick, last=last):
            layer_kernel(
                *refs, tick=tick, micro=micro, steps=steps, stations=stations,
                total_steps=total_steps, last=last,
            )

        kept, squares = pl.pallas_call(
            kernel,
            in_specs=[SMEM] * 3 + [VMEM] * 6,
            out_specs=[VMEM, VMEM],
            out_shape=out_shape,
            compiler_params=PARAMS,
            cost_estimate=cost(4 * own_rows * features * 3 * HEAD, 16 * own_bytes),
            name="layer",
        )(place, record_start, record_pad, own, normed, left, right, head_proj, kept)
        if not last:
            across = [(tick * rep_count + r, (tick + 1) * rep_count + r) for r in range(rep_count)]
            own = lax.ppermute(
                kept, "section", [(tick, tick + 1)]
            )
            partner = lax.ppermute(
                squares,
                ("section", "rep"),
                [(a, (tick + 1) * rep_count + (b + 1) % rep_count) for a, b in across],
            )
    return kept


def solution(mesh):
    return jax.shard_map(
        body,
        mesh=mesh,
        in_specs=(P(None, "seq", None, "rep"), P("section", "rep", None, None), P(), P()),
        out_specs=P("section", None, "seq", None, "rep"),
        check_vma=False,
    )
```

```python
import math

import jax
import jax.numpy as jnp
from jax import lax
from jax.experimental import pallas as pl
from jax.experimental.pallas import tpu as pltpu
from jax.sharding import PartitionSpec as P

HEADS = 32
HEAD = 128
WIN = 4
GROUP = 4
EPS = 1e-06
BIG = 1e30

HBM = pl.BlockSpec(memory_space=pltpu.HBM)
VMEM = pl.BlockSpec(memory_space=pltpu.VMEM)
PARAMS = pltpu.CompilerParams(vmem_limit_bytes=16 * 1024 * 1024)


def cost(flops, moved):
    return pl.CostEstimate(flops=flops, bytes_accessed=moved, transcendentals=0)


def first_kernel(
    signal_hbm, weights_hbm, first_hbm, pad_hbm, own_ref, head_ref, tail_ref, squares_ref,
    weights_ref, time_ref, station_ref, signal_ref, first_ref, pad_ref, arrived,
    *, total_steps,
):
    copies = [
        pltpu.make_async_copy(signal_hbm, signal_ref, arrived.at[0]),
        pltpu.make_async_copy(first_hbm, first_ref, arrived.at[1]),
        pltpu.make_async_copy(pad_hbm, pad_ref, arrived.at[2]),
        pltpu.make_async_copy(weights_hbm, weights_ref, arrived.at[3]),
    ]
    for copy in copies:
        copy.start()
    micro, steps, stations, _ = signal_ref.shape
    rows_micro = steps * stations
    edge = WIN * stations
    copies[0].wait()
    for m in range(micro):
        for t in range(0, steps, 2):
            own_ref[pl.ds(m * rows_micro + t * stations, 2 * stations), :] = jnp.concatenate(
                [signal_ref[m, t].astype(jnp.float32), signal_ref[m, t + 1].astype(jnp.float32)],
                axis=0,
            ).astype(jnp.bfloat16)
    for m in range(micro):
        base = m * rows_micro
        head_ref[m * edge : (m + 1) * edge, :] = own_ref[base : base + edge, :]
        tail_ref[m * edge : (m + 1) * edge, :] = own_ref[base + rows_micro - edge : base + rows_micro, :]
    rows = own_ref[...]
    count = rows.shape[0]
    gram = lax.dot_general(
        rows, rows, (((1,), (1,)), ((), ())), preferred_element_type=jnp.float32
    )
    squares_ref[...] = jnp.zeros(squares_ref.shape, jnp.float32)
    squares_ref[pl.ds(lax.axis_index("seq"), 1), 0:count] = jnp.sum(
        jnp.where(same(count), gram, 0.0), axis=0, keepdims=True
    )
    copies[1].wait()
    copies[2].wait()
    fill_masks(first_ref, pad_ref, time_ref, station_ref, steps, stations, total_steps)
    copies[3].wait()


def same(count):
    return lax.broadcasted_iota(jnp.int32, (count, count), 0) == lax.broadcasted_iota(
        jnp.int32, (count, count), 1
    )


def fill_masks(first_ref, pad_ref, time_ref, station_ref, steps, stations, total_steps):
    time_base = lax.axis_index("seq") * steps
    keys = (steps + 2 * WIN) * stations
    columns = GROUP * steps * stations
    key = lax.broadcasted_iota(jnp.int32, (keys, columns), 0)
    query = lax.broadcasted_iota(jnp.int32, (keys, columns), 1) % (steps * stations)
    key_station, query_station = key % stations, query % stations
    key_time, query_time = key // stations - WIN, query // stations
    same_station = key_station == query_station
    same_time = key_time == query_time
    near = jnp.abs(key_time - query_time) <= WIN
    step = time_base + key_time
    for m in range(time_ref.shape[0]):
        first = jnp.zeros((keys, columns), jnp.int32)
        pad = jnp.zeros((keys, columns), jnp.int32)
        for s in range(stations):
            first = jnp.where(key_station == s, first_ref[m, s], first)
            pad = jnp.where(key_station == s, pad_ref[m, s], pad)
        recorded = (step >= first) & (step < total_steps - pad)
        time_ref[m] = jnp.where(same_station & near & (recorded | same_time), 0.0, -BIG)
        station_ref[m] = jnp.where(same_time & (recorded | same_station), 0.0, -BIG)[
            WIN * stations : (WIN + steps) * stations
        ]


def softmax_columns(scores):
    grown = jnp.exp(scores - jnp.max(scores, axis=0, keepdims=True))
    return (grown * (1.0 / jnp.sum(grown, axis=0, keepdims=True))).astype(jnp.bfloat16)


def layer_kernel(
    own_ref, left_ref, right_ref, own_squares_ref, left_squares_ref, right_squares_ref,
    time_ref, station_ref, weights_ref, kept_ref, out_ref, *refs, tick, micro, steps, stations, last,
):
    if last:
        normed_ref, projected_ref = refs
    else:
        head_ref, tail_ref, squares_ref, normed_ref, projected_ref = refs
    rows_micro = steps * stations
    edge = WIN * stations
    reach = rows_micro + 2 * edge
    own_rows = micro * rows_micro
    all_rows = micro * reach
    heads_dev = weights_ref.shape[1]
    active = lax.axis_index("section") == tick
    bf16, f32 = jnp.bfloat16, jnp.float32

    def write(m, lanes, values):
        if last:
            for t in range(steps):
                out_ref[0, m, t, :, lanes] = values[t * stations : (t + 1) * stations].astype(bf16)
        else:
            values = values.astype(bf16)
            out_ref[m * rows_micro : (m + 1) * rows_micro, lanes] = values
            head_ref[m * edge : (m + 1) * edge, lanes] = values[:edge]
            tail_ref[m * edge : (m + 1) * edge, lanes] = values[rows_micro - edge :]

    def column_squares():
        seq = lax.axis_index("seq")
        if tick == 0:
            before, after = jnp.maximum(seq - 1, 0), jnp.minimum(seq + 1, lax.axis_size("seq") - 1)
            sources = (
                left_squares_ref[pl.ds(before, 1), :],
                own_squares_ref[pl.ds(seq, 1), :],
                right_squares_ref[pl.ds(after, 1), :],
            )
        else:
            sources = (left_squares_ref[0:1, :], own_squares_ref[0:1, :], right_squares_ref[0:1, :])
        row = lax.broadcasted_iota(jnp.int32, (all_rows, 128), 0)
        lane = lax.broadcasted_iota(jnp.int32, (all_rows, 128), 1)
        place, base = row % reach, (row // reach) * rows_micro
        picked = jnp.where(
            place < edge,
            jnp.where(lane == base + place + rows_micro - edge, sources[0], 0.0),
            jnp.where(
                place < edge + rows_micro,
                jnp.where(lane == base + place - edge, sources[1], 0.0),
                jnp.where(lane == base + place - edge - rows_micro, sources[2], 0.0),
            ),
        )
        return jnp.sum(picked, axis=1, keepdims=True)

    @pl.when(active)
    def _():
        raw = []
        for m in range(micro):
            raw += [
                left_ref[m * edge : (m + 1) * edge, :],
                own_ref[m * rows_micro : (m + 1) * rows_micro, :],
                right_ref[m * edge : (m + 1) * edge, :],
            ]
        raw = jnp.concatenate(raw, axis=0)
        total = column_squares()
        if tick > 0:
            mine = jnp.zeros((all_rows, HEAD), f32)
            for head in range(heads_dev):
                part = raw[:, head * HEAD : (head + 1) * HEAD].astype(f32)
                mine = mine + part * part
            total = total + jnp.sum(mine, axis=1, keepdims=True)
        factor = lax.rsqrt(total / (HEADS * HEAD) + EPS)
        for head in range(heads_dev):
            lanes = slice(head * HEAD, (head + 1) * HEAD)
            normed_ref[:, lanes] = (raw[:, lanes].astype(f32) * factor).astype(bf16)
        width = 3 * HEAD
        for head in range(heads_dev):
            projected_ref[:, head * width : (head + 1) * width] = jnp.dot(
                normed_ref[:, head * HEAD : (head + 1) * HEAD],
                weights_ref[0, head],
                preferred_element_type=f32,
            ).astype(bf16)
        pairs = [(g, m) for g in range(heads_dev // GROUP) for m in range(micro)]
        blank = jnp.zeros((rows_micro, HEAD), bf16)
        scores = []
        for g, m in pairs:
            at = [(g * GROUP + j) * width for j in range(GROUP)]
            first = m * reach
            spread = jnp.concatenate(
                [
                    jnp.concatenate(
                        [
                            projected_ref[first + edge : first + edge + rows_micro, at[j] : at[j] + HEAD]
                            if i == j
                            else blank
                            for i in range(GROUP)
                        ],
                        axis=1,
                    )
                    for j in range(GROUP)
                ],
                axis=0,
            )
            keys = jnp.concatenate(
                [projected_ref[first : first + reach, a + HEAD : a + 2 * HEAD] for a in at], axis=1
            )
            scores.append(
                lax.dot_general(
                    keys, spread, (((1,), (1,)), ((), ())), preferred_element_type=f32
                )
                * (1.0 / math.sqrt(HEAD))
            )
        mixes = []
        for (g, m), score in zip(pairs, scores):
            time_weights = softmax_columns(score + time_ref[m])
            station_weights = softmax_columns(score[edge : edge + rows_micro] + station_ref[m])
            mixes.append(jnp.concatenate([time_weights, station_weights], axis=0).T)
        sums = [jnp.zeros((rows_micro, HEAD), f32) for _ in range(micro)]
        for (g, m), mix in zip(pairs, mixes):
            first = m * reach
            for j in range(GROUP):
                head = g * GROUP + j
                at = head * width + 2 * HEAD
                mixed = jnp.dot(
                    mix[j * rows_micro : (j + 1) * rows_micro],
                    jnp.concatenate(
                        [
                            projected_ref[first : first + reach, at : at + HEAD],
                            projected_ref[first + edge : first + edge + rows_micro, at : at + HEAD],
                        ],
                        axis=0,
                    ),
                    preferred_element_type=f32,
                )
                lanes = slice(head * HEAD, (head + 1) * HEAD)
                own = slice(m * rows_micro, (m + 1) * rows_micro)
                result = own_ref[own, lanes].astype(f32) + mixed
                write(m, lanes, result)
                if not last:
                    rounded = result.astype(bf16).astype(f32)
                    sums[m] = sums[m] + rounded * rounded
        if not last:
            column = jnp.sum(jnp.concatenate(sums, axis=0), axis=1, keepdims=True)
            squares_ref[...] = jnp.zeros(squares_ref.shape, f32)
            squares_ref[0:1, 0:own_rows] = jnp.sum(
                jnp.where(same(own_rows), column, 0.0), axis=0, keepdims=True
            )

    @pl.when(jnp.logical_not(active))
    def _():
        for m in range(micro):
            for head in range(heads_dev):
                lanes = slice(head * HEAD, (head + 1) * HEAD)
                write(m, lanes, kept_ref[m * rows_micro : (m + 1) * rows_micro, lanes].astype(f32))
        if not last:
            squares_ref[...] = jnp.zeros(squares_ref.shape, f32)


def body(signal, head_proj, record_start, record_pad):
    section_count = lax.axis_size("section")
    seq_count = lax.axis_size("seq")
    rep_count = lax.axis_size("rep")
    micro, steps, stations, features = signal.shape
    heads_dev = head_proj.shape[1]
    rows_micro = steps * stations
    own_rows = micro * rows_micro
    edge = WIN * stations
    reach = rows_micro + 2 * edge
    bf16, f32 = jnp.bfloat16, jnp.float32
    own_shape = jax.ShapeDtypeStruct((own_rows, features), bf16)
    edge_shape = jax.ShapeDtypeStruct((micro * edge, features), bf16)
    squares_shape = jax.ShapeDtypeStruct((8, 128), f32)
    own_bytes = own_rows * features * 2
    columns = GROUP * rows_micro

    own, head_rows, tail_rows, squares, weights, time_bias, station_bias = pl.pallas_call(
        lambda *refs: first_kernel(*refs, total_steps=steps * seq_count),
        in_specs=[HBM] * 4,
        out_specs=[VMEM] * 7,
        out_shape=[
            own_shape,
            edge_shape,
            edge_shape,
            jax.ShapeDtypeStruct((seq_count, 128), f32),
            jax.ShapeDtypeStruct(head_proj.shape, bf16),
            jax.ShapeDtypeStruct((micro, reach, columns), f32),
            jax.ShapeDtypeStruct((micro, rows_micro, columns), f32),
        ],
        scratch_shapes=[
            pltpu.VMEM(signal.shape, bf16),
            pltpu.SMEM(record_start.shape, jnp.int32),
            pltpu.SMEM(record_pad.shape, jnp.int32),
            pltpu.SemaphoreType.DMA((4,)),
        ],
        compiler_params=PARAMS,
        cost_estimate=cost(2 * own_rows * own_rows * features, 3 * own_bytes),
        name="first",
    )(*[pltpu.with_memory_space_constraint(x, pltpu.HBM) for x in (signal, head_proj, record_start, record_pad)])

    def to_next(block, source, target, step):
        route = [
            (source * seq_count + i, target * seq_count + i + step)
            for i in range(seq_count)
            if 0 <= i + step < seq_count
        ]
        return lax.ppermute(block, ("section", "seq"), route)

    def to_next_other(block, source, target, step):
        route = [
            (
                (source * seq_count + i) * rep_count + r,
                (target * seq_count + i + step) * rep_count + (r + 1) % rep_count,
            )
            for i in range(seq_count)
            if 0 <= i + step < seq_count
            for r in range(rep_count)
        ]
        return lax.ppermute(block, ("section", "seq", "rep"), route)

    helper = 1 if section_count > 1 else 0
    left = to_next(tail_rows, helper, 0, 1)
    right = to_next(head_rows, helper, 0, -1)
    own_squares = left_squares = right_squares = lax.psum(squares, ("seq", "rep"))
    kept = own
    for tick in range(section_count):
        last = tick + 1 == section_count

        def kernel(*refs, tick=tick, last=last):
            layer_kernel(*refs, tick=tick, micro=micro, steps=steps, stations=stations, last=last)

        out_shape = (
            [jax.ShapeDtypeStruct((1,) + signal.shape, bf16)]
            if last
            else [own_shape, edge_shape, edge_shape, squares_shape]
        )
        kept, *sent = pl.pallas_call(
            kernel,
            in_specs=[VMEM] * 10,
            out_specs=[VMEM] * len(out_shape),
            out_shape=out_shape,
            scratch_shapes=[
                pltpu.VMEM((micro * reach, features), bf16),
                pltpu.VMEM((micro * reach, heads_dev * 3 * HEAD), bf16),
            ],
            compiler_params=PARAMS,
            cost_estimate=cost(4 * own_rows * features * 3 * HEAD, 16 * own_bytes),
            name="layer",
        )(
            own, left, right, own_squares, left_squares, right_squares,
            time_bias, station_bias, weights, kept,
        )
        if not last:
            head_rows, tail_rows, squares = sent
            own = to_next(kept, tick, tick + 1, 0)
            left = to_next(tail_rows, tick, tick + 1, 1)
            right = to_next(head_rows, tick, tick + 1, -1)
            own_squares = to_next_other(squares, tick, tick + 1, 0)
            left_squares = to_next_other(squares, tick, tick + 1, 1)
            right_squares = to_next_other(squares, tick, tick + 1, -1)
    return kept


def solution(mesh):
    return jax.shard_map(
        body,
        mesh=mesh,
        in_specs=(P(None, "seq", None, "rep"), P("section", "rep", None, None), P(), P()),
        out_specs=P("section", None, "seq", None, "rep"),
        check_vma=False,
    )
```

```python
import math

import jax
import jax.numpy as jnp
from jax import lax
from jax.experimental import pallas as pl
from jax.experimental.pallas import tpu as pltpu
from jax.sharding import PartitionSpec as P

HEADS = 32
HEAD = 128
WIN = 4
GROUP = 4
EPS = 1e-06
BIG = 1e30

HBM = pl.BlockSpec(memory_space=pltpu.HBM)
VMEM = pl.BlockSpec(memory_space=pltpu.VMEM)
PARAMS = pltpu.CompilerParams(vmem_limit_bytes=16 * 1024 * 1024)


def cost(flops, moved):
    return pl.CostEstimate(flops=flops, bytes_accessed=moved, transcendentals=0)


def first_kernel(
    signal_hbm, weights_hbm, first_hbm, pad_hbm, own_ref, chip_ref, far_ref, squares_ref,
    weights_ref, time_ref, station_ref, signal_ref, first_ref, pad_ref, arrived,
    *, total_steps,
):
    copies = [
        pltpu.make_async_copy(signal_hbm, signal_ref, arrived.at[0]),
        pltpu.make_async_copy(first_hbm, first_ref, arrived.at[1]),
        pltpu.make_async_copy(pad_hbm, pad_ref, arrived.at[2]),
        pltpu.make_async_copy(weights_hbm, weights_ref, arrived.at[3]),
    ]
    for copy in copies:
        copy.start()
    micro, steps, stations, _ = signal_ref.shape
    rows_micro = steps * stations
    edge = WIN * stations
    copies[0].wait()
    for m in range(micro):
        for t in range(0, steps, 2):
            own_ref[pl.ds(m * rows_micro + t * stations, 2 * stations), :] = jnp.concatenate(
                [signal_ref[m, t].astype(jnp.float32), signal_ref[m, t + 1].astype(jnp.float32)],
                axis=0,
            ).astype(jnp.bfloat16)
    odd = lax.axis_index("seq") % 2
    for m in range(micro):
        chip = m * rows_micro + (1 - odd) * (rows_micro - edge)
        far = m * rows_micro + odd * (rows_micro - edge)
        chip_ref[m * edge : (m + 1) * edge, :] = own_ref[pl.ds(pl.multiple_of(chip, edge), edge), :]
        far_ref[m * edge : (m + 1) * edge, :] = own_ref[pl.ds(pl.multiple_of(far, edge), edge), :]
    squares_ref[...] = jnp.zeros(squares_ref.shape, jnp.float32)
    squares_ref[0:1, 0 : micro * rows_micro] = squares_row(own_ref[...])
    copies[1].wait()
    copies[2].wait()
    fill_masks(first_ref, pad_ref, time_ref, station_ref, steps, stations, total_steps)
    copies[3].wait()


def squares_row(rows):
    gram = lax.dot_general(
        rows, rows, (((1,), (1,)), ((), ())), preferred_element_type=jnp.float32
    )
    return jnp.sum(jnp.where(same(rows.shape[0]), gram, 0.0), axis=0, keepdims=True)


def edge_kernel(edge_ref, squares_ref, out_ref):
    out_ref[...] = squares_ref[...]
    out_ref[1:2, 0 : edge_ref.shape[0]] = squares_row(edge_ref[...])


def same(count):
    return lax.broadcasted_iota(jnp.int32, (count, count), 0) == lax.broadcasted_iota(
        jnp.int32, (count, count), 1
    )


def fill_masks(first_ref, pad_ref, time_ref, station_ref, steps, stations, total_steps):
    time_base = lax.axis_index("seq") * steps
    keys = (steps + 2 * WIN) * stations
    columns = GROUP * steps * stations
    key = lax.broadcasted_iota(jnp.int32, (keys, columns), 0)
    query = lax.broadcasted_iota(jnp.int32, (keys, columns), 1) % (steps * stations)
    key_station, query_station = key % stations, query % stations
    query_time = query // stations
    odd = lax.axis_index("seq") % 2
    after_first = steps * (1 - odd) - WIN * odd
    after_second = steps * odd - WIN * (1 - odd)
    step_of = key // stations
    key_time = jnp.where(
        step_of < steps,
        step_of,
        jnp.where(
            step_of < steps + WIN, step_of - steps + after_first, step_of - steps - WIN + after_second
        ),
    )
    same_station = key_station == query_station
    same_time = key_time == query_time
    near = jnp.abs(key_time - query_time) <= WIN
    step = time_base + key_time
    for m in range(time_ref.shape[0]):
        first = jnp.zeros((keys, columns), jnp.int32)
        pad = jnp.zeros((keys, columns), jnp.int32)
        for s in range(stations):
            first = jnp.where(key_station == s, first_ref[m, s], first)
            pad = jnp.where(key_station == s, pad_ref[m, s], pad)
        recorded = (step >= first) & (step < total_steps - pad)
        time_ref[m] = jnp.where(same_station & near & (recorded | same_time), 0.0, -BIG)
        station_ref[m] = jnp.where(same_time & (recorded | same_station), 0.0, -BIG)[: steps * stations]


def softmax_columns(scores):
    grown = jnp.exp(scores - jnp.max(scores, axis=0, keepdims=True))
    return (grown * (1.0 / jnp.sum(grown, axis=0, keepdims=True))).astype(jnp.bfloat16)


def layer_kernel(
    own_ref, chip_ref, far_ref, own_squares_ref, chip_squares_ref, far_squares_ref,
    time_ref, station_ref, weights_ref, kept_ref, out_ref, *refs, tick, micro, steps, stations, last,
):
    if last:
        normed_ref, projected_ref = refs
    else:
        next_chip_ref, next_far_ref, squares_ref, normed_ref, projected_ref = refs
    rows_micro = steps * stations
    edge = WIN * stations
    reach = rows_micro + 2 * edge
    own_rows = micro * rows_micro
    all_rows = micro * reach
    heads_dev = weights_ref.shape[1]
    active = lax.axis_index("section") == tick
    odd = lax.axis_index("seq") % 2
    bf16, f32 = jnp.bfloat16, jnp.float32

    def write(m, lanes, values):
        if last:
            for t in range(steps):
                out_ref[0, m, t, :, lanes] = values[t * stations : (t + 1) * stations].astype(bf16)
        else:
            values = values.astype(bf16)
            out_ref[m * rows_micro : (m + 1) * rows_micro, lanes] = values
            head, tail = values[:edge], values[rows_micro - edge :]
            next_chip_ref[m * edge : (m + 1) * edge, lanes] = jnp.where(odd == 1, head, tail)
            next_far_ref[m * edge : (m + 1) * edge, lanes] = jnp.where(odd == 1, tail, head)

    row = lax.broadcasted_iota(jnp.int32, (all_rows, 128), 0)
    lane = lax.broadcasted_iota(jnp.int32, (all_rows, 128), 1)
    place, of_micro = row % reach, row // reach

    def column_squares():
        base = of_micro * rows_micro
        chip_lane = base + place - rows_micro + odd * (rows_micro - edge)
        far_lane = base + place - rows_micro - edge + (1 - odd) * (rows_micro - edge)
        chip_row = chip_squares_ref[0:1, :]
        if tick == 0:
            chip_row = chip_squares_ref[1:2, :]
            chip_lane = of_micro * edge + place - rows_micro
        picked = jnp.where(
            place < rows_micro,
            jnp.where(lane == base + place, own_squares_ref[0:1, :], 0.0),
            jnp.where(
                place < rows_micro + edge,
                jnp.where(lane == chip_lane, chip_row, 0.0),
                jnp.where(lane == far_lane, far_squares_ref[0:1, :], 0.0),
            ),
        )
        return jnp.sum(picked, axis=1, keepdims=True)

    @pl.when(active)
    def _():
        raw = []
        for m in range(micro):
            raw += [
                own_ref[m * rows_micro : (m + 1) * rows_micro, :],
                chip_ref[m * edge : (m + 1) * edge, :],
                far_ref[m * edge : (m + 1) * edge, :],
            ]
        raw = jnp.concatenate(raw, axis=0)
        total = column_squares()
        mine = jnp.zeros((all_rows, HEAD), f32)
        for head in range(heads_dev):
            part = raw[:, head * HEAD : (head + 1) * HEAD].astype(f32)
            mine = mine + part * part
        if tick == 0:
            mine = jnp.where(place < rows_micro + edge, 0.0, mine)
        total = total + jnp.sum(mine, axis=1, keepdims=True)
        factor = lax.rsqrt(total / (HEADS * HEAD) + EPS)
        for head in range(heads_dev):
            lanes = slice(head * HEAD, (head + 1) * HEAD)
            normed_ref[:, lanes] = (raw[:, lanes].astype(f32) * factor).astype(bf16)
        width = 3 * HEAD
        for head in range(heads_dev):
            projected_ref[:, head * width : (head + 1) * width] = jnp.dot(
                normed_ref[:, head * HEAD : (head + 1) * HEAD],
                weights_ref[0, head],
                preferred_element_type=f32,
            ).astype(bf16)
        pairs = [(g, m) for g in range(heads_dev // GROUP) for m in range(micro)]
        blank = jnp.zeros((rows_micro, HEAD), bf16)
        scores = []
        for g, m in pairs:
            at = [(g * GROUP + j) * width for j in range(GROUP)]
            first = m * reach
            spread = jnp.concatenate(
                [
                    jnp.concatenate(
                        [
                            projected_ref[first : first + rows_micro, at[j] : at[j] + HEAD]
                            if i == j
                            else blank
                            for i in range(GROUP)
                        ],
                        axis=1,
                    )
                    for j in range(GROUP)
                ],
                axis=0,
            )
            keys = jnp.concatenate(
                [projected_ref[first : first + reach, a + HEAD : a + 2 * HEAD] for a in at], axis=1
            )
            scores.append(
                lax.dot_general(
                    keys, spread, (((1,), (1,)), ((), ())), preferred_element_type=f32
                )
                * (1.0 / math.sqrt(HEAD))
            )
        mixes = []
        for (g, m), score in zip(pairs, scores):
            time_weights = softmax_columns(score + time_ref[m])
            station_weights = softmax_columns(score[:rows_micro] + station_ref[m])
            mixes.append(jnp.concatenate([time_weights, station_weights], axis=0).T)
        sums = [jnp.zeros((rows_micro, HEAD), f32) for _ in range(micro)]
        for (g, m), mix in zip(pairs, mixes):
            first = m * reach
            for j in range(GROUP):
                head = g * GROUP + j
                at = head * width + 2 * HEAD
                mixed = jnp.dot(
                    mix[j * rows_micro : (j + 1) * rows_micro],
                    jnp.concatenate(
                        [
                            projected_ref[first : first + reach, at : at + HEAD],
                            projected_ref[first : first + rows_micro, at : at + HEAD],
                        ],
                        axis=0,
                    ),
                    preferred_element_type=f32,
                )
                lanes = slice(head * HEAD, (head + 1) * HEAD)
                own = slice(m * rows_micro, (m + 1) * rows_micro)
                result = own_ref[own, lanes].astype(f32) + mixed
                write(m, lanes, result)
                if not last:
                    rounded = result.astype(bf16).astype(f32)
                    sums[m] = sums[m] + rounded * rounded
        if not last:
            column = jnp.sum(jnp.concatenate(sums, axis=0), axis=1, keepdims=True)
            squares_ref[...] = jnp.zeros(squares_ref.shape, f32)
            squares_ref[0:1, 0:own_rows] = jnp.sum(
                jnp.where(same(own_rows), column, 0.0), axis=0, keepdims=True
            )

    @pl.when(jnp.logical_not(active))
    def _():
        for m in range(micro):
            for head in range(heads_dev):
                lanes = slice(head * HEAD, (head + 1) * HEAD)
                write(m, lanes, kept_ref[m * rows_micro : (m + 1) * rows_micro, lanes].astype(f32))
        if not last:
            squares_ref[...] = jnp.zeros(squares_ref.shape, f32)


def body(signal, head_proj, record_start, record_pad):
    section_count = lax.axis_size("section")
    seq_count = lax.axis_size("seq")
    rep_count = lax.axis_size("rep")
    micro, steps, stations, features = signal.shape
    heads_dev = head_proj.shape[1]
    rows_micro = steps * stations
    own_rows = micro * rows_micro
    edge = WIN * stations
    reach = rows_micro + 2 * edge
    bf16, f32 = jnp.bfloat16, jnp.float32
    own_shape = jax.ShapeDtypeStruct((own_rows, features), bf16)
    edge_shape = jax.ShapeDtypeStruct((micro * edge, features), bf16)
    squares_shape = jax.ShapeDtypeStruct((8, 128), f32)
    own_bytes = own_rows * features * 2
    columns = GROUP * rows_micro

    own, chip_rows, far_rows, squares, weights, time_bias, station_bias = pl.pallas_call(
        lambda *refs: first_kernel(*refs, total_steps=steps * seq_count),
        in_specs=[HBM] * 4,
        out_specs=[VMEM] * 7,
        out_shape=[
            own_shape,
            edge_shape,
            edge_shape,
            squares_shape,
            jax.ShapeDtypeStruct(head_proj.shape, bf16),
            jax.ShapeDtypeStruct((micro, reach, columns), f32),
            jax.ShapeDtypeStruct((micro, rows_micro, columns), f32),
        ],
        scratch_shapes=[
            pltpu.VMEM(signal.shape, bf16),
            pltpu.SMEM(record_start.shape, jnp.int32),
            pltpu.SMEM(record_pad.shape, jnp.int32),
            pltpu.SemaphoreType.DMA((4,)),
        ],
        compiler_params=PARAMS,
        cost_estimate=cost(2 * own_rows * own_rows * features, 3 * own_bytes),
        name="first",
    )(*[pltpu.with_memory_space_constraint(x, pltpu.HBM) for x in (signal, head_proj, record_start, record_pad)])

    def moved(block, source, target, hop, other=False):
        route = []
        for i in range(seq_count):
            to = i if hop == 0 else i + 1 - 2 * (i % 2) if hop == 1 else i - 1 + 2 * (i % 2)
            if 0 <= to < seq_count:
                for r in range(rep_count):
                    route.append(
                        (
                            (source * seq_count + i) * rep_count + r,
                            (target * seq_count + to) * rep_count
                            + ((r + 1) % rep_count if other else r),
                        )
                    )
        return lax.ppermute(block, ("section", "seq", "rep"), route)

    helper = 1 if section_count > 1 else 0
    chip_edge = moved(chip_rows, 0, 0, 1)
    far_edge = moved(far_rows, helper, 0, 2)
    far_squares = moved(squares, helper, 0, 2, other=True)
    both = pl.pallas_call(
        edge_kernel,
        in_specs=[VMEM] * 2,
        out_specs=VMEM,
        out_shape=squares_shape,
        compiler_params=PARAMS,
        name="edge",
    )(chip_edge, squares)
    own_squares = chip_squares = lax.psum(both, "rep")
    kept = own
    for tick in range(section_count):
        last = tick + 1 == section_count

        def kernel(*refs, tick=tick, last=last):
            layer_kernel(*refs, tick=tick, micro=micro, steps=steps, stations=stations, last=last)

        out_shape = (
            [jax.ShapeDtypeStruct((1,) + signal.shape, bf16)]
            if last
            else [own_shape, edge_shape, edge_shape, squares_shape]
        )
        kept, *sent = pl.pallas_call(
            kernel,
            in_specs=[VMEM] * 10,
            out_specs=[VMEM] * len(out_shape),
            out_shape=out_shape,
            scratch_shapes=[
                pltpu.VMEM((micro * reach, features), bf16),
                pltpu.VMEM((micro * reach, heads_dev * 3 * HEAD), bf16),
            ],
            compiler_params=PARAMS,
            cost_estimate=cost(4 * own_rows * features * 3 * HEAD, 16 * own_bytes),
            name="layer",
        )(
            own, chip_edge, far_edge, own_squares, chip_squares, far_squares,
            time_bias, station_bias, weights, kept,
        )
        if not last:
            chip_rows, far_rows, squares = sent
            own_squares = moved(squares, tick, tick + 1, 0, other=True)
            own = moved(kept, tick, tick + 1, 0)
            chip_edge = moved(chip_rows, tick, tick + 1, 1)
            far_edge = moved(far_rows, tick, tick + 1, 2)
            chip_squares = moved(squares, tick, tick + 1, 1, other=True)
            squares, _ = lax.optimization_barrier((squares, own_squares))
            far_squares = moved(squares, tick, tick + 1, 2, other=True)
    return kept


def solution(mesh):
    return jax.shard_map(
        body,
        mesh=mesh,
        in_specs=(P(None, "seq", None, "rep"), P("section", "rep", None, None), P(), P()),
        out_specs=P("section", None, "seq", None, "rep"),
        check_vma=False,
    )
```

```python
import math

import jax
import jax.numpy as jnp
from jax import lax
from jax.experimental import pallas as pl
from jax.experimental.pallas import tpu as pltpu
from jax.sharding import PartitionSpec as P

HEADS = 32
HEAD = 128
WIN = 4
GROUP = 4
EPS = 1e-06
BIG = 1e30
CHIP, FAR, NEXT_CHIP, NEXT_FAR = range(4)

HBM = pl.BlockSpec(memory_space=pltpu.HBM)
VMEM = pl.BlockSpec(memory_space=pltpu.VMEM)
PARAMS = pltpu.CompilerParams(vmem_limit_bytes=16 * 1024 * 1024)


def cost(flops, moved):
    return pl.CostEstimate(flops=flops, bytes_accessed=moved, transcendentals=0)


def odd_device():
    return lax.axis_index("seq") % 2


def first_step(half):
    odd = odd_device()
    return {
        CHIP: WIN * (1 - odd),
        FAR: WIN * odd,
        NEXT_CHIP: 2 * WIN * (1 - odd) - WIN * odd,
        NEXT_FAR: 2 * WIN * odd - WIN * (1 - odd),
    }[half]


def same(count):
    return lax.broadcasted_iota(jnp.int32, (count, count), 0) == lax.broadcasted_iota(
        jnp.int32, (count, count), 1
    )


def squares_row(rows):
    gram = lax.dot_general(
        rows, rows, (((1,), (1,)), ((), ())), preferred_element_type=jnp.float32
    )
    return jnp.sum(jnp.where(same(rows.shape[0]), gram, 0.0), axis=0, keepdims=True)


def fill_masks(first_ref, pad_ref, time_ref, station_ref, stations, total_steps):
    own = 2 * WIN * stations
    keys, columns = 2 * own, GROUP * own
    key = lax.broadcasted_iota(jnp.int32, (keys, columns), 0)
    query = lax.broadcasted_iota(jnp.int32, (keys, columns), 1) % own

    def time_of(row):
        half, step = row // (WIN * stations), (row // stations) % WIN
        start = jnp.where(half == CHIP, first_step(CHIP), first_step(FAR))
        start = jnp.where(half == NEXT_CHIP, first_step(NEXT_CHIP), start)
        return step + jnp.where(half == NEXT_FAR, first_step(NEXT_FAR), start)

    key_station, query_station = key % stations, query % stations
    key_time, query_time = time_of(key), time_of(query)
    same_station = key_station == query_station
    same_time = key_time == query_time
    near = jnp.abs(key_time - query_time) <= WIN
    step = lax.axis_index("seq") * (2 * WIN) + key_time
    for m in range(time_ref.shape[0]):
        first = jnp.zeros((keys, columns), jnp.int32)
        pad = jnp.zeros((keys, columns), jnp.int32)
        for s in range(stations):
            first = jnp.where(key_station == s, first_ref[m, s], first)
            pad = jnp.where(key_station == s, pad_ref[m, s], pad)
        recorded = (step >= first) & (step < total_steps - pad)
        time_ref[m] = jnp.where(same_station & near & (recorded | same_time), 0.0, -BIG)
        station_ref[m] = jnp.where(same_time & (recorded | same_station), 0.0, -BIG)[:own]


def first_kernel(
    signal_hbm, weights_hbm, first_hbm, pad_hbm, chip_ref, far_ref, squares_ref,
    weights_ref, time_ref, station_ref, signal_ref, first_ref, pad_ref, arrived,
    *, total_steps,
):
    copies = [
        pltpu.make_async_copy(signal_hbm, signal_ref, arrived.at[0]),
        pltpu.make_async_copy(first_hbm, first_ref, arrived.at[1]),
        pltpu.make_async_copy(pad_hbm, pad_ref, arrived.at[2]),
        pltpu.make_async_copy(weights_hbm, weights_ref, arrived.at[3]),
    ]
    for copy in copies:
        copy.start()
    micro, _, stations, _ = signal_ref.shape
    edge = WIN * stations
    copies[0].wait()
    for half, half_ref in ((CHIP, chip_ref), (FAR, far_ref)):
        start = first_step(half)
        for m in range(micro):
            for t in range(0, WIN, 2):
                pair = [signal_ref[m, start + t + i].astype(jnp.float32) for i in range(2)]
                at = m * edge + t * stations
                half_ref[at : at + 2 * stations, :] = jnp.concatenate(pair, axis=0).astype(
                    jnp.bfloat16
                )
    squares_ref[...] = jnp.zeros(squares_ref.shape, jnp.float32)
    for half, half_ref in ((CHIP, chip_ref), (FAR, far_ref)):
        squares_ref[half : half + 1, 0 : micro * edge] = squares_row(half_ref[...])
    copies[1].wait()
    copies[2].wait()
    fill_masks(first_ref, pad_ref, time_ref, station_ref, stations, total_steps)
    copies[3].wait()


def edge_kernel(next_chip_ref, next_far_ref, squares_ref, out_ref):
    out_ref[...] = squares_ref[...]
    for half, half_ref in ((NEXT_CHIP, next_chip_ref), (NEXT_FAR, next_far_ref)):
        out_ref[half : half + 1, 0 : half_ref.shape[0]] = squares_row(half_ref[...])


def norm_kernel(chip_ref, squares_ref, _, normed_ref):
    rows = chip_ref[...]
    count = rows.shape[0]
    total = squares_row(rows) + squares_ref[CHIP : CHIP + 1, 0:count]
    factor = lax.rsqrt(total / (HEADS * HEAD) + EPS)
    column = jnp.sum(jnp.where(same(count), factor, 0.0), axis=1, keepdims=True)
    normed_ref[...] = (rows.astype(jnp.float32) * column).astype(jnp.bfloat16)


def softmax_columns(scores):
    grown = jnp.exp(scores - jnp.max(scores, axis=0, keepdims=True))
    return (grown * (1.0 / jnp.sum(grown, axis=0, keepdims=True))).astype(jnp.bfloat16)


def layer_kernel(
    chip_ref, far_ref, next_chip_ref, next_far_ref, squares_ref, far_squares_ref,
    time_ref, station_ref, weights_ref, kept_chip_ref, kept_far_ref, *refs, tick, stations, last,
):
    if last:
        out_ref, normed_ref, projected_ref = refs
    else:
        out_chip_ref, out_far_ref, out_squares_ref, normed_ref, projected_ref = refs
    edge = WIN * stations
    micro = chip_ref.shape[0] // edge
    own, reach = 2 * edge, 4 * edge
    heads_dev = weights_ref.shape[1]
    width = 3 * HEAD
    bf16, f32 = jnp.bfloat16, jnp.float32
    active = lax.axis_index("section") == tick

    def write(m, lanes, values):
        for half in (CHIP, FAR):
            part = values[half * edge : (half + 1) * edge].astype(bf16)
            if last:
                for t in range(WIN):
                    out_ref[0, m, first_step(half) + t, :, lanes] = part[
                        t * stations : (t + 1) * stations
                    ]
            else:
                half_ref = (out_chip_ref, out_far_ref)[half]
                half_ref[m * edge : (m + 1) * edge, lanes] = part

    def norm_rows(half, half_ref, squares_row_ref, complete):
        lane = lax.broadcasted_iota(jnp.int32, (micro * edge, 128), 1)
        row = lax.broadcasted_iota(jnp.int32, (micro * edge, 128), 0)
        total = jnp.where(lane == row, squares_row_ref, 0.0)
        if not complete:
            for head in range(heads_dev):
                part = half_ref[:, head * HEAD : (head + 1) * HEAD].astype(f32)
                total = total + part * part
        factor = lax.rsqrt(jnp.sum(total, axis=1, keepdims=True) / (HEADS * HEAD) + EPS)
        for head in range(heads_dev):
            lanes = slice(head * HEAD, (head + 1) * HEAD)
            put_normed(half, lanes, (half_ref[:, lanes].astype(f32) * factor).astype(bf16))

    def put_normed(half, lanes, rows):
        for m in range(micro):
            at = m * reach + half * edge
            normed_ref[at : at + edge, lanes] = rows[m * edge : (m + 1) * edge]

    @pl.when(active)
    def _():
        if tick == 0:
            for half, half_ref in enumerate((chip_ref, far_ref, next_chip_ref, next_far_ref)):
                norm_rows(half, half_ref, squares_ref[half : half + 1, :], True)
        else:
            norm_rows(CHIP, chip_ref, squares_ref[CHIP : CHIP + 1, :], False)
            norm_rows(FAR, far_ref, squares_ref[FAR : FAR + 1, :], False)
            put_normed(NEXT_CHIP, slice(None), next_chip_ref[...])
            norm_rows(NEXT_FAR, next_far_ref, far_squares_ref[FAR : FAR + 1, :], False)
        for head in range(heads_dev):
            projected_ref[:, head * width : (head + 1) * width] = jnp.dot(
                normed_ref[:, head * HEAD : (head + 1) * HEAD],
                weights_ref[0, head],
                preferred_element_type=f32,
            ).astype(bf16)
        pairs = [(g, m) for g in range(heads_dev // GROUP) for m in range(micro)]
        blank = jnp.zeros((own, HEAD), bf16)
        scores = []
        for g, m in pairs:
            at = [(g * GROUP + j) * width for j in range(GROUP)]
            first = m * reach
            spread = jnp.concatenate(
                [
                    jnp.concatenate(
                        [
                            projected_ref[first : first + own, at[j] : at[j] + HEAD]
                            if i == j
                            else blank
                            for i in range(GROUP)
                        ],
                        axis=1,
                    )
                    for j in range(GROUP)
                ],
                axis=0,
            )
            keys = jnp.concatenate(
                [projected_ref[first : first + reach, a + HEAD : a + 2 * HEAD] for a in at], axis=1
            )
            scores.append(
                lax.dot_general(
                    keys, spread, (((1,), (1,)), ((), ())), preferred_element_type=f32
                )
                * (1.0 / math.sqrt(HEAD))
            )
        mixes = []
        for (g, m), score in zip(pairs, scores):
            time_weights = softmax_columns(score + time_ref[m])
            station_weights = softmax_columns(score[:own] + station_ref[m])
            mixes.append(jnp.concatenate([time_weights, station_weights], axis=0).T)
        sums = [jnp.zeros((own, HEAD), f32) for _ in range(micro)]
        for (g, m), mix in zip(pairs, mixes):
            first = m * reach
            for j in range(GROUP):
                head = g * GROUP + j
                at = head * width + 2 * HEAD
                mixed = jnp.dot(
                    mix[j * own : (j + 1) * own],
                    jnp.concatenate(
                        [
                            projected_ref[first : first + reach, at : at + HEAD],
                            projected_ref[first : first + own, at : at + HEAD],
                        ],
                        axis=0,
                    ),
                    preferred_element_type=f32,
                )
                lanes = slice(head * HEAD, (head + 1) * HEAD)
                hidden = jnp.concatenate(
                    [ref[m * edge : (m + 1) * edge, lanes] for ref in (chip_ref, far_ref)], axis=0
                )
                result = hidden.astype(f32) + mixed
                write(m, lanes, result)
                if not last:
                    rounded = result.astype(bf16).astype(f32)
                    sums[m] = sums[m] + rounded * rounded
        if not last:
            out_squares_ref[...] = jnp.zeros(out_squares_ref.shape, f32)
            for half in (CHIP, FAR):
                parts = [s[half * edge : (half + 1) * edge] for s in sums]
                column = jnp.sum(jnp.concatenate(parts, axis=0), axis=1, keepdims=True)
                out_squares_ref[half : half + 1, 0 : micro * edge] = jnp.sum(
                    jnp.where(same(micro * edge), column, 0.0), axis=0, keepdims=True
                )

    @pl.when(jnp.logical_not(active))
    def _():
        for m in range(micro):
            for head in range(heads_dev):
                lanes = slice(head * HEAD, (head + 1) * HEAD)
                kept = [
                    ref[m * edge : (m + 1) * edge, lanes] for ref in (kept_chip_ref, kept_far_ref)
                ]
                write(m, lanes, jnp.concatenate(kept, axis=0).astype(f32))
        if not last:
            out_squares_ref[...] = jnp.zeros(out_squares_ref.shape, f32)


def body(signal, head_proj, record_start, record_pad):
    section_count = lax.axis_size("section")
    seq_count = lax.axis_size("seq")
    rep_count = lax.axis_size("rep")
    micro, steps, stations, features = signal.shape
    heads_dev = head_proj.shape[1]
    edge = WIN * stations
    own, reach = 2 * edge, 4 * edge
    bf16, f32 = jnp.bfloat16, jnp.float32
    half_shape = jax.ShapeDtypeStruct((micro * edge, features), bf16)
    squares_shape = jax.ShapeDtypeStruct((8, 128), f32)
    signal_bytes = signal.size * 2

    chip, far, squares, weights, time_bias, station_bias = pl.pallas_call(
        lambda *refs: first_kernel(*refs, total_steps=steps * seq_count),
        in_specs=[HBM] * 4,
        out_specs=[VMEM] * 6,
        out_shape=[
            half_shape,
            half_shape,
            squares_shape,
            jax.ShapeDtypeStruct(head_proj.shape, bf16),
            jax.ShapeDtypeStruct((micro, reach, GROUP * own), f32),
            jax.ShapeDtypeStruct((micro, own, GROUP * own), f32),
        ],
        scratch_shapes=[
            pltpu.VMEM(signal.shape, bf16),
            pltpu.SMEM(record_start.shape, jnp.int32),
            pltpu.SMEM(record_pad.shape, jnp.int32),
            pltpu.SemaphoreType.DMA((4,)),
        ],
        compiler_params=PARAMS,
        cost_estimate=cost(2 * micro * own * signal.size, 3 * signal_bytes),
        name="first",
    )(
        *[
            pltpu.with_memory_space_constraint(x, pltpu.HBM)
            for x in (signal, head_proj, record_start, record_pad)
        ]
    )

    def moved(block, source, target, hop, other=False):
        route = []
        for i in range(seq_count):
            to = i if hop == 0 else i + 1 - 2 * (i % 2) if hop == 1 else i - 1 + 2 * (i % 2)
            if 0 <= to < seq_count:
                for r in range(rep_count):
                    route.append(
                        (
                            (source * seq_count + i) * rep_count + r,
                            (target * seq_count + to) * rep_count
                            + ((r + 1) % rep_count if other else r),
                        )
                    )
        return lax.ppermute(block, ("section", "seq", "rep"), route)

    helper = 1 if section_count > 1 else 0
    next_far = moved(far, helper, 0, 2)
    next_chip = moved(chip, 0, 0, 1)
    squares = pl.pallas_call(
        edge_kernel,
        in_specs=[VMEM] * 3,
        out_specs=VMEM,
        out_shape=squares_shape,
        compiler_params=PARAMS,
        name="edge",
    )(next_chip, next_far, squares)
    squares = far_squares = lax.psum(squares, "rep")
    kept = (chip, far)
    for tick in range(section_count):
        last = tick + 1 == section_count

        def kernel(*refs, tick=tick, last=last):
            layer_kernel(*refs, tick=tick, stations=stations, last=last)

        out_shape = (
            [jax.ShapeDtypeStruct((1,) + signal.shape, bf16)]
            if last
            else [half_shape, half_shape, squares_shape]
        )
        outputs = pl.pallas_call(
            kernel,
            in_specs=[VMEM] * 11,
            out_specs=[VMEM] * len(out_shape),
            out_shape=out_shape,
            scratch_shapes=[
                pltpu.VMEM((micro * reach, features), bf16),
                pltpu.VMEM((micro * reach, heads_dev * 3 * HEAD), bf16),
            ],
            compiler_params=PARAMS,
            cost_estimate=cost(8 * signal.size * 3 * HEAD, 16 * signal_bytes),
            name="layer",
        )(
            chip, far, next_chip, next_far, squares, far_squares,
            time_bias, station_bias, weights, *kept,
        )
        if last:
            return outputs[0]
        kept = outputs[:2]
        mine = outputs[2]
        chip = moved(kept[0], tick, tick + 1, 0)
        squares = moved(mine, tick, tick + 1, 0, other=True)
        far = moved(kept[1], tick, tick + 1, 0)
        next_far = moved(kept[1], tick, tick + 1, 2)
        far_squares = moved(mine, tick, tick + 1, 2, other=True)
        normed_chip = pl.pallas_call(
            norm_kernel,
            in_specs=[VMEM] * 3,
            out_specs=VMEM,
            out_shape=half_shape,
            compiler_params=PARAMS,
            name="norm",
        )(chip, squares, far_squares)
        next_chip = moved(normed_chip, tick + 1, tick + 1, 1)


def solution(mesh):
    return jax.shard_map(
        body,
        mesh=mesh,
        in_specs=(P(None, "seq", None, "rep"), P("section", "rep", None, None), P(), P()),
        out_specs=P("section", None, "seq", None, "rep"),
        check_vma=False,
    )
```

```python
import math

import jax
import jax.numpy as jnp
from jax import lax
from jax.experimental import pallas as pl
from jax.experimental.pallas import tpu as pltpu
from jax.sharding import PartitionSpec as P

HEADS = 32
HEAD = 128
WIN = 4
GROUP = 4
EPS = 1e-06
BIG = 1e30
CHIP, FAR, NEXT_CHIP, NEXT_FAR = range(4)

HBM = pl.BlockSpec(memory_space=pltpu.HBM)
VMEM = pl.BlockSpec(memory_space=pltpu.VMEM)
PARAMS = pltpu.CompilerParams(vmem_limit_bytes=16 * 1024 * 1024)


def cost(flops, moved):
    return pl.CostEstimate(flops=flops, bytes_accessed=moved, transcendentals=0)


def odd_device():
    return lax.axis_index("seq") % 2


def first_step(half):
    odd = odd_device()
    return {
        CHIP: WIN * (1 - odd),
        FAR: WIN * odd,
        NEXT_CHIP: 2 * WIN * (1 - odd) - WIN * odd,
        NEXT_FAR: 2 * WIN * odd - WIN * (1 - odd),
    }[half]


def same(count):
    return lax.broadcasted_iota(jnp.int32, (count, count), 0) == lax.broadcasted_iota(
        jnp.int32, (count, count), 1
    )


def squares_row(rows):
    gram = lax.dot_general(
        rows, rows, (((1,), (1,)), ((), ())), preferred_element_type=jnp.float32
    )
    return jnp.sum(jnp.where(same(rows.shape[0]), gram, 0.0), axis=0, keepdims=True)


def fill_masks(first_ref, pad_ref, time_ref, station_ref, stations, total_steps):
    own = 2 * WIN * stations
    keys, columns = 2 * own, GROUP * own
    key = lax.broadcasted_iota(jnp.int32, (keys, columns), 0)
    query = lax.broadcasted_iota(jnp.int32, (keys, columns), 1) % own

    def time_of(row):
        half, step = row // (WIN * stations), (row // stations) % WIN
        start = jnp.where(half == CHIP, first_step(CHIP), first_step(FAR))
        start = jnp.where(half == NEXT_CHIP, first_step(NEXT_CHIP), start)
        return step + jnp.where(half == NEXT_FAR, first_step(NEXT_FAR), start)

    key_station, query_station = key % stations, query % stations
    key_time, query_time = time_of(key), time_of(query)
    same_station = key_station == query_station
    same_time = key_time == query_time
    near = jnp.abs(key_time - query_time) <= WIN
    step = lax.axis_index("seq") * (2 * WIN) + key_time
    for m in range(time_ref.shape[0]):
        first = jnp.zeros((keys, columns), jnp.int32)
        pad = jnp.zeros((keys, columns), jnp.int32)
        for s in range(stations):
            first = jnp.where(key_station == s, first_ref[m, s], first)
            pad = jnp.where(key_station == s, pad_ref[m, s], pad)
        recorded = (step >= first) & (step < total_steps - pad)
        time_ref[m] = jnp.where(same_station & near & (recorded | same_time), 0.0, -BIG)
        station_ref[m] = jnp.where(same_time & (recorded | same_station), 0.0, -BIG)[:own]


def halves_kernel(signal_hbm, chip_ref, far_ref, signal_ref, arrived):
    copy = pltpu.make_async_copy(signal_hbm, signal_ref, arrived)
    copy.start()
    micro, _, stations, _ = signal_ref.shape
    edge = WIN * stations
    copy.wait()
    for half, half_ref in ((FAR, far_ref), (CHIP, chip_ref)):
        start = first_step(half)
        for m in range(micro):
            for t in range(0, WIN, 2):
                pair = [signal_ref[m, start + t + i].astype(jnp.float32) for i in range(2)]
                at = m * edge + t * stations
                half_ref[at : at + 2 * stations, :] = jnp.concatenate(pair, axis=0).astype(
                    jnp.bfloat16
                )


def fixed_kernel(
    weights_hbm, first_hbm, pad_hbm, _, weights_ref, time_ref, station_ref,
    first_ref, pad_ref, arrived, *, stations, total_steps,
):
    copies = [
        pltpu.make_async_copy(first_hbm, first_ref, arrived.at[0]),
        pltpu.make_async_copy(pad_hbm, pad_ref, arrived.at[1]),
        pltpu.make_async_copy(weights_hbm, weights_ref, arrived.at[2]),
    ]
    for copy in copies:
        copy.start()
    copies[0].wait()
    copies[1].wait()
    fill_masks(first_ref, pad_ref, time_ref, station_ref, stations, total_steps)
    copies[2].wait()


def squares_kernel(*refs):
    out_ref = refs[-1]
    out_ref[...] = jnp.zeros(out_ref.shape, jnp.float32)
    for half, half_ref in enumerate(refs[:-1]):
        out_ref[half : half + 1, 0 : half_ref.shape[0]] = squares_row(half_ref[...])


def norm_kernel(chip_ref, squares_ref, *refs):
    rows = chip_ref[...]
    count = rows.shape[0]
    total = squares_row(rows) + squares_ref[CHIP : CHIP + 1, 0:count]
    factor = lax.rsqrt(total / (HEADS * HEAD) + EPS)
    column = jnp.sum(jnp.where(same(count), factor, 0.0), axis=1, keepdims=True)
    refs[-1][...] = (rows.astype(jnp.float32) * column).astype(jnp.bfloat16)


def softmax_columns(scores):
    grown = jnp.exp(scores - jnp.max(scores, axis=0, keepdims=True))
    return (grown * (1.0 / jnp.sum(grown, axis=0, keepdims=True))).astype(jnp.bfloat16)


def layer_kernel(
    chip_ref, far_ref, next_chip_ref, next_far_ref, squares_ref, far_squares_ref,
    time_ref, station_ref, weights_ref, kept_chip_ref, kept_far_ref, *refs, tick, stations, last,
):
    if last:
        out_ref, normed_ref, projected_ref = refs
    else:
        out_chip_ref, out_far_ref, normed_ref, projected_ref = refs
    edge = WIN * stations
    micro = chip_ref.shape[0] // edge
    own, reach = 2 * edge, 4 * edge
    heads_dev = weights_ref.shape[1]
    width = 3 * HEAD
    bf16, f32 = jnp.bfloat16, jnp.float32
    active = lax.axis_index("section") == tick

    def write(m, lanes, values):
        for half in (CHIP, FAR):
            part = values[half * edge : (half + 1) * edge].astype(bf16)
            if last:
                for t in range(WIN):
                    out_ref[0, m, first_step(half) + t, :, lanes] = part[
                        t * stations : (t + 1) * stations
                    ]
            else:
                half_ref = (out_chip_ref, out_far_ref)[half]
                half_ref[m * edge : (m + 1) * edge, lanes] = part

    def norm_rows(half, half_ref, squares_row_ref, complete):
        lane = lax.broadcasted_iota(jnp.int32, (micro * edge, 128), 1)
        row = lax.broadcasted_iota(jnp.int32, (micro * edge, 128), 0)
        total = jnp.where(lane == row, squares_row_ref, 0.0)
        if not complete:
            for head in range(heads_dev):
                part = half_ref[:, head * HEAD : (head + 1) * HEAD].astype(f32)
                total = total + part * part
        factor = lax.rsqrt(jnp.sum(total, axis=1, keepdims=True) / (HEADS * HEAD) + EPS)
        for head in range(heads_dev):
            lanes = slice(head * HEAD, (head + 1) * HEAD)
            put_normed(half, lanes, (half_ref[:, lanes].astype(f32) * factor).astype(bf16))

    def put_normed(half, lanes, rows):
        for m in range(micro):
            at = m * reach + half * edge
            normed_ref[at : at + edge, lanes] = rows[m * edge : (m + 1) * edge]

    @pl.when(active)
    def _():
        if tick == 0:
            for half, half_ref in enumerate((chip_ref, far_ref, next_chip_ref, next_far_ref)):
                norm_rows(half, half_ref, squares_ref[half : half + 1, :], True)
        else:
            norm_rows(CHIP, chip_ref, squares_ref[CHIP : CHIP + 1, :], False)
            norm_rows(FAR, far_ref, squares_ref[FAR : FAR + 1, :], False)
            put_normed(NEXT_CHIP, slice(None), next_chip_ref[...])
            norm_rows(NEXT_FAR, next_far_ref, far_squares_ref[FAR : FAR + 1, :], False)
        for head in range(heads_dev):
            projected_ref[:, head * width : (head + 1) * width] = jnp.dot(
                normed_ref[:, head * HEAD : (head + 1) * HEAD],
                weights_ref[0, head],
                preferred_element_type=f32,
            ).astype(bf16)
        pairs = [(g, m) for g in range(heads_dev // GROUP) for m in range(micro)]
        blank = jnp.zeros((own, HEAD), bf16)
        scores = []
        for g, m in pairs:
            at = [(g * GROUP + j) * width for j in range(GROUP)]
            first = m * reach
            spread = jnp.concatenate(
                [
                    jnp.concatenate(
                        [
                            projected_ref[first : first + own, at[j] : at[j] + HEAD]
                            if i == j
                            else blank
                            for i in range(GROUP)
                        ],
                        axis=1,
                    )
                    for j in range(GROUP)
                ],
                axis=0,
            )
            keys = jnp.concatenate(
                [projected_ref[first : first + reach, a + HEAD : a + 2 * HEAD] for a in at], axis=1
            )
            scores.append(
                lax.dot_general(
                    keys, spread, (((1,), (1,)), ((), ())), preferred_element_type=f32
                )
                * (1.0 / math.sqrt(HEAD))
            )
        mixes = []
        for (g, m), score in zip(pairs, scores):
            time_weights = softmax_columns(score + time_ref[m])
            station_weights = softmax_columns(score[:own] + station_ref[m])
            mixes.append(jnp.concatenate([time_weights, station_weights], axis=0).T)
        for (g, m), mix in zip(pairs, mixes):
            first = m * reach
            for j in range(GROUP):
                head = g * GROUP + j
                at = head * width + 2 * HEAD
                mixed = jnp.dot(
                    mix[j * own : (j + 1) * own],
                    jnp.concatenate(
                        [
                            projected_ref[first : first + reach, at : at + HEAD],
                            projected_ref[first : first + own, at : at + HEAD],
                        ],
                        axis=0,
                    ),
                    preferred_element_type=f32,
                )
                lanes = slice(head * HEAD, (head + 1) * HEAD)
                hidden = jnp.concatenate(
                    [ref[m * edge : (m + 1) * edge, lanes] for ref in (chip_ref, far_ref)], axis=0
                )
                result = hidden.astype(f32) + mixed
                write(m, lanes, result)

    @pl.when(jnp.logical_not(active))
    def _():
        for m in range(micro):
            for head in range(heads_dev):
                lanes = slice(head * HEAD, (head + 1) * HEAD)
                kept = [
                    ref[m * edge : (m + 1) * edge, lanes] for ref in (kept_chip_ref, kept_far_ref)
                ]
                write(m, lanes, jnp.concatenate(kept, axis=0).astype(f32))


def body(signal, head_proj, record_start, record_pad):
    section_count = lax.axis_size("section")
    seq_count = lax.axis_size("seq")
    rep_count = lax.axis_size("rep")
    micro, steps, stations, features = signal.shape
    heads_dev = head_proj.shape[1]
    edge = WIN * stations
    own, reach = 2 * edge, 4 * edge
    bf16, f32 = jnp.bfloat16, jnp.float32
    half_shape = jax.ShapeDtypeStruct((micro * edge, features), bf16)
    squares_shape = jax.ShapeDtypeStruct((8, 128), f32)
    signal_bytes = signal.size * 2

    def in_hbm(block):
        return pltpu.with_memory_space_constraint(block, pltpu.HBM)

    def squares_of(*halves):
        return pl.pallas_call(
            squares_kernel,
            in_specs=[VMEM] * len(halves),
            out_specs=VMEM,
            out_shape=squares_shape,
            compiler_params=PARAMS,
            name="squares",
        )(*halves)

    chip, far = pl.pallas_call(
        halves_kernel,
        in_specs=[HBM],
        out_specs=[VMEM] * 2,
        out_shape=[half_shape] * 2,
        scratch_shapes=[pltpu.VMEM(signal.shape, bf16), pltpu.SemaphoreType.DMA],
        compiler_params=PARAMS,
        cost_estimate=cost(signal.size, 2 * signal_bytes),
        name="halves",
    )(in_hbm(signal))
    weights, time_bias, station_bias = pl.pallas_call(
        lambda *refs: fixed_kernel(*refs, stations=stations, total_steps=steps * seq_count),
        in_specs=[HBM] * 3 + [VMEM],
        out_specs=[VMEM] * 3,
        out_shape=[
            jax.ShapeDtypeStruct(head_proj.shape, bf16),
            jax.ShapeDtypeStruct((micro, reach, GROUP * own), f32),
            jax.ShapeDtypeStruct((micro, own, GROUP * own), f32),
        ],
        scratch_shapes=[
            pltpu.SMEM(record_start.shape, jnp.int32),
            pltpu.SMEM(record_pad.shape, jnp.int32),
            pltpu.SemaphoreType.DMA((3,)),
        ],
        compiler_params=PARAMS,
        cost_estimate=cost(signal.size, 2 * head_proj.size),
        name="fixed",
    )(in_hbm(head_proj), in_hbm(record_start), in_hbm(record_pad), chip)

    def moved(block, source, target, hop, other=False):
        route = []
        for i in range(seq_count):
            to = i if hop == 0 else i + 1 - 2 * (i % 2) if hop == 1 else i - 1 + 2 * (i % 2)
            if 0 <= to < seq_count:
                for r in range(rep_count):
                    route.append(
                        (
                            (source * seq_count + i) * rep_count + r,
                            (target * seq_count + to) * rep_count
                            + ((r + 1) % rep_count if other else r),
                        )
                    )
        return lax.ppermute(block, ("section", "seq", "rep"), route)

    helper = 1 if section_count > 1 else 0
    next_far = moved(far, helper, 0, 2)
    next_chip = moved(chip, 0, 0, 1)
    squares = squares_of(chip, far, next_chip, next_far)
    squares = far_squares = lax.psum(squares, "rep")
    kept = (chip, far)
    for tick in range(section_count):
        last = tick + 1 == section_count

        def kernel(*refs, tick=tick, last=last):
            layer_kernel(*refs, tick=tick, stations=stations, last=last)

        out_shape = (
            [jax.ShapeDtypeStruct((1,) + signal.shape, bf16)]
            if last
            else [half_shape, half_shape]
        )
        outputs = pl.pallas_call(
            kernel,
            in_specs=[VMEM] * 11,
            out_specs=[VMEM] * len(out_shape),
            out_shape=out_shape,
            scratch_shapes=[
                pltpu.VMEM((micro * reach, features), bf16),
                pltpu.VMEM((micro * reach, heads_dev * 3 * HEAD), bf16),
            ],
            compiler_params=PARAMS,
            cost_estimate=cost(8 * signal.size * 3 * HEAD, 16 * signal_bytes),
            name="layer",
        )(
            chip, far, next_chip, next_far, squares, far_squares,
            time_bias, station_bias, weights, *kept,
        )
        if last:
            return outputs[0]
        kept = outputs
        mine = squares_of(*kept)
        chip = moved(kept[0], tick, tick + 1, 0)
        next_far = moved(kept[1], tick, tick + 1, 2)
        far = moved(kept[1], tick, tick + 1, 0)
        squares = moved(mine, tick, tick + 1, 0, other=True)
        far_squares = moved(mine, tick, tick + 1, 2, other=True)
        normed_chip = pl.pallas_call(
            norm_kernel,
            in_specs=[VMEM] * 4,
            out_specs=VMEM,
            out_shape=half_shape,
            compiler_params=PARAMS,
            name="norm",
        )(chip, squares, far_squares, next_far)
        next_chip = moved(normed_chip, tick + 1, tick + 1, 1)


def solution(mesh):
    return jax.shard_map(
        body,
        mesh=mesh,
        in_specs=(P(None, "seq", None, "rep"), P("section", "rep", None, None), P(), P()),
        out_specs=P("section", None, "seq", None, "rep"),
        check_vma=False,
    )
```

```python
import math

import jax
import jax.numpy as jnp
from jax import lax
from jax.experimental import pallas as pl
from jax.experimental.pallas import tpu as pltpu
from jax.sharding import PartitionSpec as P

HEADS = 32
HEAD = 128
WIN = 4
GROUP = 4
EPS = 1e-06
BIG = 1e30
CHIP, FAR, NEXT_CHIP, NEXT_FAR = range(4)

HBM = pl.BlockSpec(memory_space=pltpu.HBM)
VMEM = pl.BlockSpec(memory_space=pltpu.VMEM)
PARAMS = pltpu.CompilerParams(vmem_limit_bytes=16 * 1024 * 1024)


def cost(flops, moved):
    return pl.CostEstimate(flops=flops, bytes_accessed=moved, transcendentals=0)


def odd_device():
    return lax.axis_index("seq") % 2


def first_step(half):
    odd = odd_device()
    return {
        CHIP: WIN * (1 - odd),
        FAR: WIN * odd,
        NEXT_CHIP: 2 * WIN * (1 - odd) - WIN * odd,
        NEXT_FAR: 2 * WIN * odd - WIN * (1 - odd),
    }[half]


def same(count):
    return lax.broadcasted_iota(jnp.int32, (count, count), 0) == lax.broadcasted_iota(
        jnp.int32, (count, count), 1
    )


def squares_row(rows):
    gram = lax.dot_general(
        rows, rows, (((1,), (1,)), ((), ())), preferred_element_type=jnp.float32
    )
    return jnp.sum(jnp.where(same(rows.shape[0]), gram, 0.0), axis=0, keepdims=True)


def fill_masks(first_ref, pad_ref, time_ref, station_ref, stations, total_steps):
    own = 2 * WIN * stations
    keys, columns = 2 * own, GROUP * own
    key = lax.broadcasted_iota(jnp.int32, (keys, columns), 0)
    query = lax.broadcasted_iota(jnp.int32, (keys, columns), 1) % own

    def time_of(row):
        half, step = row // (WIN * stations), (row // stations) % WIN
        start = jnp.where(half == CHIP, first_step(CHIP), first_step(FAR))
        start = jnp.where(half == NEXT_CHIP, first_step(NEXT_CHIP), start)
        return step + jnp.where(half == NEXT_FAR, first_step(NEXT_FAR), start)

    key_station, query_station = key % stations, query % stations
    key_time, query_time = time_of(key), time_of(query)
    same_station = key_station == query_station
    same_time = key_time == query_time
    near = jnp.abs(key_time - query_time) <= WIN
    step = lax.axis_index("seq") * (2 * WIN) + key_time
    for m in range(time_ref.shape[0]):
        first = jnp.zeros((keys, columns), jnp.int32)
        pad = jnp.zeros((keys, columns), jnp.int32)
        for s in range(stations):
            first = jnp.where(key_station == s, first_ref[m, s], first)
            pad = jnp.where(key_station == s, pad_ref[m, s], pad)
        recorded = (step >= first) & (step < total_steps - pad)
        time_ref[m] = jnp.where(same_station & near & (recorded | same_time), 0.0, -BIG)
        station_ref[m] = jnp.where(same_time & (recorded | same_station), 0.0, -BIG)[:own]


def halves_kernel(signal_hbm, chip_ref, far_ref, signal_ref, arrived):
    copy = pltpu.make_async_copy(signal_hbm, signal_ref, arrived)
    copy.start()
    micro, _, stations, _ = signal_ref.shape
    edge = WIN * stations
    copy.wait()
    for half, half_ref in ((FAR, far_ref), (CHIP, chip_ref)):
        start = first_step(half)
        for m in range(micro):
            for t in range(0, WIN, 2):
                pair = [signal_ref[m, start + t + i].astype(jnp.float32) for i in range(2)]
                at = m * edge + t * stations
                half_ref[at : at + 2 * stations, :] = jnp.concatenate(pair, axis=0).astype(
                    jnp.bfloat16
                )


def fixed_kernel(
    weights_hbm, first_hbm, pad_hbm, _, weights_ref, time_ref, station_ref,
    first_ref, pad_ref, arrived, *, stations, total_steps,
):
    copies = [
        pltpu.make_async_copy(first_hbm, first_ref, arrived.at[0]),
        pltpu.make_async_copy(pad_hbm, pad_ref, arrived.at[1]),
        pltpu.make_async_copy(weights_hbm, weights_ref, arrived.at[2]),
    ]
    for copy in copies:
        copy.start()
    copies[0].wait()
    copies[1].wait()
    fill_masks(first_ref, pad_ref, time_ref, station_ref, stations, total_steps)
    copies[2].wait()


def squares_kernel(*refs):
    out_ref = refs[-1]
    out_ref[...] = jnp.zeros(out_ref.shape, jnp.float32)
    for half, half_ref in enumerate(refs[:-1]):
        out_ref[half : half + 1, 0 : half_ref.shape[0]] = squares_row(half_ref[...])


def norm_kernel(half_ref, squares_ref, normed_ref, *, line):
    rows = half_ref[...]
    count = rows.shape[0]
    total = squares_row(rows) + squares_ref[line : line + 1, 0:count]
    factor = lax.rsqrt(total / (HEADS * HEAD) + EPS)
    column = jnp.sum(jnp.where(same(count), factor, 0.0), axis=1, keepdims=True)
    normed_ref[...] = (rows.astype(jnp.float32) * column).astype(jnp.bfloat16)


def softmax_columns(scores):
    grown = jnp.exp(scores - jnp.max(scores, axis=0, keepdims=True))
    return (grown * (1.0 / jnp.sum(grown, axis=0, keepdims=True))).astype(jnp.bfloat16)


def layer_kernel(
    chip_ref, far_ref, next_chip_ref, next_far_ref, squares_ref,
    time_ref, station_ref, weights_ref, kept_chip_ref, kept_far_ref, *refs, tick, stations, last,
):
    if last:
        out_ref, normed_ref, projected_ref = refs
    else:
        out_chip_ref, out_far_ref, normed_ref, projected_ref = refs
    edge = WIN * stations
    micro = chip_ref.shape[0] // edge
    own, reach = 2 * edge, 4 * edge
    heads_dev = weights_ref.shape[1]
    width = 3 * HEAD
    bf16, f32 = jnp.bfloat16, jnp.float32
    active = lax.axis_index("section") == tick

    def write(m, lanes, values):
        for half in (CHIP, FAR):
            part = values[half * edge : (half + 1) * edge].astype(bf16)
            if last:
                for t in range(WIN):
                    out_ref[0, m, first_step(half) + t, :, lanes] = part[
                        t * stations : (t + 1) * stations
                    ]
            else:
                half_ref = (out_chip_ref, out_far_ref)[half]
                half_ref[m * edge : (m + 1) * edge, lanes] = part

    def norm_rows(half, half_ref, squares_row_ref, complete):
        lane = lax.broadcasted_iota(jnp.int32, (micro * edge, 128), 1)
        row = lax.broadcasted_iota(jnp.int32, (micro * edge, 128), 0)
        total = jnp.where(lane == row, squares_row_ref, 0.0)
        if not complete:
            for head in range(heads_dev):
                part = half_ref[:, head * HEAD : (head + 1) * HEAD].astype(f32)
                total = total + part * part
        factor = lax.rsqrt(jnp.sum(total, axis=1, keepdims=True) / (HEADS * HEAD) + EPS)
        for head in range(heads_dev):
            lanes = slice(head * HEAD, (head + 1) * HEAD)
            put_normed(half, lanes, (half_ref[:, lanes].astype(f32) * factor).astype(bf16))

    def put_normed(half, lanes, rows):
        for m in range(micro):
            at = m * reach + half * edge
            normed_ref[at : at + edge, lanes] = rows[m * edge : (m + 1) * edge]

    @pl.when(active)
    def _():
        if tick == 0:
            for half, half_ref in enumerate((chip_ref, far_ref, next_chip_ref, next_far_ref)):
                norm_rows(half, half_ref, squares_ref[half : half + 1, :], True)
        else:
            norm_rows(CHIP, chip_ref, squares_ref[CHIP : CHIP + 1, :], False)
            norm_rows(FAR, far_ref, squares_ref[FAR : FAR + 1, :], False)
            put_normed(NEXT_CHIP, slice(None), next_chip_ref[...])
            put_normed(NEXT_FAR, slice(None), next_far_ref[...])
        for head in range(heads_dev):
            projected_ref[:, head * width : (head + 1) * width] = jnp.dot(
                normed_ref[:, head * HEAD : (head + 1) * HEAD],
                weights_ref[0, head],
                preferred_element_type=f32,
            ).astype(bf16)
        pairs = [(g, m) for g in range(heads_dev // GROUP) for m in range(micro)]
        blank = jnp.zeros((own, HEAD), bf16)
        scores = []
        for g, m in pairs:
            at = [(g * GROUP + j) * width for j in range(GROUP)]
            first = m * reach
            spread = jnp.concatenate(
                [
                    jnp.concatenate(
                        [
                            projected_ref[first : first + own, at[j] : at[j] + HEAD]
                            if i == j
                            else blank
                            for i in range(GROUP)
                        ],
                        axis=1,
                    )
                    for j in range(GROUP)
                ],
                axis=0,
            )
            keys = jnp.concatenate(
                [projected_ref[first : first + reach, a + HEAD : a + 2 * HEAD] for a in at], axis=1
            )
            scores.append(
                lax.dot_general(
                    keys, spread, (((1,), (1,)), ((), ())), preferred_element_type=f32
                )
                * (1.0 / math.sqrt(HEAD))
            )
        mixes = []
        for (g, m), score in zip(pairs, scores):
            time_weights = softmax_columns(score + time_ref[m])
            station_weights = softmax_columns(score[:own] + station_ref[m])
            mixes.append(jnp.concatenate([time_weights, station_weights], axis=0).T)
        for (g, m), mix in zip(pairs, mixes):
            first = m * reach
            for j in range(GROUP):
                head = g * GROUP + j
                at = head * width + 2 * HEAD
                mixed = jnp.dot(
                    mix[j * own : (j + 1) * own],
                    jnp.concatenate(
                        [
                            projected_ref[first : first + reach, at : at + HEAD],
                            projected_ref[first : first + own, at : at + HEAD],
                        ],
                        axis=0,
                    ),
                    preferred_element_type=f32,
                )
                lanes = slice(head * HEAD, (head + 1) * HEAD)
                hidden = jnp.concatenate(
                    [ref[m * edge : (m + 1) * edge, lanes] for ref in (chip_ref, far_ref)], axis=0
                )
                result = hidden.astype(f32) + mixed
                write(m, lanes, result)

    @pl.when(jnp.logical_not(active))
    def _():
        for m in range(micro):
            for head in range(heads_dev):
                lanes = slice(head * HEAD, (head + 1) * HEAD)
                kept = [
                    ref[m * edge : (m + 1) * edge, lanes] for ref in (kept_chip_ref, kept_far_ref)
                ]
                write(m, lanes, jnp.concatenate(kept, axis=0).astype(f32))


def body(signal, head_proj, record_start, record_pad):
    section_count = lax.axis_size("section")
    seq_count = lax.axis_size("seq")
    rep_count = lax.axis_size("rep")
    micro, steps, stations, features = signal.shape
    heads_dev = head_proj.shape[1]
    edge = WIN * stations
    own, reach = 2 * edge, 4 * edge
    bf16, f32 = jnp.bfloat16, jnp.float32
    half_shape = jax.ShapeDtypeStruct((micro * edge, features), bf16)
    squares_shape = jax.ShapeDtypeStruct((8, 128), f32)
    signal_bytes = signal.size * 2

    def in_hbm(block):
        return pltpu.with_memory_space_constraint(block, pltpu.HBM)

    def squares_of(*halves):
        return pl.pallas_call(
            squares_kernel,
            in_specs=[VMEM] * len(halves),
            out_specs=VMEM,
            out_shape=squares_shape,
            compiler_params=PARAMS,
            name="squares",
        )(*halves)

    def normed(rows, squares, line):
        return pl.pallas_call(
            lambda *refs: norm_kernel(*refs, line=line),
            in_specs=[VMEM] * 2,
            out_specs=VMEM,
            out_shape=half_shape,
            compiler_params=PARAMS,
            cost_estimate=cost(2000000000, 4 * half_shape.size),
            name="norm",
        )(rows, squares)

    chip, far = pl.pallas_call(
        halves_kernel,
        in_specs=[HBM],
        out_specs=[VMEM] * 2,
        out_shape=[half_shape] * 2,
        scratch_shapes=[pltpu.VMEM(signal.shape, bf16), pltpu.SemaphoreType.DMA],
        compiler_params=PARAMS,
        cost_estimate=cost(signal.size, 2 * signal_bytes),
        name="halves",
    )(in_hbm(signal))
    weights, time_bias, station_bias = pl.pallas_call(
        lambda *refs: fixed_kernel(*refs, stations=stations, total_steps=steps * seq_count),
        in_specs=[HBM] * 3 + [VMEM],
        out_specs=[VMEM] * 3,
        out_shape=[
            jax.ShapeDtypeStruct(head_proj.shape, bf16),
            jax.ShapeDtypeStruct((micro, reach, GROUP * own), f32),
            jax.ShapeDtypeStruct((micro, own, GROUP * own), f32),
        ],
        scratch_shapes=[
            pltpu.SMEM(record_start.shape, jnp.int32),
            pltpu.SMEM(record_pad.shape, jnp.int32),
            pltpu.SemaphoreType.DMA((3,)),
        ],
        compiler_params=PARAMS,
        cost_estimate=cost(signal.size, 2 * head_proj.size),
        name="fixed",
    )(in_hbm(head_proj), in_hbm(record_start), in_hbm(record_pad), chip)

    def moved(block, source, target, hop, other=False):
        route = []
        for i in range(seq_count):
            to = i if hop == 0 else i + 1 - 2 * (i % 2) if hop == 1 else i - 1 + 2 * (i % 2)
            if 0 <= to < seq_count:
                for r in range(rep_count):
                    route.append(
                        (
                            (source * seq_count + i) * rep_count + r,
                            (target * seq_count + to) * rep_count
                            + ((r + 1) % rep_count if other else r),
                        )
                    )
        return lax.ppermute(block, ("section", "seq", "rep"), route)

    next_far = moved(far, 0, 0, 2)
    next_chip = moved(chip, 0, 0, 1)
    squares = squares_of(chip, far, next_chip, next_far)
    squares = lax.psum(squares, "rep")
    kept = (chip, far)
    for tick in range(section_count):
        last = tick + 1 == section_count

        def kernel(*refs, tick=tick, last=last):
            layer_kernel(*refs, tick=tick, stations=stations, last=last)

        out_shape = (
            [jax.ShapeDtypeStruct((1,) + signal.shape, bf16)]
            if last
            else [half_shape, half_shape]
        )
        outputs = pl.pallas_call(
            kernel,
            in_specs=[VMEM] * 10,
            out_specs=[VMEM] * len(out_shape),
            out_shape=out_shape,
            scratch_shapes=[
                pltpu.VMEM((micro * reach, features), bf16),
                pltpu.VMEM((micro * reach, heads_dev * 3 * HEAD), bf16),
            ],
            compiler_params=PARAMS,
            cost_estimate=cost(8 * signal.size * 3 * HEAD, 16 * signal_bytes),
            name="layer",
        )(
            chip, far, next_chip, next_far, squares,
            time_bias, station_bias, weights, *kept,
        )
        if last:
            return outputs[0]
        kept = outputs
        mine = squares_of(*kept)
        chip = moved(kept[0], tick, tick + 1, 0)
        next_far = moved(kept[1], tick, tick + 1, 2)
        far = moved(kept[1], tick, tick + 1, 0)
        squares = moved(mine, tick, tick + 1, 0, other=True)
        far_squares = moved(mine, tick, tick + 1, 2, other=True)
        next_chip = moved(normed(chip, squares, CHIP), tick + 1, tick + 1, 1)
        next_far = normed(next_far, far_squares, FAR)


def solution(mesh):
    return jax.shard_map(
        body,
        mesh=mesh,
        in_specs=(P(None, "seq", None, "rep"), P("section", "rep", None, None), P(), P()),
        out_specs=P("section", None, "seq", None, "rep"),
        check_vma=False,
    )
```

```python
import math

import jax
import jax.numpy as jnp
from jax import lax
from jax.experimental import pallas as pl
from jax.experimental.pallas import tpu as pltpu
from jax.sharding import PartitionSpec as P

HEADS = 32
HEAD = 128
WIN = 4
GROUP = 4
EPS = 1e-06
BIG = 1e30
CHIP, FAR, NEXT_CHIP, NEXT_FAR = range(4)

HBM = pl.BlockSpec(memory_space=pltpu.HBM)
VMEM = pl.BlockSpec(memory_space=pltpu.VMEM)
BUSY = pl.CostEstimate(flops=2000000000, bytes_accessed=300000, transcendentals=0)
PARAMS = pltpu.CompilerParams(vmem_limit_bytes=16 * 1024 * 1024)


def cost(flops, moved):
    return pl.CostEstimate(flops=flops, bytes_accessed=moved, transcendentals=0)


def odd_device():
    return lax.axis_index("seq") % 2


def first_step(half):
    odd = odd_device()
    return {
        CHIP: WIN * (1 - odd),
        FAR: WIN * odd,
        NEXT_CHIP: 2 * WIN * (1 - odd) - WIN * odd,
        NEXT_FAR: 2 * WIN * odd - WIN * (1 - odd),
    }[half]


def same(count):
    return lax.broadcasted_iota(jnp.int32, (count, count), 0) == lax.broadcasted_iota(
        jnp.int32, (count, count), 1
    )


def squares_row(rows):
    gram = lax.dot_general(
        rows, rows, (((1,), (1,)), ((), ())), preferred_element_type=jnp.float32
    )
    return jnp.sum(jnp.where(same(rows.shape[0]), gram, 0.0), axis=0, keepdims=True)


def fill_masks(first_ref, pad_ref, time_ref, station_ref, stations, total_steps):
    own = 2 * WIN * stations
    keys, columns = 2 * own, GROUP * own
    key = lax.broadcasted_iota(jnp.int32, (keys, columns), 0)
    query = lax.broadcasted_iota(jnp.int32, (keys, columns), 1) % own

    def time_of(row):
        half, step = row // (WIN * stations), (row // stations) % WIN
        start = jnp.where(half == CHIP, first_step(CHIP), first_step(FAR))
        start = jnp.where(half == NEXT_CHIP, first_step(NEXT_CHIP), start)
        return step + jnp.where(half == NEXT_FAR, first_step(NEXT_FAR), start)

    key_station, query_station = key % stations, query % stations
    key_time, query_time = time_of(key), time_of(query)
    same_station = key_station == query_station
    same_time = key_time == query_time
    near = jnp.abs(key_time - query_time) <= WIN
    step = lax.axis_index("seq") * (2 * WIN) + key_time
    for m in range(time_ref.shape[0]):
        first = jnp.zeros((keys, columns), jnp.int32)
        pad = jnp.zeros((keys, columns), jnp.int32)
        for s in range(stations):
            first = jnp.where(key_station == s, first_ref[m, s], first)
            pad = jnp.where(key_station == s, pad_ref[m, s], pad)
        recorded = (step >= first) & (step < total_steps - pad)
        time_ref[m] = jnp.where(same_station & near & (recorded | same_time), 0.0, -BIG)
        station_ref[m] = jnp.where(same_time & (recorded | same_station), 0.0, -BIG)[:own]


def halves_kernel(signal_hbm, chip_ref, far_ref, squares_ref, signal_ref, arrived):
    copy = pltpu.make_async_copy(signal_hbm, signal_ref, arrived)
    copy.start()
    micro, _, stations, _ = signal_ref.shape
    edge = WIN * stations
    copy.wait()
    for half, half_ref in ((FAR, far_ref), (CHIP, chip_ref)):
        start = first_step(half)
        for m in range(micro):
            for t in range(0, WIN, 2):
                pair = [signal_ref[m, start + t + i].astype(jnp.float32) for i in range(2)]
                at = m * edge + t * stations
                half_ref[at : at + 2 * stations, :] = jnp.concatenate(pair, axis=0).astype(
                    jnp.bfloat16
                )
    squares_kernel(chip_ref, far_ref, squares_ref)


def fixed_kernel(
    weights_hbm, first_hbm, pad_hbm, _, weights_ref, time_ref, station_ref,
    first_ref, pad_ref, arrived, *, stations, total_steps,
):
    copies = [
        pltpu.make_async_copy(first_hbm, first_ref, arrived.at[0]),
        pltpu.make_async_copy(pad_hbm, pad_ref, arrived.at[1]),
        pltpu.make_async_copy(weights_hbm, weights_ref, arrived.at[2]),
    ]
    for copy in copies:
        copy.start()
    copies[0].wait()
    copies[1].wait()
    fill_masks(first_ref, pad_ref, time_ref, station_ref, stations, total_steps)
    copies[2].wait()


def squares_kernel(*refs):
    out_ref = refs[-1]
    out_ref[...] = jnp.zeros(out_ref.shape, jnp.float32)
    for half, half_ref in enumerate(refs[:-1]):
        out_ref[half : half + 1, 0 : half_ref.shape[0]] = squares_row(half_ref[...])


def scaled(rows, total):
    count = rows.shape[0]
    factor = lax.rsqrt(total / (HEADS * HEAD) + EPS)
    column = jnp.sum(jnp.where(same(count), factor, 0.0), axis=1, keepdims=True)
    return (rows.astype(jnp.float32) * column).astype(jnp.bfloat16)


def first_norm_kernel(half_ref, squares_ref, *refs, line):
    rows = half_ref[...]
    refs[-1][...] = scaled(rows, squares_ref[line : line + 1, 0 : rows.shape[0]])


def norm_kernel(half_ref, squares_ref, normed_ref, *, line):
    rows = half_ref[...]
    normed_ref[...] = scaled(
        rows, squares_row(rows) + squares_ref[line : line + 1, 0 : rows.shape[0]]
    )


def project_kernel(weights_ref, *refs):
    count = len(refs) // 2
    halves, outs = refs[:count], refs[count:]
    rows = halves[0].shape[0]
    width = 3 * HEAD
    for head in range(weights_ref.shape[1]):
        lanes = slice(head * HEAD, (head + 1) * HEAD)
        projected = jnp.dot(
            jnp.concatenate([half[:, lanes] for half in halves], axis=0),
            weights_ref[0, head],
            preferred_element_type=jnp.float32,
        ).astype(jnp.bfloat16)
        for i, out in enumerate(outs):
            out[:, head * width : (head + 1) * width] = projected[i * rows : (i + 1) * rows]


def softmax_columns(scores):
    grown = jnp.exp(scores - jnp.max(scores, axis=0, keepdims=True))
    return (grown * (1.0 / jnp.sum(grown, axis=0, keepdims=True))).astype(jnp.bfloat16)


def layer_kernel(
    chip_ref, far_ref, squares_ref, time_ref, station_ref, weights_ref, kept_chip_ref, kept_far_ref,
    *refs, tick, stations, last,
):
    edge = WIN * stations
    micro = chip_ref.shape[0] // edge
    own = 2 * edge
    heads_dev = weights_ref.shape[1]
    width = 3 * HEAD
    bf16, f32 = jnp.bfloat16, jnp.float32
    active = lax.axis_index("section") == tick
    if tick == 0:
        projected_chip, projected_far, next_far_ref, next_chip_ref, *refs = refs
    else:
        projected_chip, projected_next_chip, projected_next_far, *refs = refs
    if last:
        out_ref, *refs = refs
    else:
        out_chip_ref, out_far_ref, *refs = refs
    if tick == 0:
        projected_next_chip, projected_next_far = refs
    else:
        (projected_far,) = refs
    projected = (projected_chip, projected_far, projected_next_chip, projected_next_far)

    def write(m, lanes, values):
        for half in (CHIP, FAR):
            part = values[half * edge : (half + 1) * edge].astype(bf16)
            if last:
                for t in range(WIN):
                    out_ref[0, m, first_step(half) + t, :, lanes] = part[
                        t * stations : (t + 1) * stations
                    ]
            else:
                half_ref = (out_chip_ref, out_far_ref)[half]
                half_ref[m * edge : (m + 1) * edge, lanes] = part

    def rows_of(halves, m, at):
        return [projected[half][m * edge : (m + 1) * edge, at : at + HEAD] for half in halves]

    @pl.when(active)
    def _():
        if tick == 0:
            project_kernel(
                weights_ref, next_chip_ref, next_far_ref, projected_next_chip, projected_next_far
            )
        else:
            lane = lax.broadcasted_iota(jnp.int32, (micro * edge, 128), 1)
            row = lax.broadcasted_iota(jnp.int32, (micro * edge, 128), 0)
            total = jnp.where(lane == row, squares_ref[FAR : FAR + 1, :], 0.0)
            for head in range(heads_dev):
                part = far_ref[:, head * HEAD : (head + 1) * HEAD].astype(f32)
                total = total + part * part
            factor = lax.rsqrt(jnp.sum(total, axis=1, keepdims=True) / (HEADS * HEAD) + EPS)
            for head in range(heads_dev):
                projected_far[:, head * width : (head + 1) * width] = jnp.dot(
                    (far_ref[:, head * HEAD : (head + 1) * HEAD].astype(f32) * factor).astype(bf16),
                    weights_ref[0, head],
                    preferred_element_type=f32,
                ).astype(bf16)
        pairs = [(g, m) for g in range(heads_dev // GROUP) for m in range(micro)]
        blank = jnp.zeros((own, HEAD), bf16)
        scores = []
        for g, m in pairs:
            at = [(g * GROUP + j) * width for j in range(GROUP)]
            queries = [jnp.concatenate(rows_of((CHIP, FAR), m, a), axis=0) for a in at]
            spread = jnp.concatenate(
                [
                    jnp.concatenate(
                        [queries[j] if i == j else blank for i in range(GROUP)],
                        axis=1,
                    )
                    for j in range(GROUP)
                ],
                axis=0,
            )
            keys = jnp.concatenate(
                [jnp.concatenate(rows_of(range(4), m, a + HEAD), axis=0) for a in at], axis=1
            )
            scores.append(
                lax.dot_general(
                    keys, spread, (((1,), (1,)), ((), ())), preferred_element_type=f32
                )
                * (1.0 / math.sqrt(HEAD))
            )
        mixes = []
        for (g, m), score in zip(pairs, scores):
            time_weights = softmax_columns(score + time_ref[m])
            station_weights = softmax_columns(score[:own] + station_ref[m])
            mixes.append(jnp.concatenate([time_weights, station_weights], axis=0).T)
        for (g, m), mix in zip(pairs, mixes):
            for j in range(GROUP):
                head = g * GROUP + j
                at = head * width + 2 * HEAD
                mixed = jnp.dot(
                    mix[j * own : (j + 1) * own],
                    jnp.concatenate(rows_of((0, 1, 2, 3, CHIP, FAR), m, at), axis=0),
                    preferred_element_type=f32,
                )
                lanes = slice(head * HEAD, (head + 1) * HEAD)
                hidden = jnp.concatenate(
                    [ref[m * edge : (m + 1) * edge, lanes] for ref in (chip_ref, far_ref)], axis=0
                )
                result = hidden.astype(f32) + mixed
                write(m, lanes, result)

    @pl.when(jnp.logical_not(active))
    def _():
        for m in range(micro):
            for head in range(heads_dev):
                lanes = slice(head * HEAD, (head + 1) * HEAD)
                kept = [
                    ref[m * edge : (m + 1) * edge, lanes] for ref in (kept_chip_ref, kept_far_ref)
                ]
                write(m, lanes, jnp.concatenate(kept, axis=0).astype(f32))


def body(signal, head_proj, record_start, record_pad):
    section_count = lax.axis_size("section")
    seq_count = lax.axis_size("seq")
    rep_count = lax.axis_size("rep")
    micro, steps, stations, features = signal.shape
    heads_dev = head_proj.shape[1]
    edge = WIN * stations
    own, reach = 2 * edge, 4 * edge
    bf16, f32 = jnp.bfloat16, jnp.float32
    half_shape = jax.ShapeDtypeStruct((micro * edge, features), bf16)
    squares_shape = jax.ShapeDtypeStruct((8, 128), f32)
    projected_shape = jax.ShapeDtypeStruct((micro * edge, heads_dev * 3 * HEAD), bf16)
    signal_bytes = signal.size * 2

    def in_hbm(block):
        return pltpu.with_memory_space_constraint(block, pltpu.HBM)

    def squares_of(*halves):
        return pl.pallas_call(
            squares_kernel,
            in_specs=[VMEM] * len(halves),
            out_specs=VMEM,
            out_shape=squares_shape,
            compiler_params=PARAMS,
            name="squares",
        )(*halves)

    def normed(rows, squares, line):
        return pl.pallas_call(
            lambda *refs: norm_kernel(*refs, line=line),
            in_specs=[VMEM] * 2,
            out_specs=VMEM,
            out_shape=half_shape,
            compiler_params=PARAMS,
            cost_estimate=BUSY,
            name="norm",
        )(rows, squares)

    def project(*halves):
        return pl.pallas_call(
            project_kernel,
            in_specs=[VMEM] * (1 + len(halves)),
            out_specs=[VMEM] * len(halves),
            out_shape=[projected_shape] * len(halves),
            compiler_params=PARAMS,
            cost_estimate=BUSY,
            name="project",
        )(weights, *halves)

    chip, far, squares = pl.pallas_call(
        halves_kernel,
        in_specs=[HBM],
        out_specs=[VMEM] * 3,
        out_shape=[half_shape, half_shape, squares_shape],
        scratch_shapes=[pltpu.VMEM(signal.shape, bf16), pltpu.SemaphoreType.DMA],
        compiler_params=PARAMS,
        cost_estimate=cost(signal.size, 2 * signal_bytes),
        name="halves",
    )(in_hbm(signal))
    squares = lax.psum(squares, "rep")
    def first_normed(line, *operands):
        return pl.pallas_call(
            lambda *refs: first_norm_kernel(*refs, line=line),
            in_specs=[VMEM] * len(operands),
            out_specs=VMEM,
            out_shape=half_shape,
            compiler_params=PARAMS,
            cost_estimate=BUSY,
            name="norm",
        )(*operands)

    normed_far = first_normed(FAR, far, squares)
    normed_chip = first_normed(CHIP, chip, squares, normed_far)
    weights, time_bias, station_bias = pl.pallas_call(
        lambda *refs: fixed_kernel(*refs, stations=stations, total_steps=steps * seq_count),
        in_specs=[HBM] * 3 + [VMEM],
        out_specs=[VMEM] * 3,
        out_shape=[
            jax.ShapeDtypeStruct(head_proj.shape, bf16),
            jax.ShapeDtypeStruct((micro, reach, GROUP * own), f32),
            jax.ShapeDtypeStruct((micro, own, GROUP * own), f32),
        ],
        scratch_shapes=[
            pltpu.SMEM(record_start.shape, jnp.int32),
            pltpu.SMEM(record_pad.shape, jnp.int32),
            pltpu.SemaphoreType.DMA((3,)),
        ],
        compiler_params=PARAMS,
        cost_estimate=cost(signal.size, 2 * head_proj.size),
        name="fixed",
    )(in_hbm(head_proj), in_hbm(record_start), in_hbm(record_pad), normed_chip)

    def moved(block, source, target, hop, other=False):
        route = []
        for i in range(seq_count):
            to = i if hop == 0 else i + 1 - 2 * (i % 2) if hop == 1 else i - 1 + 2 * (i % 2)
            if 0 <= to < seq_count:
                for r in range(rep_count):
                    route.append(
                        (
                            (source * seq_count + i) * rep_count + r,
                            (target * seq_count + to) * rep_count
                            + ((r + 1) % rep_count if other else r),
                        )
                    )
        return lax.ppermute(block, ("section", "seq", "rep"), route)

    next_far = moved(normed_far, 0, 0, 2)
    next_chip = moved(normed_chip, 0, 0, 1)
    inputs = (*project(normed_chip, normed_far), next_far, next_chip)
    kept = (chip, far)
    for tick in range(section_count):
        last = tick + 1 == section_count

        def kernel(*refs, tick=tick, last=last):
            layer_kernel(*refs, tick=tick, stations=stations, last=last)

        out_shape = (
            [jax.ShapeDtypeStruct((1,) + signal.shape, bf16)]
            if last
            else [half_shape, half_shape]
        )
        outputs = pl.pallas_call(
            kernel,
            in_specs=[VMEM] * (8 + len(inputs)),
            out_specs=[VMEM] * len(out_shape),
            out_shape=out_shape,
            scratch_shapes=[pltpu.VMEM(projected_shape.shape, bf16)] * (2 if tick == 0 else 1),
            compiler_params=PARAMS,
            cost_estimate=cost(8 * signal.size * 3 * HEAD, 16 * signal_bytes),
            name="layer",
        )(
            chip, far, squares, time_bias, station_bias, weights, *kept, *inputs,
        )
        if last:
            return outputs[0]
        kept = outputs
        mine = squares_of(*kept)
        chip = moved(kept[0], tick, tick + 1, 0)
        next_far = moved(kept[1], tick, tick + 1, 2)
        far = moved(kept[1], tick, tick + 1, 0)
        squares = moved(mine, tick, tick + 1, 0, other=True)
        far_squares = moved(mine, tick, tick + 1, 2, other=True)
        normed_chip = normed(chip, squares, CHIP)
        next_chip = moved(normed_chip, tick + 1, tick + 1, 1)
        next_far = normed(next_far, far_squares, FAR)
        inputs = project(normed_chip, next_chip, next_far)


def solution(mesh):
    return jax.shard_map(
        body,
        mesh=mesh,
        in_specs=(P(None, "seq", None, "rep"), P("section", "rep", None, None), P(), P()),
        out_specs=P("section", None, "seq", None, "rep"),
        check_vma=False,
    )
```

```python
import math

import jax
import jax.numpy as jnp
from jax import lax
from jax.experimental import pallas as pl
from jax.experimental.pallas import tpu as pltpu
from jax.sharding import PartitionSpec as P

HEADS = 32
HEAD = 128
WIN = 4
GROUP = 4
EPS = 1e-06
BIG = 1e30
CHIP, FAR, NEXT_FAR, NEXT_CHIP = range(4)

HBM = pl.BlockSpec(memory_space=pltpu.HBM)
VMEM = pl.BlockSpec(memory_space=pltpu.VMEM)
BUSY = pl.CostEstimate(flops=2000000000, bytes_accessed=300000, transcendentals=0)
PARAMS = pltpu.CompilerParams(vmem_limit_bytes=16 * 1024 * 1024)


def cost(flops, moved):
    return pl.CostEstimate(flops=flops, bytes_accessed=moved, transcendentals=0)


def odd_device():
    return lax.axis_index("seq") % 2


def first_step(half):
    odd = odd_device()
    return {
        CHIP: WIN * (1 - odd),
        FAR: WIN * odd,
        NEXT_CHIP: 2 * WIN * (1 - odd) - WIN * odd,
        NEXT_FAR: 2 * WIN * odd - WIN * (1 - odd),
    }[half]


def same(count):
    return lax.broadcasted_iota(jnp.int32, (count, count), 0) == lax.broadcasted_iota(
        jnp.int32, (count, count), 1
    )


def squares_row(rows):
    gram = lax.dot_general(
        rows, rows, (((1,), (1,)), ((), ())), preferred_element_type=jnp.float32
    )
    return jnp.sum(jnp.where(same(rows.shape[0]), gram, 0.0), axis=0, keepdims=True)


def fill_masks(first_ref, pad_ref, time_ref, station_ref, stations, total_steps):
    own = 2 * WIN * stations
    keys, columns = 2 * own, GROUP * own
    key = lax.broadcasted_iota(jnp.int32, (keys, columns), 0)
    query = lax.broadcasted_iota(jnp.int32, (keys, columns), 1) % own

    def time_of(row):
        half, step = row // (WIN * stations), (row // stations) % WIN
        start = jnp.where(half == CHIP, first_step(CHIP), first_step(FAR))
        start = jnp.where(half == NEXT_CHIP, first_step(NEXT_CHIP), start)
        return step + jnp.where(half == NEXT_FAR, first_step(NEXT_FAR), start)

    key_station, query_station = key % stations, query % stations
    key_time, query_time = time_of(key), time_of(query)
    same_station = key_station == query_station
    same_time = key_time == query_time
    near = jnp.abs(key_time - query_time) <= WIN
    step = lax.axis_index("seq") * (2 * WIN) + key_time
    for m in range(time_ref.shape[0]):
        first = jnp.zeros((keys, columns), jnp.int32)
        pad = jnp.zeros((keys, columns), jnp.int32)
        for s in range(stations):
            first = jnp.where(key_station == s, first_ref[m, s], first)
            pad = jnp.where(key_station == s, pad_ref[m, s], pad)
        recorded = (step >= first) & (step < total_steps - pad)
        time_ref[m] = jnp.where(same_station & near & (recorded | same_time), 0.0, -BIG)
        station_ref[m] = jnp.where(same_time & (recorded | same_station), 0.0, -BIG)[:own]


def first_kernel(
    signal_hbm, weights_hbm, first_hbm, pad_hbm, chip_ref, far_ref, weights_ref, time_ref, station_ref,
    signal_ref, first_ref, pad_ref, arrived, *, total_steps,
):
    copies = [
        pltpu.make_async_copy(signal_hbm, signal_ref, arrived.at[0]),
        pltpu.make_async_copy(first_hbm, first_ref, arrived.at[1]),
        pltpu.make_async_copy(pad_hbm, pad_ref, arrived.at[2]),
        pltpu.make_async_copy(weights_hbm, weights_ref, arrived.at[3]),
    ]
    for copy in copies:
        copy.start()
    micro, _, stations, _ = signal_ref.shape
    edge = WIN * stations
    copies[1].wait()
    copies[2].wait()
    fill_masks(first_ref, pad_ref, time_ref, station_ref, stations, total_steps)
    copies[0].wait()
    for half, half_ref in ((FAR, far_ref), (CHIP, chip_ref)):
        start = first_step(half)
        for m in range(micro):
            for t in range(0, WIN, 2):
                pair = [signal_ref[m, start + t + i].astype(jnp.float32) for i in range(2)]
                at = m * edge + t * stations
                half_ref[at : at + 2 * stations, :] = jnp.concatenate(pair, axis=0).astype(
                    jnp.bfloat16
                )
    copies[3].wait()


def squares_kernel(*refs):
    out_ref = refs[-1]
    out_ref[...] = jnp.zeros(out_ref.shape, jnp.float32)
    for half, half_ref in enumerate(refs[:-1]):
        out_ref[half : half + 1, 0 : half_ref.shape[0]] = squares_row(half_ref[...])


def scaled(rows, total):
    count = rows.shape[0]
    factor = lax.rsqrt(total / (HEADS * HEAD) + EPS)
    column = jnp.sum(jnp.where(same(count), factor, 0.0), axis=1, keepdims=True)
    return (rows.astype(jnp.float32) * column).astype(jnp.bfloat16)


def norm_kernel(half_ref, squares_ref, normed_ref, *, line):
    rows = half_ref[...]
    normed_ref[...] = scaled(
        rows, squares_row(rows) + squares_ref[line : line + 1, 0 : rows.shape[0]]
    )


def copy_kernel(squares_ref, half_ref, squares_out_ref, half_out_ref):
    squares_out_ref[...] = squares_ref[...]
    half_out_ref[...] = half_ref[...]


def add_kernel(mine_ref, other_ref, out_ref):
    out_ref[...] = jnp.zeros(out_ref.shape, jnp.float32)
    out_ref[0:1, :] = mine_ref[0:1, :] + other_ref[FAR : FAR + 1, :]


def project_kernel(weights_ref, *refs):
    count = len(refs) // 2
    halves, outs = refs[:count], refs[count:]
    rows = halves[0].shape[0]
    width = 3 * HEAD
    for head in range(weights_ref.shape[1]):
        lanes = slice(head * HEAD, (head + 1) * HEAD)
        projected = jnp.dot(
            jnp.concatenate([half[:, lanes] for half in halves], axis=0),
            weights_ref[0, head],
            preferred_element_type=jnp.float32,
        ).astype(jnp.bfloat16)
        for i, out in enumerate(outs):
            out[:, head * width : (head + 1) * width] = projected[i * rows : (i + 1) * rows]


def softmax_columns(scores):
    grown = jnp.exp(scores - jnp.max(scores, axis=0, keepdims=True))
    return (grown * (1.0 / jnp.sum(grown, axis=0, keepdims=True))).astype(jnp.bfloat16)


def layer_kernel(
    chip_ref, far_ref, squares_ref, time_ref, station_ref, weights_ref, kept_chip_ref, kept_far_ref,
    *refs, tick, stations, last,
):
    edge = WIN * stations
    micro = chip_ref.shape[0] // edge
    own = 2 * edge
    heads_dev = weights_ref.shape[1]
    width = 3 * HEAD
    bf16, f32 = jnp.bfloat16, jnp.float32
    active = lax.axis_index("section") == tick
    projected = [None] * 4
    if tick == 0:
        next_chip_ref, next_far_ref, *refs = refs
        late = [
            (half, half_ref, squares_ref[half : half + 1, :], True)
            for half, half_ref in enumerate((chip_ref, far_ref, next_far_ref, next_chip_ref))
        ]
    else:
        next_far_ref, far_squares_ref, projected[CHIP], projected[NEXT_CHIP], *refs = refs
        late = [
            (FAR, far_ref, squares_ref[FAR : FAR + 1, :], False),
            (NEXT_FAR, next_far_ref, far_squares_ref[0:1, :], True),
        ]
    outs, refs = (refs[:1], refs[1:]) if last else (refs[:2], refs[2:])
    normed = refs[: len(late)]
    for (half, *_), half_ref in zip(late, refs[len(late) :]):
        projected[half] = half_ref

    def write(m, lanes, values):
        for half in (CHIP, FAR):
            part = values[half * edge : (half + 1) * edge].astype(bf16)
            if last:
                for t in range(WIN):
                    outs[0][0, m, first_step(half) + t, :, lanes] = part[
                        t * stations : (t + 1) * stations
                    ]
            else:
                outs[half][m * edge : (m + 1) * edge, lanes] = part

    def rows_of(halves, m, at):
        return [projected[half][m * edge : (m + 1) * edge, at : at + HEAD] for half in halves]

    @pl.when(active)
    def _():
        lane = lax.broadcasted_iota(jnp.int32, (micro * edge, 128), 1)
        row = lax.broadcasted_iota(jnp.int32, (micro * edge, 128), 0)
        for (_, half_ref, line, complete), normed_ref in zip(late, normed):
            total = jnp.where(lane == row, line, 0.0)
            if not complete:
                for head in range(heads_dev):
                    part = half_ref[:, head * HEAD : (head + 1) * HEAD].astype(f32)
                    total = total + part * part
            factor = lax.rsqrt(jnp.sum(total, axis=1, keepdims=True) / (HEADS * HEAD) + EPS)
            normed_ref[...] = (half_ref[...].astype(f32) * factor).astype(bf16)
        project_kernel(weights_ref, *normed, *[projected[half] for half, *_ in late])
        pairs = [(g, m) for g in range(heads_dev // GROUP) for m in range(micro)]
        blank = jnp.zeros((own, HEAD), bf16)
        scores = []
        for g, m in pairs:
            at = [(g * GROUP + j) * width for j in range(GROUP)]
            queries = [jnp.concatenate(rows_of((CHIP, FAR), m, a), axis=0) for a in at]
            spread = jnp.concatenate(
                [
                    jnp.concatenate(
                        [queries[j] if i == j else blank for i in range(GROUP)],
                        axis=1,
                    )
                    for j in range(GROUP)
                ],
                axis=0,
            )
            keys = jnp.concatenate(
                [jnp.concatenate(rows_of(range(4), m, a + HEAD), axis=0) for a in at], axis=1
            )
            scores.append(
                lax.dot_general(
                    keys, spread, (((1,), (1,)), ((), ())), preferred_element_type=f32
                )
                * (1.0 / math.sqrt(HEAD))
            )
        mixes = []
        for (g, m), score in zip(pairs, scores):
            time_weights = softmax_columns(score + time_ref[m])
            station_weights = softmax_columns(score[:own] + station_ref[m])
            mixes.append(jnp.concatenate([time_weights, station_weights], axis=0).T)
        for (g, m), mix in zip(pairs, mixes):
            for j in range(GROUP):
                head = g * GROUP + j
                at = head * width + 2 * HEAD
                mixed = jnp.dot(
                    mix[j * own : (j + 1) * own],
                    jnp.concatenate(rows_of((0, 1, 2, 3, CHIP, FAR), m, at), axis=0),
                    preferred_element_type=f32,
                )
                lanes = slice(head * HEAD, (head + 1) * HEAD)
                hidden = jnp.concatenate(
                    [ref[m * edge : (m + 1) * edge, lanes] for ref in (chip_ref, far_ref)], axis=0
                )
                result = hidden.astype(f32) + mixed
                write(m, lanes, result)

    @pl.when(jnp.logical_not(active))
    def _():
        for m in range(micro):
            for head in range(heads_dev):
                lanes = slice(head * HEAD, (head + 1) * HEAD)
                kept = [
                    ref[m * edge : (m + 1) * edge, lanes] for ref in (kept_chip_ref, kept_far_ref)
                ]
                write(m, lanes, jnp.concatenate(kept, axis=0).astype(f32))


def body(signal, head_proj, record_start, record_pad):
    section_count = lax.axis_size("section")
    seq_count = lax.axis_size("seq")
    rep_count = lax.axis_size("rep")
    micro, steps, stations, features = signal.shape
    heads_dev = head_proj.shape[1]
    edge = WIN * stations
    own, reach = 2 * edge, 4 * edge
    bf16, f32 = jnp.bfloat16, jnp.float32
    half_shape = jax.ShapeDtypeStruct((micro * edge, features), bf16)
    squares_shape = jax.ShapeDtypeStruct((8, 128), f32)
    projected_shape = jax.ShapeDtypeStruct((micro * edge, heads_dev * 3 * HEAD), bf16)
    signal_bytes = signal.size * 2

    def in_hbm(block):
        return pltpu.with_memory_space_constraint(block, pltpu.HBM)

    def squares_of(*halves):
        return pl.pallas_call(
            squares_kernel,
            in_specs=[VMEM] * len(halves),
            out_specs=VMEM,
            out_shape=squares_shape,
            compiler_params=PARAMS,
            name="squares",
        )(*halves)

    def normed(rows, squares, line):
        return pl.pallas_call(
            lambda *refs: norm_kernel(*refs, line=line),
            in_specs=[VMEM] * 2,
            out_specs=VMEM,
            out_shape=half_shape,
            compiler_params=PARAMS,
            cost_estimate=BUSY,
            name="norm",
        )(rows, squares)

    def project(*halves):
        return pl.pallas_call(
            project_kernel,
            in_specs=[VMEM] * (1 + len(halves)),
            out_specs=[VMEM] * len(halves),
            out_shape=[projected_shape] * len(halves),
            compiler_params=PARAMS,
            cost_estimate=BUSY,
            name="project",
        )(weights, *halves)

    chip, far, weights, time_bias, station_bias = pl.pallas_call(
        lambda *refs: first_kernel(*refs, total_steps=steps * seq_count),
        in_specs=[HBM] * 4,
        out_specs=[VMEM] * 5,
        out_shape=[
            half_shape,
            half_shape,
            jax.ShapeDtypeStruct(head_proj.shape, bf16),
            jax.ShapeDtypeStruct((micro, reach, GROUP * own), f32),
            jax.ShapeDtypeStruct((micro, own, GROUP * own), f32),
        ],
        scratch_shapes=[
            pltpu.VMEM(signal.shape, bf16),
            pltpu.SMEM(record_start.shape, jnp.int32),
            pltpu.SMEM(record_pad.shape, jnp.int32),
            pltpu.SemaphoreType.DMA((4,)),
        ],
        compiler_params=PARAMS,
        cost_estimate=cost(signal.size, 2 * head_proj.size),
        name="first",
    )(in_hbm(signal), in_hbm(head_proj), in_hbm(record_start), in_hbm(record_pad))

    def moved(block, source, target, hop, other=False):
        route = []
        for i in range(seq_count):
            to = i if hop == 0 else i + 1 - 2 * (i % 2) if hop == 1 else i - 1 + 2 * (i % 2)
            if 0 <= to < seq_count:
                for r in range(rep_count):
                    route.append(
                        (
                            (source * seq_count + i) * rep_count + r,
                            (target * seq_count + to) * rep_count
                            + ((r + 1) % rep_count if other else r),
                        )
                    )
        return lax.ppermute(block, ("section", "seq", "rep"), route)

    next_far = moved(far, 0, 0, 2)
    next_chip = moved(chip, 0, 0, 1)
    squares = lax.psum(squares_of(chip, far, next_far, next_chip), "rep")
    inputs = (next_chip, next_far)
    kept = (chip, far)
    for tick in range(section_count):
        last = tick + 1 == section_count

        def kernel(*refs, tick=tick, last=last):
            layer_kernel(*refs, tick=tick, stations=stations, last=last)

        out_shape = (
            [jax.ShapeDtypeStruct((1,) + signal.shape, bf16)]
            if last
            else [half_shape, half_shape]
        )
        outputs = pl.pallas_call(
            kernel,
            in_specs=[VMEM] * (8 + len(inputs)),
            out_specs=[VMEM] * len(out_shape),
            out_shape=out_shape,
            scratch_shapes=[
                pltpu.VMEM(shape.shape, bf16)
                for shape in (half_shape, projected_shape)
                for _ in range(4 if tick == 0 else 2)
            ],
            compiler_params=PARAMS,
            cost_estimate=cost(8 * signal.size * 3 * HEAD, 16 * signal_bytes),
            name="layer",
        )(
            chip, far, squares, time_bias, station_bias, weights, *kept, *inputs,
        )
        if last:
            return outputs[0]
        kept = outputs
        mine = squares_of(*kept)
        chip = moved(kept[0], tick, tick + 1, 0)
        next_far = moved(kept[1], tick, tick + 1, 2)
        squares = moved(mine, tick, tick + 1, 0, other=True)
        mine_again, far_again = pl.pallas_call(
            copy_kernel,
            in_specs=[VMEM] * 2,
            out_specs=[VMEM] * 2,
            out_shape=[squares_shape, half_shape],
            compiler_params=PARAMS,
            cost_estimate=BUSY,
            name="copy",
        )(mine, kept[1])
        far = moved(far_again, tick, tick + 1, 0)
        far_squares = moved(mine_again, tick, tick + 1, 2, other=True)
        normed_chip = normed(chip, squares, CHIP)
        next_chip = moved(normed_chip, tick + 1, tick + 1, 1)
        far_squares = pl.pallas_call(
            add_kernel,
            in_specs=[VMEM] * 2,
            out_specs=VMEM,
            out_shape=squares_shape,
            compiler_params=PARAMS,
            cost_estimate=BUSY,
            name="add",
        )(squares_of(next_far), far_squares)
        inputs = (next_far, far_squares, *project(normed_chip, next_chip))


def solution(mesh):
    return jax.shard_map(
        body,
        mesh=mesh,
        in_specs=(P(None, "seq", None, "rep"), P("section", "rep", None, None), P(), P()),
        out_specs=P("section", None, "seq", None, "rep"),
        check_vma=False,
    )
```

```python
import math

import jax
import jax.numpy as jnp
from jax import lax
from jax.experimental import pallas as pl
from jax.experimental.pallas import tpu as pltpu
from jax.sharding import PartitionSpec as P

HEADS = 32
HEAD = 128
WIN = 4
GROUP = 4
EPS = 1e-06
BIG = 1e30
CHIP, FAR, NEXT_FAR, NEXT_CHIP = range(4)

HBM = pl.BlockSpec(memory_space=pltpu.HBM)
VMEM = pl.BlockSpec(memory_space=pltpu.VMEM)
BUSY = pl.CostEstimate(flops=2000000000, bytes_accessed=300000, transcendentals=0)
PARAMS = pltpu.CompilerParams(vmem_limit_bytes=16 * 1024 * 1024)


def cost(flops, moved):
    return pl.CostEstimate(flops=flops, bytes_accessed=moved, transcendentals=0)


def odd_device():
    return lax.axis_index("seq") % 2


def first_step(half):
    odd = odd_device()
    return {
        CHIP: WIN * (1 - odd),
        FAR: WIN * odd,
        NEXT_CHIP: 2 * WIN * (1 - odd) - WIN * odd,
        NEXT_FAR: 2 * WIN * odd - WIN * (1 - odd),
    }[half]


def same(count):
    return lax.broadcasted_iota(jnp.int32, (count, count), 0) == lax.broadcasted_iota(
        jnp.int32, (count, count), 1
    )


def squares_row(rows):
    gram = lax.dot_general(
        rows, rows, (((1,), (1,)), ((), ())), preferred_element_type=jnp.float32
    )
    return jnp.sum(jnp.where(same(rows.shape[0]), gram, 0.0), axis=0, keepdims=True)


def fill_masks(first_ref, pad_ref, time_ref, station_ref, stations, total_steps):
    own = 2 * WIN * stations
    keys, columns = 2 * own, GROUP * own
    key = lax.broadcasted_iota(jnp.int32, (keys, columns), 0)
    query = lax.broadcasted_iota(jnp.int32, (keys, columns), 1) % own

    def time_of(row):
        half, step = row // (WIN * stations), (row // stations) % WIN
        start = jnp.where(half == CHIP, first_step(CHIP), first_step(FAR))
        start = jnp.where(half == NEXT_CHIP, first_step(NEXT_CHIP), start)
        return step + jnp.where(half == NEXT_FAR, first_step(NEXT_FAR), start)

    key_station, query_station = key % stations, query % stations
    key_time, query_time = time_of(key), time_of(query)
    same_station = key_station == query_station
    same_time = key_time == query_time
    near = jnp.abs(key_time - query_time) <= WIN
    step = lax.axis_index("seq") * (2 * WIN) + key_time
    for m in range(time_ref.shape[0]):
        first = jnp.zeros((keys, columns), jnp.int32)
        pad = jnp.zeros((keys, columns), jnp.int32)
        for s in range(stations):
            first = jnp.where(key_station == s, first_ref[m, s], first)
            pad = jnp.where(key_station == s, pad_ref[m, s], pad)
        recorded = (step >= first) & (step < total_steps - pad)
        time_ref[m] = jnp.where(same_station & near & (recorded | same_time), 0.0, -BIG)
        station_ref[m] = jnp.where(same_time & (recorded | same_station), 0.0, -BIG)[:own]


def halves_kernel(signal_hbm, chip_ref, far_ref, signal_ref, arrived):
    copy = pltpu.make_async_copy(signal_hbm, signal_ref, arrived)
    copy.start()
    micro, _, stations, _ = signal_ref.shape
    edge = WIN * stations
    copy.wait()
    for half, half_ref in ((FAR, far_ref), (CHIP, chip_ref)):
        start = first_step(half)
        for m in range(micro):
            for t in range(0, WIN, 2):
                pair = [signal_ref[m, start + t + i].astype(jnp.float32) for i in range(2)]
                at = m * edge + t * stations
                half_ref[at : at + 2 * stations, :] = jnp.concatenate(pair, axis=0).astype(
                    jnp.bfloat16
                )


def fixed_kernel(
    weights_hbm, first_hbm, pad_hbm, _, weights_ref, time_ref, station_ref,
    first_ref, pad_ref, arrived, *, stations, total_steps,
):
    copies = [
        pltpu.make_async_copy(first_hbm, first_ref, arrived.at[0]),
        pltpu.make_async_copy(pad_hbm, pad_ref, arrived.at[1]),
        pltpu.make_async_copy(weights_hbm, weights_ref, arrived.at[2]),
    ]
    for copy in copies:
        copy.start()
    copies[0].wait()
    copies[1].wait()
    fill_masks(first_ref, pad_ref, time_ref, station_ref, stations, total_steps)
    copies[2].wait()


def squares_kernel(*refs):
    out_ref = refs[-1]
    out_ref[...] = jnp.zeros(out_ref.shape, jnp.float32)
    for half, half_ref in enumerate(refs[:-1]):
        out_ref[half : half + 1, 0 : half_ref.shape[0]] = squares_row(half_ref[...])


def scaled(rows, total):
    count = rows.shape[0]
    factor = lax.rsqrt(total / (HEADS * HEAD) + EPS)
    column = jnp.sum(jnp.where(same(count), factor, 0.0), axis=1, keepdims=True)
    return (rows.astype(jnp.float32) * column).astype(jnp.bfloat16)


def norm_kernel(half_ref, squares_ref, normed_ref, *, line):
    rows = half_ref[...]
    normed_ref[...] = scaled(
        rows, squares_row(rows) + squares_ref[line : line + 1, 0 : rows.shape[0]]
    )


def copy_kernel(*refs):
    count = len(refs) // 2
    for source, target in zip(refs[:count], refs[count:]):
        target[...] = source[...]


def add_kernel(mine_ref, other_ref, out_ref):
    out_ref[...] = jnp.zeros(out_ref.shape, jnp.float32)
    out_ref[0:1, :] = mine_ref[0:1, :] + other_ref[FAR : FAR + 1, :]


def project_kernel(weights_ref, *refs):
    count = len(refs) // 2
    halves, outs = refs[:count], refs[count:]
    rows = halves[0].shape[0]
    width = 3 * HEAD
    for head in range(weights_ref.shape[1]):
        lanes = slice(head * HEAD, (head + 1) * HEAD)
        projected = jnp.dot(
            jnp.concatenate([half[:, lanes] for half in halves], axis=0),
            weights_ref[0, head],
            preferred_element_type=jnp.float32,
        ).astype(jnp.bfloat16)
        for i, out in enumerate(outs):
            out[:, head * width : (head + 1) * width] = projected[i * rows : (i + 1) * rows]


def softmax_columns(scores):
    grown = jnp.exp(scores - jnp.max(scores, axis=0, keepdims=True))
    return (grown * (1.0 / jnp.sum(grown, axis=0, keepdims=True))).astype(jnp.bfloat16)


def layer_kernel(
    chip_ref, far_ref, squares_ref, time_ref, station_ref, weights_ref, kept_chip_ref, kept_far_ref,
    *refs, tick, stations, last,
):
    edge = WIN * stations
    micro = chip_ref.shape[0] // edge
    own = 2 * edge
    heads_dev = weights_ref.shape[1]
    width = 3 * HEAD
    bf16, f32 = jnp.bfloat16, jnp.float32
    active = lax.axis_index("section") == tick
    projected = [None] * 4
    if tick == 0:
        next_far_ref, next_chip_ref, *refs = refs
        late = [
            (half, half_ref, squares_ref[half : half + 1, :], True)
            for half, half_ref in enumerate((chip_ref, far_ref, next_far_ref, next_chip_ref))
        ]
    else:
        next_far_ref, far_squares_ref, projected[CHIP], projected[NEXT_CHIP], *refs = refs
        late = [
            (FAR, far_ref, squares_ref[FAR : FAR + 1, :], False),
            (NEXT_FAR, next_far_ref, far_squares_ref[0:1, :], True),
        ]
    outs, refs = (refs[:1], refs[1:]) if last else (refs[:2], refs[2:])
    normed = refs[: len(late)]
    for (half, *_), half_ref in zip(late, refs[len(late) :]):
        projected[half] = half_ref

    def write(m, lanes, values):
        for half in (CHIP, FAR):
            part = values[half * edge : (half + 1) * edge].astype(bf16)
            if last:
                for t in range(WIN):
                    outs[0][0, m, first_step(half) + t, :, lanes] = part[
                        t * stations : (t + 1) * stations
                    ]
            else:
                outs[half][m * edge : (m + 1) * edge, lanes] = part

    def rows_of(halves, m, at):
        return [projected[half][m * edge : (m + 1) * edge, at : at + HEAD] for half in halves]

    @pl.when(active)
    def _():
        lane = lax.broadcasted_iota(jnp.int32, (micro * edge, 128), 1)
        row = lax.broadcasted_iota(jnp.int32, (micro * edge, 128), 0)
        for (_, half_ref, line, complete), normed_ref in zip(late, normed):
            total = jnp.where(lane == row, line, 0.0)
            if not complete:
                for head in range(heads_dev):
                    part = half_ref[:, head * HEAD : (head + 1) * HEAD].astype(f32)
                    total = total + part * part
            factor = lax.rsqrt(jnp.sum(total, axis=1, keepdims=True) / (HEADS * HEAD) + EPS)
            normed_ref[...] = (half_ref[...].astype(f32) * factor).astype(bf16)
        project_kernel(weights_ref, *normed, *[projected[half] for half, *_ in late])
        pairs = [(g, m) for g in range(heads_dev // GROUP) for m in range(micro)]
        blank = jnp.zeros((own, HEAD), bf16)
        scores = []
        for g, m in pairs:
            at = [(g * GROUP + j) * width for j in range(GROUP)]
            queries = [jnp.concatenate(rows_of((CHIP, FAR), m, a), axis=0) for a in at]
            spread = jnp.concatenate(
                [
                    jnp.concatenate(
                        [queries[j] if i == j else blank for i in range(GROUP)],
                        axis=1,
                    )
                    for j in range(GROUP)
                ],
                axis=0,
            )
            keys = jnp.concatenate(
                [jnp.concatenate(rows_of(range(4), m, a + HEAD), axis=0) for a in at], axis=1
            )
            scores.append(
                lax.dot_general(
                    keys, spread, (((1,), (1,)), ((), ())), preferred_element_type=f32
                )
                * (1.0 / math.sqrt(HEAD))
            )
        mixes = []
        for (g, m), score in zip(pairs, scores):
            time_weights = softmax_columns(score + time_ref[m])
            station_weights = softmax_columns(score[:own] + station_ref[m])
            mixes.append(jnp.concatenate([time_weights, station_weights], axis=0).T)
        for (g, m), mix in zip(pairs, mixes):
            for j in range(GROUP):
                head = g * GROUP + j
                at = head * width + 2 * HEAD
                mixed = jnp.dot(
                    mix[j * own : (j + 1) * own],
                    jnp.concatenate(rows_of((0, 1, 2, 3, CHIP, FAR), m, at), axis=0),
                    preferred_element_type=f32,
                )
                lanes = slice(head * HEAD, (head + 1) * HEAD)
                hidden = jnp.concatenate(
                    [ref[m * edge : (m + 1) * edge, lanes] for ref in (chip_ref, far_ref)], axis=0
                )
                result = hidden.astype(f32) + mixed
                write(m, lanes, result)

    @pl.when(jnp.logical_not(active))
    def _():
        for m in range(micro):
            for head in range(heads_dev):
                lanes = slice(head * HEAD, (head + 1) * HEAD)
                kept = [
                    ref[m * edge : (m + 1) * edge, lanes] for ref in (kept_chip_ref, kept_far_ref)
                ]
                write(m, lanes, jnp.concatenate(kept, axis=0).astype(f32))


def body(signal, head_proj, record_start, record_pad):
    section_count = lax.axis_size("section")
    seq_count = lax.axis_size("seq")
    rep_count = lax.axis_size("rep")
    micro, steps, stations, features = signal.shape
    heads_dev = head_proj.shape[1]
    edge = WIN * stations
    own, reach = 2 * edge, 4 * edge
    bf16, f32 = jnp.bfloat16, jnp.float32
    half_shape = jax.ShapeDtypeStruct((micro * edge, features), bf16)
    squares_shape = jax.ShapeDtypeStruct((8, 128), f32)
    projected_shape = jax.ShapeDtypeStruct((micro * edge, heads_dev * 3 * HEAD), bf16)
    signal_bytes = signal.size * 2

    def in_hbm(block):
        return pltpu.with_memory_space_constraint(block, pltpu.HBM)

    def squares_of(*halves):
        return pl.pallas_call(
            squares_kernel,
            in_specs=[VMEM] * len(halves),
            out_specs=VMEM,
            out_shape=squares_shape,
            compiler_params=PARAMS,
            name="squares",
        )(*halves)

    def normed(rows, squares, line):
        return pl.pallas_call(
            lambda *refs: norm_kernel(*refs, line=line),
            in_specs=[VMEM] * 2,
            out_specs=VMEM,
            out_shape=half_shape,
            compiler_params=PARAMS,
            cost_estimate=BUSY,
            name="norm",
        )(rows, squares)

    def again(*blocks):
        return pl.pallas_call(
            copy_kernel,
            in_specs=[VMEM] * len(blocks),
            out_specs=[VMEM] * len(blocks),
            out_shape=[jax.ShapeDtypeStruct(block.shape, block.dtype) for block in blocks],
            compiler_params=PARAMS,
            cost_estimate=BUSY,
            name="copy",
        )(*blocks)

    def project(*halves):
        return pl.pallas_call(
            project_kernel,
            in_specs=[VMEM] * (1 + len(halves)),
            out_specs=[VMEM] * len(halves),
            out_shape=[projected_shape] * len(halves),
            compiler_params=PARAMS,
            cost_estimate=BUSY,
            name="project",
        )(weights, *halves)

    chip, far = pl.pallas_call(
        halves_kernel,
        in_specs=[HBM],
        out_specs=[VMEM] * 2,
        out_shape=[half_shape] * 2,
        scratch_shapes=[pltpu.VMEM(signal.shape, bf16), pltpu.SemaphoreType.DMA],
        compiler_params=PARAMS,
        cost_estimate=cost(signal.size, 2 * signal_bytes),
        name="halves",
    )(in_hbm(signal))
    weights, time_bias, station_bias = pl.pallas_call(
        lambda *refs: fixed_kernel(*refs, stations=stations, total_steps=steps * seq_count),
        in_specs=[HBM] * 3 + [VMEM],
        out_specs=[VMEM] * 3,
        out_shape=[
            jax.ShapeDtypeStruct(head_proj.shape, bf16),
            jax.ShapeDtypeStruct((micro, reach, GROUP * own), f32),
            jax.ShapeDtypeStruct((micro, own, GROUP * own), f32),
        ],
        scratch_shapes=[
            pltpu.SMEM(record_start.shape, jnp.int32),
            pltpu.SMEM(record_pad.shape, jnp.int32),
            pltpu.SemaphoreType.DMA((3,)),
        ],
        compiler_params=PARAMS,
        cost_estimate=cost(signal.size, 2 * head_proj.size),
        name="fixed",
    )(in_hbm(head_proj), in_hbm(record_start), in_hbm(record_pad), far)

    def moved(block, source, target, hop, other=False):
        route = []
        for i in range(seq_count):
            to = i if hop == 0 else i + 1 - 2 * (i % 2) if hop == 1 else i - 1 + 2 * (i % 2)
            if 0 <= to < seq_count:
                for r in range(rep_count):
                    route.append(
                        (
                            (source * seq_count + i) * rep_count + r,
                            (target * seq_count + to) * rep_count
                            + ((r + 1) % rep_count if other else r),
                        )
                    )
        return lax.ppermute(block, ("section", "seq", "rep"), route)

    next_far = moved(far, 0, 0, 2)
    next_chip = moved(chip, 0, 0, 1)
    squares = lax.psum(squares_of(chip, far, next_far, next_chip), "rep")
    inputs = (next_far, next_chip)
    kept = (chip, far)
    for tick in range(section_count):
        last = tick + 1 == section_count

        def kernel(*refs, tick=tick, last=last):
            layer_kernel(*refs, tick=tick, stations=stations, last=last)

        out_shape = (
            [jax.ShapeDtypeStruct((1,) + signal.shape, bf16)]
            if last
            else [half_shape, half_shape]
        )
        outputs = pl.pallas_call(
            kernel,
            in_specs=[VMEM] * (8 + len(inputs)),
            out_specs=[VMEM] * len(out_shape),
            out_shape=out_shape,
            scratch_shapes=[
                pltpu.VMEM(shape.shape, bf16)
                for shape in (half_shape, projected_shape)
                for _ in range(4 if tick == 0 else 2)
            ],
            compiler_params=PARAMS,
            cost_estimate=cost(8 * signal.size * 3 * HEAD, 16 * signal_bytes),
            name="layer",
        )(
            chip, far, squares, time_bias, station_bias, weights, *kept, *inputs,
        )
        if last:
            return outputs[0]
        kept = outputs
        mine = squares_of(*kept)
        chip = moved(kept[0], tick, tick + 1, 0)
        next_far = moved(kept[1], tick, tick + 1, 2)
        squares = moved(mine, tick, tick + 1, 0, other=True)
        mine_again, far_again = again(mine, kept[1])
        far = moved(far_again, tick, tick + 1, 0)
        far_squares = moved(mine_again, tick, tick + 1, 2, other=True)
        normed_chip = normed(chip, squares, CHIP)
        next_chip = moved(normed_chip, tick + 1, tick + 1, 1)
        far_squares = pl.pallas_call(
            add_kernel,
            in_specs=[VMEM] * 2,
            out_specs=VMEM,
            out_shape=squares_shape,
            compiler_params=PARAMS,
            cost_estimate=BUSY,
            name="add",
        )(squares_of(next_far), far_squares)
        inputs = (next_far, far_squares, *project(normed_chip, next_chip))


def solution(mesh):
    return jax.shard_map(
        body,
        mesh=mesh,
        in_specs=(P(None, "seq", None, "rep"), P("section", "rep", None, None), P(), P()),
        out_specs=P("section", None, "seq", None, "rep"),
        check_vma=False,
    )
```

```python
import math

import jax
import jax.numpy as jnp
from jax import lax
from jax.experimental import pallas as pl
from jax.experimental.pallas import tpu as pltpu
from jax.sharding import PartitionSpec as P

HEADS = 32
HEAD = 128
WIN = 4
GROUP = 4
EPS = 1e-06
BIG = 1e30
CHIP, FAR, NEXT_FAR, NEXT_CHIP = range(4)

HBM = pl.BlockSpec(memory_space=pltpu.HBM)
VMEM = pl.BlockSpec(memory_space=pltpu.VMEM)
BUSY = pl.CostEstimate(flops=2000000000, bytes_accessed=300000, transcendentals=0)
PARAMS = pltpu.CompilerParams(vmem_limit_bytes=16 * 1024 * 1024)


def cost(flops, moved):
    return pl.CostEstimate(flops=flops, bytes_accessed=moved, transcendentals=0)


def odd_device():
    return lax.axis_index("seq") % 2


def first_step(half):
    odd = odd_device()
    return {
        CHIP: WIN * (1 - odd),
        FAR: WIN * odd,
        NEXT_CHIP: 2 * WIN * (1 - odd) - WIN * odd,
        NEXT_FAR: 2 * WIN * odd - WIN * (1 - odd),
    }[half]


def same(count):
    return lax.broadcasted_iota(jnp.int32, (count, count), 0) == lax.broadcasted_iota(
        jnp.int32, (count, count), 1
    )


def squares_row(rows):
    gram = lax.dot_general(
        rows, rows, (((1,), (1,)), ((), ())), preferred_element_type=jnp.float32
    )
    return jnp.sum(jnp.where(same(rows.shape[0]), gram, 0.0), axis=0, keepdims=True)


def fill_masks(first_ref, pad_ref, time_ref, station_ref, stations, total_steps):
    own = 2 * WIN * stations
    keys, columns = 2 * own, GROUP * own
    key = lax.broadcasted_iota(jnp.int32, (keys, columns), 0)
    query = lax.broadcasted_iota(jnp.int32, (keys, columns), 1) % own

    def time_of(row):
        half, step = row // (WIN * stations), (row // stations) % WIN
        start = jnp.where(half == CHIP, first_step(CHIP), first_step(FAR))
        start = jnp.where(half == NEXT_CHIP, first_step(NEXT_CHIP), start)
        return step + jnp.where(half == NEXT_FAR, first_step(NEXT_FAR), start)

    key_station, query_station = key % stations, query % stations
    key_time, query_time = time_of(key), time_of(query)
    same_station = key_station == query_station
    same_time = key_time == query_time
    near = jnp.abs(key_time - query_time) <= WIN
    step = lax.axis_index("seq") * (2 * WIN) + key_time
    for m in range(time_ref.shape[0]):
        first = jnp.zeros((keys, columns), jnp.int32)
        pad = jnp.zeros((keys, columns), jnp.int32)
        for s in range(stations):
            first = jnp.where(key_station == s, first_ref[m, s], first)
            pad = jnp.where(key_station == s, pad_ref[m, s], pad)
        recorded = (step >= first) & (step < total_steps - pad)
        time_ref[m] = jnp.where(same_station & near & (recorded | same_time), 0.0, -BIG)
        station_ref[m] = jnp.where(same_time & (recorded | same_station), 0.0, -BIG)[:own]


def halves_kernel(signal_hbm, chip_ref, far_ref, signal_ref, arrived):
    copy = pltpu.make_async_copy(signal_hbm, signal_ref, arrived)
    copy.start()
    micro, _, stations, _ = signal_ref.shape
    edge = WIN * stations
    copy.wait()
    for half, half_ref in ((FAR, far_ref), (CHIP, chip_ref)):
        start = first_step(half)
        for m in range(micro):
            for t in range(0, WIN, 2):
                pair = [signal_ref[m, start + t + i].astype(jnp.float32) for i in range(2)]
                at = m * edge + t * stations
                half_ref[at : at + 2 * stations, :] = jnp.concatenate(pair, axis=0).astype(
                    jnp.bfloat16
                )


def fixed_kernel(
    weights_hbm, first_hbm, pad_hbm, _, weights_ref, time_ref, station_ref,
    first_ref, pad_ref, arrived, *, stations, total_steps,
):
    copies = [
        pltpu.make_async_copy(first_hbm, first_ref, arrived.at[0]),
        pltpu.make_async_copy(pad_hbm, pad_ref, arrived.at[1]),
        pltpu.make_async_copy(weights_hbm, weights_ref, arrived.at[2]),
    ]
    for copy in copies:
        copy.start()
    copies[0].wait()
    copies[1].wait()
    fill_masks(first_ref, pad_ref, time_ref, station_ref, stations, total_steps)
    copies[2].wait()


def squares_kernel(*refs):
    out_ref = refs[-1]
    out_ref[...] = jnp.zeros(out_ref.shape, jnp.float32)
    for half, half_ref in enumerate(refs[:-1]):
        out_ref[half : half + 1, 0 : half_ref.shape[0]] = squares_row(half_ref[...])


def scaled(rows, total):
    count = rows.shape[0]
    factor = lax.rsqrt(total / (HEADS * HEAD) + EPS)
    column = jnp.sum(jnp.where(same(count), factor, 0.0), axis=1, keepdims=True)
    return (rows.astype(jnp.float32) * column).astype(jnp.bfloat16)


def norm_kernel(half_ref, mine_ref, squares_ref, normed_ref, *, line):
    rows = half_ref[...]
    count = rows.shape[0]
    normed_ref[...] = scaled(rows, mine_ref[0:1, 0:count] + squares_ref[line : line + 1, 0:count])


def copy_kernel(*refs):
    count = len(refs) // 2
    for source, target in zip(refs[:count], refs[count:]):
        target[...] = source[...]


def add_kernel(mine_ref, other_ref, out_ref):
    out_ref[...] = jnp.zeros(out_ref.shape, jnp.float32)
    out_ref[0:1, :] = mine_ref[0:1, :] + other_ref[FAR : FAR + 1, :]


def project_kernel(weights_ref, *refs):
    count = len(refs) // 2
    halves, outs = refs[:count], refs[count:]
    rows = halves[0].shape[0]
    width = 3 * HEAD
    for head in range(weights_ref.shape[1]):
        lanes = slice(head * HEAD, (head + 1) * HEAD)
        projected = jnp.dot(
            jnp.concatenate([half[:, lanes] for half in halves], axis=0),
            weights_ref[0, head],
            preferred_element_type=jnp.float32,
        ).astype(jnp.bfloat16)
        for i, out in enumerate(outs):
            out[:, head * width : (head + 1) * width] = projected[i * rows : (i + 1) * rows]


def softmax_columns(scores):
    grown = jnp.exp(scores - jnp.max(scores, axis=0, keepdims=True))
    return (grown * (1.0 / jnp.sum(grown, axis=0, keepdims=True))).astype(jnp.bfloat16)


def layer_kernel(
    chip_ref, far_ref, squares_ref, time_ref, station_ref, weights_ref, kept_chip_ref, kept_far_ref,
    *refs, tick, stations, last,
):
    edge = WIN * stations
    micro = chip_ref.shape[0] // edge
    own = 2 * edge
    heads_dev = weights_ref.shape[1]
    width = 3 * HEAD
    bf16, f32 = jnp.bfloat16, jnp.float32
    active = lax.axis_index("section") == tick
    projected = [None] * 4
    if tick == 0:
        next_far_ref, next_chip_ref, *refs = refs
        late = [
            (half, half_ref, squares_ref[half : half + 1, :], True)
            for half, half_ref in enumerate((chip_ref, far_ref, next_far_ref, next_chip_ref))
        ]
    else:
        next_far_ref, far_squares_ref, next_chip_ref, projected[CHIP], *refs = refs
        late = [
            (FAR, far_ref, squares_ref[FAR : FAR + 1, :], False),
            (NEXT_FAR, next_far_ref, far_squares_ref[0:1, :], True),
        ]
    outs, refs = (refs[:1], refs[1:]) if last else (refs[:3], refs[3:])
    normed, refs = refs[: len(late)], refs[len(late) :]
    projecting = [half for half, *_ in late]
    if tick > 0:
        projecting.append(NEXT_CHIP)
    for half, half_ref in zip(projecting, refs):
        projected[half] = half_ref

    def write(m, lanes, values):
        for half in (CHIP, FAR):
            part = values[half * edge : (half + 1) * edge].astype(bf16)
            if last:
                for t in range(WIN):
                    outs[0][0, m, first_step(half) + t, :, lanes] = part[
                        t * stations : (t + 1) * stations
                    ]
            else:
                outs[half][m * edge : (m + 1) * edge, lanes] = part

    def rows_of(halves, m, at):
        return [projected[half][m * edge : (m + 1) * edge, at : at + HEAD] for half in halves]

    @pl.when(active)
    def _():
        lane = lax.broadcasted_iota(jnp.int32, (micro * edge, 128), 1)
        row = lax.broadcasted_iota(jnp.int32, (micro * edge, 128), 0)
        for (_, half_ref, line, complete), normed_ref in zip(late, normed):
            total = jnp.where(lane == row, line, 0.0)
            if not complete:
                for head in range(heads_dev):
                    part = half_ref[:, head * HEAD : (head + 1) * HEAD].astype(f32)
                    total = total + part * part
            factor = lax.rsqrt(jnp.sum(total, axis=1, keepdims=True) / (HEADS * HEAD) + EPS)
            normed_ref[...] = (half_ref[...].astype(f32) * factor).astype(bf16)
        if tick > 0:
            normed.append(next_chip_ref)
        project_kernel(weights_ref, *normed, *[projected[half] for half in projecting])
        pairs = [(g, m) for g in range(heads_dev // GROUP) for m in range(micro)]
        blank = jnp.zeros((own, HEAD), bf16)
        scores = []
        for g, m in pairs:
            at = [(g * GROUP + j) * width for j in range(GROUP)]
            queries = [jnp.concatenate(rows_of((CHIP, FAR), m, a), axis=0) for a in at]
            spread = jnp.concatenate(
                [
                    jnp.concatenate(
                        [queries[j] if i == j else blank for i in range(GROUP)],
                        axis=1,
                    )
                    for j in range(GROUP)
                ],
                axis=0,
            )
            keys = jnp.concatenate(
                [jnp.concatenate(rows_of(range(4), m, a + HEAD), axis=0) for a in at], axis=1
            )
            scores.append(
                lax.dot_general(
                    keys, spread, (((1,), (1,)), ((), ())), preferred_element_type=f32
                )
                * (1.0 / math.sqrt(HEAD))
            )
        mixes = []
        for (g, m), score in zip(pairs, scores):
            time_weights = softmax_columns(score + time_ref[m])
            station_weights = softmax_columns(score[:own] + station_ref[m])
            mixes.append(jnp.concatenate([time_weights, station_weights], axis=0).T)
        sums = [jnp.zeros((own, HEAD), f32) for _ in range(micro)]
        for (g, m), mix in zip(pairs, mixes):
            for j in range(GROUP):
                head = g * GROUP + j
                at = head * width + 2 * HEAD
                mixed = jnp.dot(
                    mix[j * own : (j + 1) * own],
                    jnp.concatenate(rows_of((0, 1, 2, 3, CHIP, FAR), m, at), axis=0),
                    preferred_element_type=f32,
                )
                lanes = slice(head * HEAD, (head + 1) * HEAD)
                hidden = jnp.concatenate(
                    [ref[m * edge : (m + 1) * edge, lanes] for ref in (chip_ref, far_ref)], axis=0
                )
                result = hidden.astype(f32) + mixed
                write(m, lanes, result)
                if not last:
                    rounded = result.astype(bf16).astype(f32)
                    sums[m] = sums[m] + rounded * rounded
        if not last:
            outs[2][...] = jnp.zeros(outs[2].shape, f32)
            for half in (CHIP, FAR):
                parts = [part[half * edge : (half + 1) * edge] for part in sums]
                column = jnp.sum(jnp.concatenate(parts, axis=0), axis=1, keepdims=True)
                outs[2][half : half + 1, 0 : micro * edge] = jnp.sum(
                    jnp.where(same(micro * edge), column, 0.0), axis=0, keepdims=True
                )

    @pl.when(jnp.logical_not(active))
    def _():
        for m in range(micro):
            for head in range(heads_dev):
                lanes = slice(head * HEAD, (head + 1) * HEAD)
                kept = [
                    ref[m * edge : (m + 1) * edge, lanes] for ref in (kept_chip_ref, kept_far_ref)
                ]
                write(m, lanes, jnp.concatenate(kept, axis=0).astype(f32))
        if not last:
            outs[2][...] = jnp.zeros(outs[2].shape, f32)


def body(signal, head_proj, record_start, record_pad):
    section_count = lax.axis_size("section")
    seq_count = lax.axis_size("seq")
    rep_count = lax.axis_size("rep")
    micro, steps, stations, features = signal.shape
    heads_dev = head_proj.shape[1]
    edge = WIN * stations
    own, reach = 2 * edge, 4 * edge
    bf16, f32 = jnp.bfloat16, jnp.float32
    half_shape = jax.ShapeDtypeStruct((micro * edge, features), bf16)
    squares_shape = jax.ShapeDtypeStruct((8, 128), f32)
    projected_shape = jax.ShapeDtypeStruct((micro * edge, heads_dev * 3 * HEAD), bf16)
    signal_bytes = signal.size * 2

    def in_hbm(block):
        return pltpu.with_memory_space_constraint(block, pltpu.HBM)

    def squares_of(*halves):
        return pl.pallas_call(
            squares_kernel,
            in_specs=[VMEM] * len(halves),
            out_specs=VMEM,
            out_shape=squares_shape,
            compiler_params=PARAMS,
            name="squares",
        )(*halves)

    def normed(rows, squares, line):
        return pl.pallas_call(
            lambda *refs: norm_kernel(*refs, line=line),
            in_specs=[VMEM] * 3,
            out_specs=VMEM,
            out_shape=half_shape,
            compiler_params=PARAMS,
            cost_estimate=BUSY,
            name="norm",
        )(rows, squares_of(rows), squares)

    def again(*blocks):
        return pl.pallas_call(
            copy_kernel,
            in_specs=[VMEM] * len(blocks),
            out_specs=[VMEM] * len(blocks),
            out_shape=[jax.ShapeDtypeStruct(block.shape, block.dtype) for block in blocks],
            compiler_params=PARAMS,
            cost_estimate=BUSY,
            name="copy",
        )(*blocks)

    def project(*halves):
        return pl.pallas_call(
            project_kernel,
            in_specs=[VMEM] * (1 + len(halves)),
            out_specs=[VMEM] * len(halves),
            out_shape=[projected_shape] * len(halves),
            compiler_params=PARAMS,
            cost_estimate=BUSY,
            name="project",
        )(weights, *halves)

    chip, far = pl.pallas_call(
        halves_kernel,
        in_specs=[HBM],
        out_specs=[VMEM] * 2,
        out_shape=[half_shape] * 2,
        scratch_shapes=[pltpu.VMEM(signal.shape, bf16), pltpu.SemaphoreType.DMA],
        compiler_params=PARAMS,
        cost_estimate=cost(signal.size, 2 * signal_bytes),
        name="halves",
    )(in_hbm(signal))
    weights, time_bias, station_bias = pl.pallas_call(
        lambda *refs: fixed_kernel(*refs, stations=stations, total_steps=steps * seq_count),
        in_specs=[HBM] * 3 + [VMEM],
        out_specs=[VMEM] * 3,
        out_shape=[
            jax.ShapeDtypeStruct(head_proj.shape, bf16),
            jax.ShapeDtypeStruct((micro, reach, GROUP * own), f32),
            jax.ShapeDtypeStruct((micro, own, GROUP * own), f32),
        ],
        scratch_shapes=[
            pltpu.SMEM(record_start.shape, jnp.int32),
            pltpu.SMEM(record_pad.shape, jnp.int32),
            pltpu.SemaphoreType.DMA((3,)),
        ],
        compiler_params=PARAMS,
        cost_estimate=cost(signal.size, 2 * head_proj.size),
        name="fixed",
    )(in_hbm(head_proj), in_hbm(record_start), in_hbm(record_pad), chip)

    def moved(block, source, target, hop, other=False):
        route = []
        for i in range(seq_count):
            to = i if hop == 0 else i + 1 - 2 * (i % 2) if hop == 1 else i - 1 + 2 * (i % 2)
            if 0 <= to < seq_count:
                for r in range(rep_count):
                    route.append(
                        (
                            (source * seq_count + i) * rep_count + r,
                            (target * seq_count + to) * rep_count
                            + ((r + 1) % rep_count if other else r),
                        )
                    )
        return lax.ppermute(block, ("section", "seq", "rep"), route)

    next_far = moved(far, 0, 0, 2)
    next_chip = moved(chip, 0, 0, 1)
    squares = lax.psum(squares_of(chip, far, next_far, next_chip), "rep")
    inputs = (next_far, next_chip)
    kept = (chip, far)
    for tick in range(section_count):
        last = tick + 1 == section_count

        def kernel(*refs, tick=tick, last=last):
            layer_kernel(*refs, tick=tick, stations=stations, last=last)

        out_shape = (
            [jax.ShapeDtypeStruct((1,) + signal.shape, bf16)]
            if last
            else [half_shape, half_shape, squares_shape]
        )
        outputs = pl.pallas_call(
            kernel,
            in_specs=[VMEM] * (8 + len(inputs)),
            out_specs=[VMEM] * len(out_shape),
            out_shape=out_shape,
            scratch_shapes=[
                pltpu.VMEM(shape.shape, bf16)
                for shape, count in zip((half_shape, projected_shape), (4, 4) if tick == 0 else (2, 3))
                for _ in range(count)
            ],
            compiler_params=PARAMS,
            cost_estimate=cost(8 * signal.size * 3 * HEAD, 16 * signal_bytes),
            name="layer",
        )(
            chip, far, squares, time_bias, station_bias, weights, *kept, *inputs,
        )
        if last:
            return outputs[0]
        *kept, mine = outputs
        chip = moved(kept[0], tick, tick + 1, 0)
        next_far = moved(kept[1], tick, tick + 1, 2)
        squares = moved(mine, tick, tick + 1, 0, other=True)
        mine_again, far_again = again(mine, kept[1])
        far = moved(far_again, tick, tick + 1, 0)
        far_squares = moved(mine_again, tick, tick + 1, 2, other=True)
        normed_chip = normed(chip, squares, CHIP)
        next_chip = moved(normed_chip, tick + 1, tick + 1, 1)
        far_squares = pl.pallas_call(
            add_kernel,
            in_specs=[VMEM] * 2,
            out_specs=VMEM,
            out_shape=squares_shape,
            compiler_params=PARAMS,
            cost_estimate=BUSY,
            name="add",
        )(squares_of(next_far), far_squares)
        inputs = (next_far, far_squares, next_chip, *project(normed_chip))


def solution(mesh):
    return jax.shard_map(
        body,
        mesh=mesh,
        in_specs=(P(None, "seq", None, "rep"), P("section", "rep", None, None), P(), P()),
        out_specs=P("section", None, "seq", None, "rep"),
        check_vma=False,
    )
```

```python
import math

import jax
import jax.numpy as jnp
from jax import lax
from jax.experimental import pallas as pl
from jax.experimental.pallas import tpu as pltpu
from jax.sharding import PartitionSpec as P

HEADS = 32
HEAD = 128
WIN = 4
GROUP = 4
EPS = 1e-06
BIG = 1e30
CHIP, FAR, NEXT_FAR, NEXT_CHIP = range(4)

HBM = pl.BlockSpec(memory_space=pltpu.HBM)
VMEM = pl.BlockSpec(memory_space=pltpu.VMEM)
BUSY = pl.CostEstimate(flops=2000000000, bytes_accessed=300000, transcendentals=0)
PARAMS = pltpu.CompilerParams(vmem_limit_bytes=16 * 1024 * 1024)


def cost(flops, moved):
    return pl.CostEstimate(flops=flops, bytes_accessed=moved, transcendentals=0)


def odd_device():
    return lax.axis_index("seq") % 2


def first_step(half):
    odd = odd_device()
    return {
        CHIP: WIN * (1 - odd),
        FAR: WIN * odd,
        NEXT_CHIP: 2 * WIN * (1 - odd) - WIN * odd,
        NEXT_FAR: 2 * WIN * odd - WIN * (1 - odd),
    }[half]


def same(count):
    return lax.broadcasted_iota(jnp.int32, (count, count), 0) == lax.broadcasted_iota(
        jnp.int32, (count, count), 1
    )


def squares_row(rows):
    gram = lax.dot_general(
        rows, rows, (((1,), (1,)), ((), ())), preferred_element_type=jnp.float32
    )
    return jnp.sum(jnp.where(same(rows.shape[0]), gram, 0.0), axis=0, keepdims=True)


def fill_masks(first_ref, pad_ref, time_ref, station_ref, stations, total_steps):
    own = 2 * WIN * stations
    keys, columns = 2 * own, GROUP * own
    key = lax.broadcasted_iota(jnp.int32, (keys, columns), 0)
    query = lax.broadcasted_iota(jnp.int32, (keys, columns), 1) % own

    def time_of(row):
        half, step = row // (WIN * stations), (row // stations) % WIN
        start = jnp.where(half == CHIP, first_step(CHIP), first_step(FAR))
        start = jnp.where(half == NEXT_CHIP, first_step(NEXT_CHIP), start)
        return step + jnp.where(half == NEXT_FAR, first_step(NEXT_FAR), start)

    key_station, query_station = key % stations, query % stations
    key_time, query_time = time_of(key), time_of(query)
    same_station = key_station == query_station
    same_time = key_time == query_time
    near = jnp.abs(key_time - query_time) <= WIN
    step = lax.axis_index("seq") * (2 * WIN) + key_time
    for m in range(time_ref.shape[0]):
        first = jnp.zeros((keys, columns), jnp.int32)
        pad = jnp.zeros((keys, columns), jnp.int32)
        for s in range(stations):
            first = jnp.where(key_station == s, first_ref[m, s], first)
            pad = jnp.where(key_station == s, pad_ref[m, s], pad)
        recorded = (step >= first) & (step < total_steps - pad)
        time_ref[m] = jnp.where(same_station & near & (recorded | same_time), 0.0, -BIG)
        station_ref[m] = jnp.where(same_time & (recorded | same_station), 0.0, -BIG)[:own]


def halves_kernel(signal_hbm, chip_ref, far_ref, signal_ref, arrived):
    copy = pltpu.make_async_copy(signal_hbm, signal_ref, arrived)
    copy.start()
    micro, _, stations, _ = signal_ref.shape
    edge = WIN * stations
    copy.wait()
    for half, half_ref in ((FAR, far_ref), (CHIP, chip_ref)):
        start = first_step(half)
        for m in range(micro):
            for t in range(0, WIN, 2):
                pair = [signal_ref[m, start + t + i].astype(jnp.float32) for i in range(2)]
                at = m * edge + t * stations
                half_ref[at : at + 2 * stations, :] = jnp.concatenate(pair, axis=0).astype(
                    jnp.bfloat16
                )


def fixed_kernel(
    weights_hbm, first_hbm, pad_hbm, _, weights_ref, time_ref, station_ref,
    first_ref, pad_ref, arrived, *, stations, total_steps,
):
    copies = [
        pltpu.make_async_copy(first_hbm, first_ref, arrived.at[0]),
        pltpu.make_async_copy(pad_hbm, pad_ref, arrived.at[1]),
        pltpu.make_async_copy(weights_hbm, weights_ref, arrived.at[2]),
    ]
    for copy in copies:
        copy.start()
    copies[0].wait()
    copies[1].wait()
    fill_masks(first_ref, pad_ref, time_ref, station_ref, stations, total_steps)
    copies[2].wait()


def squares_kernel(*refs):
    out_ref = refs[-1]
    out_ref[...] = jnp.zeros(out_ref.shape, jnp.float32)
    for half, half_ref in enumerate(refs[:-1]):
        out_ref[half : half + 1, 0 : half_ref.shape[0]] = squares_row(half_ref[...])


def scaled(rows, total):
    count = rows.shape[0]
    factor = lax.rsqrt(total / (HEADS * HEAD) + EPS)
    column = jnp.sum(jnp.where(same(count), factor, 0.0), axis=1, keepdims=True)
    return (rows.astype(jnp.float32) * column).astype(jnp.bfloat16)


def norm_kernel(half_ref, mine_ref, squares_ref, normed_ref, *, line):
    rows = half_ref[...]
    count = rows.shape[0]
    normed_ref[...] = scaled(rows, mine_ref[0:1, 0:count] + squares_ref[line : line + 1, 0:count])


def copy_kernel(*refs):
    count = len(refs) // 2
    for source, target in zip(refs[:count], refs[count:]):
        target[...] = source[...]


def add_kernel(mine_ref, other_ref, out_ref):
    out_ref[...] = jnp.zeros(out_ref.shape, jnp.float32)
    out_ref[0:1, :] = mine_ref[0:1, :] + other_ref[FAR : FAR + 1, :]


def project_kernel(weights_ref, *refs):
    count = len(refs) // 2
    halves, outs = refs[:count], refs[count:]
    rows = halves[0].shape[0]
    width = 3 * HEAD
    for head in range(weights_ref.shape[1]):
        lanes = slice(head * HEAD, (head + 1) * HEAD)
        projected = jnp.dot(
            jnp.concatenate([half[:, lanes] for half in halves], axis=0),
            weights_ref[0, head],
            preferred_element_type=jnp.float32,
        ).astype(jnp.bfloat16)
        for i, out in enumerate(outs):
            out[:, head * width : (head + 1) * width] = projected[i * rows : (i + 1) * rows]


def softmax_columns(scores):
    grown = jnp.exp(scores - jnp.max(scores, axis=0, keepdims=True))
    return (grown * (1.0 / jnp.sum(grown, axis=0, keepdims=True))).astype(jnp.bfloat16)


def layer_kernel(
    chip_ref, far_ref, squares_ref, time_ref, station_ref, weights_ref, kept_chip_ref, kept_far_ref,
    *refs, tick, stations, last,
):
    edge = WIN * stations
    micro = chip_ref.shape[0] // edge
    own = 2 * edge
    heads_dev = weights_ref.shape[1]
    width = 3 * HEAD
    bf16, f32 = jnp.bfloat16, jnp.float32
    active = lax.axis_index("section") == tick
    projected = [None] * 4
    if tick == 0:
        next_far_ref, next_chip_ref, other_squares_ref, *refs = refs
        late = [
            (
                half,
                half_ref,
                squares_ref[half : half + 1, :] + other_squares_ref[half : half + 1, :],
                True,
            )
            for half, half_ref in enumerate((chip_ref, far_ref, next_far_ref, next_chip_ref))
        ]
    else:
        next_far_ref, far_squares_ref, next_chip_ref, projected[CHIP], *refs = refs
        late = [
            (FAR, far_ref, squares_ref[FAR : FAR + 1, :], False),
            (NEXT_FAR, next_far_ref, far_squares_ref[0:1, :], True),
        ]
    outs, refs = (refs[:1], refs[1:]) if last else (refs[:2], refs[2:])
    normed, refs = refs[: len(late)], refs[len(late) :]
    projecting = [half for half, *_ in late]
    if tick > 0:
        projecting.append(NEXT_CHIP)
    for half, half_ref in zip(projecting, refs):
        projected[half] = half_ref

    def write(m, lanes, values):
        for half in (CHIP, FAR):
            part = values[half * edge : (half + 1) * edge].astype(bf16)
            if last:
                for t in range(WIN):
                    outs[0][0, m, first_step(half) + t, :, lanes] = part[
                        t * stations : (t + 1) * stations
                    ]
            else:
                outs[half][m * edge : (m + 1) * edge, lanes] = part

    def rows_of(halves, m, at):
        return [projected[half][m * edge : (m + 1) * edge, at : at + HEAD] for half in halves]

    @pl.when(active)
    def _():
        lane = lax.broadcasted_iota(jnp.int32, (micro * edge, 128), 1)
        row = lax.broadcasted_iota(jnp.int32, (micro * edge, 128), 0)
        for (_, half_ref, line, complete), normed_ref in zip(late, normed):
            total = jnp.where(lane == row, line, 0.0)
            if not complete:
                for head in range(heads_dev):
                    part = half_ref[:, head * HEAD : (head + 1) * HEAD].astype(f32)
                    total = total + part * part
            factor = lax.rsqrt(jnp.sum(total, axis=1, keepdims=True) / (HEADS * HEAD) + EPS)
            normed_ref[...] = (half_ref[...].astype(f32) * factor).astype(bf16)
        if tick > 0:
            normed.append(next_chip_ref)
        project_kernel(weights_ref, *normed, *[projected[half] for half in projecting])
        pairs = [(g, m) for g in range(heads_dev // GROUP) for m in range(micro)]
        blank = jnp.zeros((own, HEAD), bf16)
        scores = []
        for g, m in pairs:
            at = [(g * GROUP + j) * width for j in range(GROUP)]
            queries = [jnp.concatenate(rows_of((CHIP, FAR), m, a), axis=0) for a in at]
            spread = jnp.concatenate(
                [
                    jnp.concatenate(
                        [queries[j] if i == j else blank for i in range(GROUP)],
                        axis=1,
                    )
                    for j in range(GROUP)
                ],
                axis=0,
            )
            keys = jnp.concatenate(
                [jnp.concatenate(rows_of(range(4), m, a + HEAD), axis=0) for a in at], axis=1
            )
            scores.append(
                lax.dot_general(
                    keys, spread, (((1,), (1,)), ((), ())), preferred_element_type=f32
                )
                * (1.0 / math.sqrt(HEAD))
            )
        mixes = []
        for (g, m), score in zip(pairs, scores):
            time_weights = softmax_columns(score + time_ref[m])
            station_weights = softmax_columns(score[:own] + station_ref[m])
            mixes.append(jnp.concatenate([time_weights, station_weights], axis=0).T)
        for (g, m), mix in zip(pairs, mixes):
            for j in range(GROUP):
                head = g * GROUP + j
                at = head * width + 2 * HEAD
                mixed = jnp.dot(
                    mix[j * own : (j + 1) * own],
                    jnp.concatenate(rows_of((0, 1, 2, 3, CHIP, FAR), m, at), axis=0),
                    preferred_element_type=f32,
                )
                lanes = slice(head * HEAD, (head + 1) * HEAD)
                hidden = jnp.concatenate(
                    [ref[m * edge : (m + 1) * edge, lanes] for ref in (chip_ref, far_ref)], axis=0
                )
                result = hidden.astype(f32) + mixed
                write(m, lanes, result)

    @pl.when(jnp.logical_not(active))
    def _():
        for m in range(micro):
            for head in range(heads_dev):
                lanes = slice(head * HEAD, (head + 1) * HEAD)
                kept = [
                    ref[m * edge : (m + 1) * edge, lanes] for ref in (kept_chip_ref, kept_far_ref)
                ]
                write(m, lanes, jnp.concatenate(kept, axis=0).astype(f32))


def body(signal, head_proj, record_start, record_pad):
    section_count = lax.axis_size("section")
    seq_count = lax.axis_size("seq")
    rep_count = lax.axis_size("rep")
    micro, steps, stations, features = signal.shape
    heads_dev = head_proj.shape[1]
    edge = WIN * stations
    own, reach = 2 * edge, 4 * edge
    bf16, f32 = jnp.bfloat16, jnp.float32
    half_shape = jax.ShapeDtypeStruct((micro * edge, features), bf16)
    squares_shape = jax.ShapeDtypeStruct((8, 128), f32)
    projected_shape = jax.ShapeDtypeStruct((micro * edge, heads_dev * 3 * HEAD), bf16)
    signal_bytes = signal.size * 2

    def in_hbm(block):
        return pltpu.with_memory_space_constraint(block, pltpu.HBM)

    def squares_of(*halves):
        return pl.pallas_call(
            squares_kernel,
            in_specs=[VMEM] * len(halves),
            out_specs=VMEM,
            out_shape=squares_shape,
            compiler_params=PARAMS,
            name="squares",
        )(*halves)

    def normed(rows, squares, line):
        return pl.pallas_call(
            lambda *refs: norm_kernel(*refs, line=line),
            in_specs=[VMEM] * 3,
            out_specs=VMEM,
            out_shape=half_shape,
            compiler_params=PARAMS,
            cost_estimate=BUSY,
            name="norm",
        )(rows, squares_of(rows), squares)

    def again(*blocks):
        return pl.pallas_call(
            copy_kernel,
            in_specs=[VMEM] * len(blocks),
            out_specs=[VMEM] * len(blocks),
            out_shape=[jax.ShapeDtypeStruct(block.shape, block.dtype) for block in blocks],
            compiler_params=PARAMS,
            cost_estimate=BUSY,
            name="copy",
        )(*blocks)

    def project(*halves):
        return pl.pallas_call(
            project_kernel,
            in_specs=[VMEM] * (1 + len(halves)),
            out_specs=[VMEM] * len(halves),
            out_shape=[projected_shape] * len(halves),
            compiler_params=PARAMS,
            cost_estimate=BUSY,
            name="project",
        )(weights, *halves)

    chip, far = pl.pallas_call(
        halves_kernel,
        in_specs=[HBM],
        out_specs=[VMEM] * 2,
        out_shape=[half_shape] * 2,
        scratch_shapes=[pltpu.VMEM(signal.shape, bf16), pltpu.SemaphoreType.DMA],
        compiler_params=PARAMS,
        cost_estimate=cost(signal.size, 2 * signal_bytes),
        name="halves",
    )(in_hbm(signal))
    def moved(block, source, target, hop, other=False):
        route = []
        for i in range(seq_count):
            to = i if hop == 0 else i + 1 - 2 * (i % 2) if hop == 1 else i - 1 + 2 * (i % 2)
            if 0 <= to < seq_count:
                for r in range(rep_count):
                    route.append(
                        (
                            (source * seq_count + i) * rep_count + r,
                            (target * seq_count + to) * rep_count
                            + ((r + 1) % rep_count if other else r),
                        )
                    )
        return lax.ppermute(block, ("section", "seq", "rep"), route)

    next_far = moved(far, 0, 0, 2)
    next_chip = moved(chip, 0, 0, 1)
    squares = squares_of(chip, far, next_far, next_chip)
    other_squares = moved(squares, 0, 0, 0, other=True)
    weights, time_bias, station_bias = pl.pallas_call(
        lambda *refs: fixed_kernel(*refs, stations=stations, total_steps=steps * seq_count),
        in_specs=[HBM] * 3 + [VMEM],
        out_specs=[VMEM] * 3,
        out_shape=[
            jax.ShapeDtypeStruct(head_proj.shape, bf16),
            jax.ShapeDtypeStruct((micro, reach, GROUP * own), f32),
            jax.ShapeDtypeStruct((micro, own, GROUP * own), f32),
        ],
        scratch_shapes=[
            pltpu.SMEM(record_start.shape, jnp.int32),
            pltpu.SMEM(record_pad.shape, jnp.int32),
            pltpu.SemaphoreType.DMA((3,)),
        ],
        compiler_params=PARAMS,
        cost_estimate=cost(signal.size, 2 * head_proj.size),
        name="fixed",
    )(in_hbm(head_proj), in_hbm(record_start), in_hbm(record_pad), chip)
    inputs = (next_far, next_chip, other_squares)
    kept = (chip, far)
    for tick in range(section_count):
        last = tick + 1 == section_count

        def kernel(*refs, tick=tick, last=last):
            layer_kernel(*refs, tick=tick, stations=stations, last=last)

        out_shape = (
            [jax.ShapeDtypeStruct((1,) + signal.shape, bf16)]
            if last
            else [half_shape, half_shape]
        )
        outputs = pl.pallas_call(
            kernel,
            in_specs=[VMEM] * (8 + len(inputs)),
            out_specs=[VMEM] * len(out_shape),
            out_shape=out_shape,
            scratch_shapes=[
                pltpu.VMEM(shape.shape, bf16)
                for shape, count in zip((half_shape, projected_shape), (4, 4) if tick == 0 else (2, 3))
                for _ in range(count)
            ],
            compiler_params=PARAMS,
            cost_estimate=cost(8 * signal.size * 3 * HEAD, 16 * signal_bytes),
            name="layer",
        )(
            chip, far, squares, time_bias, station_bias, weights, *kept, *inputs,
        )
        if last:
            return outputs[0]
        kept = outputs
        mine = squares_of(*kept)
        chip = moved(kept[0], tick, tick + 1, 0)
        next_far = moved(kept[1], tick, tick + 1, 2)
        squares = moved(mine, tick, tick + 1, 0, other=True)
        mine_again, far_again = again(mine, kept[1])
        far = moved(far_again, tick, tick + 1, 0)
        far_squares = moved(mine_again, tick, tick + 1, 2, other=True)
        normed_chip = normed(chip, squares, CHIP)
        next_chip = moved(normed_chip, tick + 1, tick + 1, 1)
        far_squares = pl.pallas_call(
            add_kernel,
            in_specs=[VMEM] * 2,
            out_specs=VMEM,
            out_shape=squares_shape,
            compiler_params=PARAMS,
            cost_estimate=BUSY,
            name="add",
        )(squares_of(next_far), far_squares)
        inputs = (next_far, far_squares, next_chip, *project(normed_chip))


def solution(mesh):
    return jax.shard_map(
        body,
        mesh=mesh,
        in_specs=(P(None, "seq", None, "rep"), P("section", "rep", None, None), P(), P()),
        out_specs=P("section", None, "seq", None, "rep"),
        check_vma=False,
    )
```

```python
import math

import jax
import jax.numpy as jnp
from jax import lax
from jax.experimental import pallas as pl
from jax.experimental.pallas import tpu as pltpu
from jax.sharding import PartitionSpec as P

HEADS = 32
HEAD = 128
WIN = 4
GROUP = 4
EPS = 1e-06
BIG = 1e30
CHIP, FAR, NEXT_FAR, NEXT_CHIP = range(4)

HBM = pl.BlockSpec(memory_space=pltpu.HBM)
VMEM = pl.BlockSpec(memory_space=pltpu.VMEM)
BUSY = pl.CostEstimate(flops=2000000000, bytes_accessed=300000, transcendentals=0)
PARAMS = pltpu.CompilerParams(vmem_limit_bytes=16 * 1024 * 1024)


def cost(flops, moved):
    return pl.CostEstimate(flops=flops, bytes_accessed=moved, transcendentals=0)


def odd_device():
    return lax.axis_index("seq") % 2


def first_step(half):
    odd = odd_device()
    return {
        CHIP: WIN * (1 - odd),
        FAR: WIN * odd,
        NEXT_CHIP: 2 * WIN * (1 - odd) - WIN * odd,
        NEXT_FAR: 2 * WIN * odd - WIN * (1 - odd),
    }[half]


def same(count):
    return lax.broadcasted_iota(jnp.int32, (count, count), 0) == lax.broadcasted_iota(
        jnp.int32, (count, count), 1
    )


def squares_row(rows):
    gram = lax.dot_general(
        rows, rows, (((1,), (1,)), ((), ())), preferred_element_type=jnp.float32
    )
    return jnp.sum(jnp.where(same(rows.shape[0]), gram, 0.0), axis=0, keepdims=True)


def fill_masks(first_ref, pad_ref, time_ref, station_ref, stations, total_steps):
    own = 2 * WIN * stations
    keys, columns = 2 * own, GROUP * own
    key = lax.broadcasted_iota(jnp.int32, (keys, columns), 0)
    query = lax.broadcasted_iota(jnp.int32, (keys, columns), 1) % own

    def time_of(row):
        half, step = row // (WIN * stations), (row // stations) % WIN
        start = jnp.where(half == CHIP, first_step(CHIP), first_step(FAR))
        start = jnp.where(half == NEXT_CHIP, first_step(NEXT_CHIP), start)
        return step + jnp.where(half == NEXT_FAR, first_step(NEXT_FAR), start)

    key_station, query_station = key % stations, query % stations
    key_time, query_time = time_of(key), time_of(query)
    same_station = key_station == query_station
    same_time = key_time == query_time
    near = jnp.abs(key_time - query_time) <= WIN
    step = lax.axis_index("seq") * (2 * WIN) + key_time
    for m in range(time_ref.shape[0]):
        first = jnp.zeros((keys, columns), jnp.int32)
        pad = jnp.zeros((keys, columns), jnp.int32)
        for s in range(stations):
            first = jnp.where(key_station == s, first_ref[m, s], first)
            pad = jnp.where(key_station == s, pad_ref[m, s], pad)
        recorded = (step >= first) & (step < total_steps - pad)
        time_ref[m] = jnp.where(same_station & near & (recorded | same_time), 0.0, -BIG)
        station_ref[m] = jnp.where(same_time & (recorded | same_station), 0.0, -BIG)[:own]


def halves_kernel(signal_hbm, chip_ref, far_ref, signal_ref, arrived):
    copy = pltpu.make_async_copy(signal_hbm, signal_ref, arrived)
    copy.start()
    micro, _, stations, _ = signal_ref.shape
    edge = WIN * stations
    copy.wait()
    for half, half_ref in ((FAR, far_ref), (CHIP, chip_ref)):
        start = first_step(half)
        for m in range(micro):
            for t in range(0, WIN, 2):
                pair = [signal_ref[m, start + t + i].astype(jnp.float32) for i in range(2)]
                at = m * edge + t * stations
                half_ref[at : at + 2 * stations, :] = jnp.concatenate(pair, axis=0).astype(
                    jnp.bfloat16
                )


def fixed_kernel(
    weights_hbm, first_hbm, pad_hbm, _, weights_ref, time_ref, station_ref,
    first_ref, pad_ref, arrived, *, stations, total_steps,
):
    copies = [
        pltpu.make_async_copy(first_hbm, first_ref, arrived.at[0]),
        pltpu.make_async_copy(pad_hbm, pad_ref, arrived.at[1]),
        pltpu.make_async_copy(weights_hbm, weights_ref, arrived.at[2]),
    ]
    for copy in copies:
        copy.start()
    copies[0].wait()
    copies[1].wait()
    fill_masks(first_ref, pad_ref, time_ref, station_ref, stations, total_steps)
    copies[2].wait()


def squares_kernel(*refs):
    out_ref = refs[-1]
    out_ref[...] = jnp.zeros(out_ref.shape, jnp.float32)
    for half, half_ref in enumerate(refs[:-1]):
        out_ref[half : half + 1, 0 : half_ref.shape[0]] = squares_row(half_ref[...])


def scaled(rows, total):
    count = rows.shape[0]
    factor = lax.rsqrt(total / (HEADS * HEAD) + EPS)
    column = jnp.sum(jnp.where(same(count), factor, 0.0), axis=1, keepdims=True)
    return (rows.astype(jnp.float32) * column).astype(jnp.bfloat16)


def norm_kernel(half_ref, mine_ref, squares_ref, normed_ref, *, line):
    rows = half_ref[...]
    count = rows.shape[0]
    normed_ref[...] = scaled(rows, mine_ref[0:1, 0:count] + squares_ref[line : line + 1, 0:count])


def copy_kernel(*refs):
    count = len(refs) // 2
    for source, target in zip(refs[:count], refs[count:]):
        target[...] = source[...]


def add_kernel(mine_ref, other_ref, out_ref):
    out_ref[...] = jnp.zeros(out_ref.shape, jnp.float32)
    out_ref[0:1, :] = mine_ref[0:1, :] + other_ref[FAR : FAR + 1, :]


def project_kernel(weights_ref, *refs):
    count = len(refs) // 2
    halves, outs = refs[:count], refs[count:]
    rows = halves[0].shape[0]
    width = 3 * HEAD
    for head in range(weights_ref.shape[1]):
        lanes = slice(head * HEAD, (head + 1) * HEAD)
        projected = jnp.dot(
            jnp.concatenate([half[:, lanes] for half in halves], axis=0),
            weights_ref[0, head],
            preferred_element_type=jnp.float32,
        ).astype(jnp.bfloat16)
        for i, out in enumerate(outs):
            out[:, head * width : (head + 1) * width] = projected[i * rows : (i + 1) * rows]


def softmax_columns(scores):
    grown = jnp.exp(scores - jnp.max(scores, axis=0, keepdims=True))
    return (grown * (1.0 / jnp.sum(grown, axis=0, keepdims=True))).astype(jnp.bfloat16)


def layer_kernel(
    chip_ref, far_ref, squares_ref, time_ref, station_ref, weights_ref, kept_chip_ref, kept_far_ref,
    *refs, tick, stations, last,
):
    edge = WIN * stations
    micro = chip_ref.shape[0] // edge
    own = 2 * edge
    heads_dev = weights_ref.shape[1]
    width = 3 * HEAD
    bf16, f32 = jnp.bfloat16, jnp.float32
    active = lax.axis_index("section") == tick
    projected = [None] * 4
    if tick == 0:
        next_far_ref, next_chip_ref, *refs = refs
        late = [
            (half, half_ref, squares_ref[half : half + 1, :], True)
            for half, half_ref in enumerate((chip_ref, far_ref, next_far_ref, next_chip_ref))
        ]
    else:
        next_far_ref, far_squares_ref, next_chip_ref, projected[CHIP], *refs = refs
        late = [
            (FAR, far_ref, squares_ref[FAR : FAR + 1, :], False),
            (NEXT_FAR, next_far_ref, far_squares_ref[0:1, :], True),
        ]
    outs, refs = (refs[:1], refs[1:]) if last else (refs[:2], refs[2:])
    normed, refs = refs[: len(late)], refs[len(late) :]
    projecting = [half for half, *_ in late]
    if tick > 0:
        projecting.append(NEXT_CHIP)
    for half, half_ref in zip(projecting, refs):
        projected[half] = half_ref

    def write(m, lanes, values):
        for half in (CHIP, FAR):
            part = values[half * edge : (half + 1) * edge].astype(bf16)
            if last:
                for t in range(WIN):
                    outs[0][0, m, first_step(half) + t, :, lanes] = part[
                        t * stations : (t + 1) * stations
                    ]
            else:
                outs[half][m * edge : (m + 1) * edge, lanes] = part

    def rows_of(halves, m, at):
        return [projected[half][m * edge : (m + 1) * edge, at : at + HEAD] for half in halves]

    @pl.when(active)
    def _():
        lane = lax.broadcasted_iota(jnp.int32, (micro * edge, 128), 1)
        row = lax.broadcasted_iota(jnp.int32, (micro * edge, 128), 0)
        for (_, half_ref, line, complete), normed_ref in zip(late, normed):
            total = jnp.where(lane == row, line, 0.0)
            if not complete:
                for head in range(heads_dev):
                    part = half_ref[:, head * HEAD : (head + 1) * HEAD].astype(f32)
                    total = total + part * part
            factor = lax.rsqrt(jnp.sum(total, axis=1, keepdims=True) / (HEADS * HEAD) + EPS)
            normed_ref[...] = (half_ref[...].astype(f32) * factor).astype(bf16)
        if tick > 0:
            normed.append(next_chip_ref)
        project_kernel(weights_ref, *normed, *[projected[half] for half in projecting])
        pairs = [(g, m) for g in range(heads_dev // GROUP) for m in range(micro)]
        blank = jnp.zeros((own, HEAD), bf16)
        scores = []
        for g, m in pairs:
            at = [(g * GROUP + j) * width for j in range(GROUP)]
            queries = [jnp.concatenate(rows_of((CHIP, FAR), m, a), axis=0) for a in at]
            spread = jnp.concatenate(
                [
                    jnp.concatenate(
                        [queries[j] if i == j else blank for i in range(GROUP)],
                        axis=1,
                    )
                    for j in range(GROUP)
                ],
                axis=0,
            )
            keys = jnp.concatenate(
                [jnp.concatenate(rows_of(range(4), m, a + HEAD), axis=0) for a in at], axis=1
            )
            scores.append(
                lax.dot_general(
                    keys, spread, (((1,), (1,)), ((), ())), preferred_element_type=f32
                )
                * (1.0 / math.sqrt(HEAD))
            )
        mixes = []
        for (g, m), score in zip(pairs, scores):
            time_weights = softmax_columns(score + time_ref[m])
            station_weights = softmax_columns(score[:own] + station_ref[m])
            mixes.append(jnp.concatenate([time_weights, station_weights], axis=0).T)
        for (g, m), mix in zip(pairs, mixes):
            for j in range(GROUP):
                head = g * GROUP + j
                at = head * width + 2 * HEAD
                mixed = jnp.dot(
                    mix[j * own : (j + 1) * own],
                    jnp.concatenate(rows_of((0, 1, 2, 3, CHIP, FAR), m, at), axis=0),
                    preferred_element_type=f32,
                )
                lanes = slice(head * HEAD, (head + 1) * HEAD)
                hidden = jnp.concatenate(
                    [ref[m * edge : (m + 1) * edge, lanes] for ref in (chip_ref, far_ref)], axis=0
                )
                result = hidden.astype(f32) + mixed
                write(m, lanes, result)

    @pl.when(jnp.logical_not(active))
    def _():
        for m in range(micro):
            for head in range(heads_dev):
                lanes = slice(head * HEAD, (head + 1) * HEAD)
                kept = [
                    ref[m * edge : (m + 1) * edge, lanes] for ref in (kept_chip_ref, kept_far_ref)
                ]
                write(m, lanes, jnp.concatenate(kept, axis=0).astype(f32))


def body(signal, head_proj, record_start, record_pad):
    section_count = lax.axis_size("section")
    seq_count = lax.axis_size("seq")
    rep_count = lax.axis_size("rep")
    micro, steps, stations, features = signal.shape
    heads_dev = head_proj.shape[1]
    edge = WIN * stations
    own, reach = 2 * edge, 4 * edge
    bf16, f32 = jnp.bfloat16, jnp.float32
    half_shape = jax.ShapeDtypeStruct((micro * edge, features), bf16)
    squares_shape = jax.ShapeDtypeStruct((8, 128), f32)
    projected_shape = jax.ShapeDtypeStruct((micro * edge, heads_dev * 3 * HEAD), bf16)
    signal_bytes = signal.size * 2

    def in_hbm(block):
        return pltpu.with_memory_space_constraint(block, pltpu.HBM)

    def squares_of(*halves):
        return pl.pallas_call(
            squares_kernel,
            in_specs=[VMEM] * len(halves),
            out_specs=VMEM,
            out_shape=squares_shape,
            compiler_params=PARAMS,
            name="squares",
        )(*halves)

    def normed(rows, squares, line):
        return pl.pallas_call(
            lambda *refs: norm_kernel(*refs, line=line),
            in_specs=[VMEM] * 3,
            out_specs=VMEM,
            out_shape=half_shape,
            compiler_params=PARAMS,
            cost_estimate=BUSY,
            name="norm",
        )(rows, squares_of(rows), squares)

    def again(*blocks):
        return pl.pallas_call(
            copy_kernel,
            in_specs=[VMEM] * len(blocks),
            out_specs=[VMEM] * len(blocks),
            out_shape=[jax.ShapeDtypeStruct(block.shape, block.dtype) for block in blocks],
            compiler_params=PARAMS,
            cost_estimate=BUSY,
            name="copy",
        )(*blocks)

    def project(*halves):
        return pl.pallas_call(
            project_kernel,
            in_specs=[VMEM] * (1 + len(halves)),
            out_specs=[VMEM] * len(halves),
            out_shape=[projected_shape] * len(halves),
            compiler_params=PARAMS,
            cost_estimate=BUSY,
            name="project",
        )(weights, *halves)

    chip, far = pl.pallas_call(
        halves_kernel,
        in_specs=[HBM],
        out_specs=[VMEM] * 2,
        out_shape=[half_shape] * 2,
        scratch_shapes=[pltpu.VMEM(signal.shape, bf16), pltpu.SemaphoreType.DMA],
        compiler_params=PARAMS,
        cost_estimate=cost(signal.size, 2 * signal_bytes),
        name="halves",
    )(in_hbm(signal))
    def moved(block, source, target, hop, other=False):
        route = []
        for i in range(seq_count):
            to = i if hop == 0 else i + 1 - 2 * (i % 2) if hop == 1 else i - 1 + 2 * (i % 2)
            if 0 <= to < seq_count:
                for r in range(rep_count):
                    route.append(
                        (
                            (source * seq_count + i) * rep_count + r,
                            (target * seq_count + to) * rep_count
                            + ((r + 1) % rep_count if other else r),
                        )
                    )
        return lax.ppermute(block, ("section", "seq", "rep"), route)

    next_far = moved(far, 0, 0, 2)
    next_chip = moved(chip, 0, 0, 1)
    squares = lax.psum(squares_of(chip, far, next_far, next_chip), "rep")
    weights, time_bias, station_bias = pl.pallas_call(
        lambda *refs: fixed_kernel(*refs, stations=stations, total_steps=steps * seq_count),
        in_specs=[HBM] * 3 + [VMEM],
        out_specs=[VMEM] * 3,
        out_shape=[
            jax.ShapeDtypeStruct(head_proj.shape, bf16),
            jax.ShapeDtypeStruct((micro, reach, GROUP * own), f32),
            jax.ShapeDtypeStruct((micro, own, GROUP * own), f32),
        ],
        scratch_shapes=[
            pltpu.SMEM(record_start.shape, jnp.int32),
            pltpu.SMEM(record_pad.shape, jnp.int32),
            pltpu.SemaphoreType.DMA((3,)),
        ],
        compiler_params=PARAMS,
        cost_estimate=cost(signal.size, 2 * head_proj.size),
        name="fixed",
    )(in_hbm(head_proj), in_hbm(record_start), in_hbm(record_pad), chip)
    inputs = (next_far, next_chip)
    kept = (chip, far)
    for tick in range(section_count):
        last = tick + 1 == section_count

        def kernel(*refs, tick=tick, last=last):
            layer_kernel(*refs, tick=tick, stations=stations, last=last)

        out_shape = (
            [jax.ShapeDtypeStruct((1,) + signal.shape, bf16)]
            if last
            else [half_shape, half_shape]
        )
        outputs = pl.pallas_call(
            kernel,
            in_specs=[VMEM] * (8 + len(inputs)),
            out_specs=[VMEM] * len(out_shape),
            out_shape=out_shape,
            scratch_shapes=[
                pltpu.VMEM(shape.shape, bf16)
                for shape, count in zip((half_shape, projected_shape), (4, 4) if tick == 0 else (2, 3))
                for _ in range(count)
            ],
            compiler_params=PARAMS,
            cost_estimate=cost(8 * signal.size * 3 * HEAD, 16 * signal_bytes),
            name="layer",
        )(
            chip, far, squares, time_bias, station_bias, weights, *kept, *inputs,
        )
        if last:
            return outputs[0]
        kept = outputs
        mine = squares_of(*kept)
        chip = moved(kept[0], tick, tick + 1, 0)
        next_far = moved(kept[1], tick, tick + 1, 2)
        squares = moved(mine, tick, tick + 1, 0, other=True)
        (mine_again,) = again(mine)
        far = moved(kept[1], tick, tick + 1, 0)
        far_squares = moved(mine_again, tick, tick + 1, 2, other=True)
        normed_chip = normed(chip, squares, CHIP)
        next_chip = moved(normed_chip, tick + 1, tick + 1, 1)
        far_squares = pl.pallas_call(
            add_kernel,
            in_specs=[VMEM] * 2,
            out_specs=VMEM,
            out_shape=squares_shape,
            compiler_params=PARAMS,
            cost_estimate=BUSY,
            name="add",
        )(squares_of(next_far), far_squares)
        inputs = (next_far, far_squares, next_chip, *project(normed_chip))


def solution(mesh):
    return jax.shard_map(
        body,
        mesh=mesh,
        in_specs=(P(None, "seq", None, "rep"), P("section", "rep", None, None), P(), P()),
        out_specs=P("section", None, "seq", None, "rep"),
        check_vma=False,
    )
```

```python
import math

import jax
import jax.numpy as jnp
from jax import lax
from jax.experimental import pallas as pl
from jax.experimental.pallas import tpu as pltpu
from jax.sharding import PartitionSpec as P

HEADS = 32
HEAD = 128
WIN = 4
GROUP = 4
EPS = 1e-06
BIG = 1e30
CHIP, FAR, NEXT_FAR, NEXT_CHIP = range(4)

HBM = pl.BlockSpec(memory_space=pltpu.HBM)
VMEM = pl.BlockSpec(memory_space=pltpu.VMEM)
BUSY = pl.CostEstimate(flops=2000000000, bytes_accessed=300000, transcendentals=0)
PARAMS = pltpu.CompilerParams(vmem_limit_bytes=16 * 1024 * 1024)


def cost(flops, moved):
    return pl.CostEstimate(flops=flops, bytes_accessed=moved, transcendentals=0)


def odd_device():
    return lax.axis_index("seq") % 2


def first_step(half):
    odd = odd_device()
    return {
        CHIP: WIN * (1 - odd),
        FAR: WIN * odd,
        NEXT_CHIP: 2 * WIN * (1 - odd) - WIN * odd,
        NEXT_FAR: 2 * WIN * odd - WIN * (1 - odd),
    }[half]


def same(count):
    return lax.broadcasted_iota(jnp.int32, (count, count), 0) == lax.broadcasted_iota(
        jnp.int32, (count, count), 1
    )


def squares_row(rows):
    gram = lax.dot_general(
        rows, rows, (((1,), (1,)), ((), ())), preferred_element_type=jnp.float32
    )
    return jnp.sum(jnp.where(same(rows.shape[0]), gram, 0.0), axis=0, keepdims=True)


def fill_masks(first_ref, pad_ref, time_ref, station_ref, stations, total_steps):
    own = 2 * WIN * stations
    keys, columns = 2 * own, GROUP * own
    key = lax.broadcasted_iota(jnp.int32, (keys, columns), 0)
    query = lax.broadcasted_iota(jnp.int32, (keys, columns), 1) % own

    def time_of(row):
        half, step = row // (WIN * stations), (row // stations) % WIN
        start = jnp.where(half == CHIP, first_step(CHIP), first_step(FAR))
        start = jnp.where(half == NEXT_CHIP, first_step(NEXT_CHIP), start)
        return step + jnp.where(half == NEXT_FAR, first_step(NEXT_FAR), start)

    key_station, query_station = key % stations, query % stations
    key_time, query_time = time_of(key), time_of(query)
    same_station = key_station == query_station
    same_time = key_time == query_time
    near = jnp.abs(key_time - query_time) <= WIN
    step = lax.axis_index("seq") * (2 * WIN) + key_time
    for m in range(time_ref.shape[0]):
        first = jnp.zeros((keys, columns), jnp.int32)
        pad = jnp.zeros((keys, columns), jnp.int32)
        for s in range(stations):
            first = jnp.where(key_station == s, first_ref[m, s], first)
            pad = jnp.where(key_station == s, pad_ref[m, s], pad)
        recorded = (step >= first) & (step < total_steps - pad)
        time_ref[m] = jnp.where(same_station & near & (recorded | same_time), 0.0, -BIG)
        station_ref[m] = jnp.where(same_time & (recorded | same_station), 0.0, -BIG)[:own]


def halves_kernel(signal_hbm, chip_ref, far_ref, signal_ref, arrived):
    copy = pltpu.make_async_copy(signal_hbm, signal_ref, arrived)
    copy.start()
    micro, _, stations, _ = signal_ref.shape
    edge = WIN * stations
    copy.wait()
    for half, half_ref in ((FAR, far_ref), (CHIP, chip_ref)):
        start = first_step(half)
        for m in range(micro):
            for t in range(0, WIN, 2):
                pair = [signal_ref[m, start + t + i].astype(jnp.float32) for i in range(2)]
                at = m * edge + t * stations
                half_ref[at : at + 2 * stations, :] = jnp.concatenate(pair, axis=0).astype(
                    jnp.bfloat16
                )


def fixed_kernel(
    weights_hbm, first_hbm, pad_hbm, _, weights_ref, time_ref, station_ref,
    first_ref, pad_ref, arrived, *, stations, total_steps,
):
    copies = [
        pltpu.make_async_copy(first_hbm, first_ref, arrived.at[0]),
        pltpu.make_async_copy(pad_hbm, pad_ref, arrived.at[1]),
        pltpu.make_async_copy(weights_hbm, weights_ref, arrived.at[2]),
    ]
    for copy in copies:
        copy.start()
    copies[0].wait()
    copies[1].wait()
    fill_masks(first_ref, pad_ref, time_ref, station_ref, stations, total_steps)
    copies[2].wait()


def squares_kernel(*refs):
    out_ref = refs[-1]
    out_ref[...] = jnp.zeros(out_ref.shape, jnp.float32)
    for half, half_ref in enumerate(refs[:-1]):
        out_ref[half : half + 1, 0 : half_ref.shape[0]] = squares_row(half_ref[...])


def scaled(rows, total):
    count = rows.shape[0]
    factor = lax.rsqrt(total / (HEADS * HEAD) + EPS)
    column = jnp.sum(jnp.where(same(count), factor, 0.0), axis=1, keepdims=True)
    return (rows.astype(jnp.float32) * column).astype(jnp.bfloat16)


def norm_kernel(half_ref, mine_ref, squares_ref, normed_ref, *, line):
    rows = half_ref[...]
    count = rows.shape[0]
    normed_ref[...] = scaled(rows, mine_ref[0:1, 0:count] + squares_ref[line : line + 1, 0:count])


def copy_kernel(*refs):
    count = len(refs) // 2
    for source, target in zip(refs[:count], refs[count:]):
        target[...] = source[...]


def add_kernel(mine_ref, other_ref, out_ref):
    out_ref[...] = jnp.zeros(out_ref.shape, jnp.float32)
    out_ref[0:1, :] = mine_ref[0:1, :] + other_ref[FAR : FAR + 1, :]


def project_kernel(weights_ref, *refs):
    count = len(refs) // 2
    halves, outs = refs[:count], refs[count:]
    rows = halves[0].shape[0]
    width = 3 * HEAD
    for head in range(weights_ref.shape[1]):
        lanes = slice(head * HEAD, (head + 1) * HEAD)
        projected = jnp.dot(
            jnp.concatenate([half[:, lanes] for half in halves], axis=0),
            weights_ref[0, head],
            preferred_element_type=jnp.float32,
        ).astype(jnp.bfloat16)
        for i, out in enumerate(outs):
            out[:, head * width : (head + 1) * width] = projected[i * rows : (i + 1) * rows]


def softmax_columns(scores):
    grown = jnp.exp(scores - jnp.max(scores, axis=0, keepdims=True))
    return (grown * (1.0 / jnp.sum(grown, axis=0, keepdims=True))).astype(jnp.bfloat16)


def layer_kernel(
    chip_ref, far_ref, squares_ref, time_ref, station_ref, weights_ref, kept_chip_ref, kept_far_ref,
    *refs, tick, stations, last,
):
    edge = WIN * stations
    micro = chip_ref.shape[0] // edge
    own = 2 * edge
    heads_dev = weights_ref.shape[1]
    width = 3 * HEAD
    bf16, f32 = jnp.bfloat16, jnp.float32
    active = lax.axis_index("section") == tick
    projected = [None] * 4
    if tick == 0:
        next_far_ref, next_chip_ref, *refs = refs
        late = [
            (half, half_ref, squares_ref[half : half + 1, :], True)
            for half, half_ref in enumerate((chip_ref, far_ref, next_far_ref, next_chip_ref))
        ]
    else:
        next_far_ref, far_squares_ref, next_chip_ref, projected[CHIP], *refs = refs
        late = [
            (FAR, far_ref, squares_ref[FAR : FAR + 1, :], False),
            (NEXT_FAR, next_far_ref, far_squares_ref[0:1, :], True),
        ]
    outs, refs = (refs[:1], refs[1:]) if last else (refs[:2], refs[2:])
    normed, refs = refs[: len(late)], refs[len(late) :]
    projecting = [half for half, *_ in late]
    if tick > 0:
        projecting.append(NEXT_CHIP)
    for half, half_ref in zip(projecting, refs):
        projected[half] = half_ref

    def write(m, lanes, values):
        for half in (CHIP, FAR):
            part = values[half * edge : (half + 1) * edge].astype(bf16)
            if last:
                for t in range(WIN):
                    outs[0][0, m, first_step(half) + t, :, lanes] = part[
                        t * stations : (t + 1) * stations
                    ]
            else:
                outs[half][m * edge : (m + 1) * edge, lanes] = part

    def rows_of(halves, m, at):
        return [projected[half][m * edge : (m + 1) * edge, at : at + HEAD] for half in halves]

    @pl.when(active)
    def _():
        lane = lax.broadcasted_iota(jnp.int32, (micro * edge, 128), 1)
        row = lax.broadcasted_iota(jnp.int32, (micro * edge, 128), 0)
        for (_, half_ref, line, complete), normed_ref in zip(late, normed):
            total = jnp.where(lane == row, line, 0.0)
            if not complete:
                for head in range(heads_dev):
                    part = half_ref[:, head * HEAD : (head + 1) * HEAD].astype(f32)
                    total = total + part * part
            factor = lax.rsqrt(jnp.sum(total, axis=1, keepdims=True) / (HEADS * HEAD) + EPS)
            normed_ref[...] = (half_ref[...].astype(f32) * factor).astype(bf16)
        if tick > 0:
            normed.append(next_chip_ref)
        project_kernel(weights_ref, *normed, *[projected[half] for half in projecting])
        groups = range(heads_dev // GROUP)
        blank = jnp.zeros((own, HEAD), bf16)
        columns = GROUP * own
        scores = {}
        for g in groups:
            at = [(g * GROUP + j) * width for j in range(GROUP)]
            spread, keys = [], []
            for m in range(micro):
                queries = [jnp.concatenate(rows_of((CHIP, FAR), m, a), axis=0) for a in at]
                for j in range(GROUP):
                    spread.append(
                        jnp.concatenate(
                            [queries[j] if i == j else blank for i in range(GROUP)], axis=1
                        )
                    )
                keys.append(
                    jnp.concatenate(
                        [jnp.concatenate(rows_of(range(4), m, a + HEAD), axis=0) for a in at], axis=1
                    )
                )
            score = lax.dot_general(
                jnp.concatenate(keys, axis=0),
                jnp.concatenate(spread, axis=0),
                (((1,), (1,)), ((), ())),
                preferred_element_type=f32,
            )
            for m in range(micro):
                scores[g, m] = score[
                    m * 2 * own : (m + 1) * 2 * own, m * columns : (m + 1) * columns
                ] * (1.0 / math.sqrt(HEAD))
        mixes = {}
        for (g, m), score in scores.items():
            time_weights = softmax_columns(score + time_ref[m])
            station_weights = softmax_columns(score[:own] + station_ref[m])
            mixes[g, m] = jnp.concatenate([time_weights, station_weights], axis=0).T
        for (g, m), mix in mixes.items():
            for j in range(0, GROUP, 2):
                pair = [g * GROUP + j, g * GROUP + j + 1]
                values = [
                    jnp.concatenate(rows_of((0, 1, 2, 3, CHIP, FAR), m, head * width + 2 * HEAD), axis=0)
                    for head in pair
                ]
                mixed = jnp.dot(
                    mix[j * own : (j + 2) * own],
                    jnp.concatenate(values, axis=1),
                    preferred_element_type=f32,
                )
                for i, head in enumerate(pair):
                    lanes = slice(head * HEAD, (head + 1) * HEAD)
                    hidden = jnp.concatenate(
                        [ref[m * edge : (m + 1) * edge, lanes] for ref in (chip_ref, far_ref)], axis=0
                    )
                    update = mixed[i * own : (i + 1) * own, i * HEAD : (i + 1) * HEAD]
                    write(m, lanes, hidden.astype(f32) + update)

    @pl.when(jnp.logical_not(active))
    def _():
        for m in range(micro):
            for head in range(heads_dev):
                lanes = slice(head * HEAD, (head + 1) * HEAD)
                kept = [
                    ref[m * edge : (m + 1) * edge, lanes] for ref in (kept_chip_ref, kept_far_ref)
                ]
                write(m, lanes, jnp.concatenate(kept, axis=0).astype(f32))


def body(signal, head_proj, record_start, record_pad):
    section_count = lax.axis_size("section")
    seq_count = lax.axis_size("seq")
    rep_count = lax.axis_size("rep")
    micro, steps, stations, features = signal.shape
    heads_dev = head_proj.shape[1]
    edge = WIN * stations
    own, reach = 2 * edge, 4 * edge
    bf16, f32 = jnp.bfloat16, jnp.float32
    half_shape = jax.ShapeDtypeStruct((micro * edge, features), bf16)
    squares_shape = jax.ShapeDtypeStruct((8, 128), f32)
    projected_shape = jax.ShapeDtypeStruct((micro * edge, heads_dev * 3 * HEAD), bf16)
    signal_bytes = signal.size * 2

    def in_hbm(block):
        return pltpu.with_memory_space_constraint(block, pltpu.HBM)

    def squares_of(*halves):
        return pl.pallas_call(
            squares_kernel,
            in_specs=[VMEM] * len(halves),
            out_specs=VMEM,
            out_shape=squares_shape,
            compiler_params=PARAMS,
            name="squares",
        )(*halves)

    def normed(rows, squares, line):
        return pl.pallas_call(
            lambda *refs: norm_kernel(*refs, line=line),
            in_specs=[VMEM] * 3,
            out_specs=VMEM,
            out_shape=half_shape,
            compiler_params=PARAMS,
            cost_estimate=BUSY,
            name="norm",
        )(rows, squares_of(rows), squares)

    def again(*blocks):
        return pl.pallas_call(
            copy_kernel,
            in_specs=[VMEM] * len(blocks),
            out_specs=[VMEM] * len(blocks),
            out_shape=[jax.ShapeDtypeStruct(block.shape, block.dtype) for block in blocks],
            compiler_params=PARAMS,
            cost_estimate=BUSY,
            name="copy",
        )(*blocks)

    def project(*halves):
        return pl.pallas_call(
            project_kernel,
            in_specs=[VMEM] * (1 + len(halves)),
            out_specs=[VMEM] * len(halves),
            out_shape=[projected_shape] * len(halves),
            compiler_params=PARAMS,
            cost_estimate=BUSY,
            name="project",
        )(weights, *halves)

    chip, far = pl.pallas_call(
        halves_kernel,
        in_specs=[HBM],
        out_specs=[VMEM] * 2,
        out_shape=[half_shape] * 2,
        scratch_shapes=[pltpu.VMEM(signal.shape, bf16), pltpu.SemaphoreType.DMA],
        compiler_params=PARAMS,
        cost_estimate=cost(signal.size, 2 * signal_bytes),
        name="halves",
    )(in_hbm(signal))
    def moved(block, source, target, hop, other=False):
        route = []
        for i in range(seq_count):
            to = i if hop == 0 else i + 1 - 2 * (i % 2) if hop == 1 else i - 1 + 2 * (i % 2)
            if 0 <= to < seq_count:
                for r in range(rep_count):
                    route.append(
                        (
                            (source * seq_count + i) * rep_count + r,
                            (target * seq_count + to) * rep_count
                            + ((r + 1) % rep_count if other else r),
                        )
                    )
        return lax.ppermute(block, ("section", "seq", "rep"), route)

    next_far = moved(far, 0, 0, 2)
    next_chip = moved(chip, 0, 0, 1)
    squares = lax.psum(squares_of(chip, far, next_far, next_chip), "rep")
    weights, time_bias, station_bias = pl.pallas_call(
        lambda *refs: fixed_kernel(*refs, stations=stations, total_steps=steps * seq_count),
        in_specs=[HBM] * 3 + [VMEM],
        out_specs=[VMEM] * 3,
        out_shape=[
            jax.ShapeDtypeStruct(head_proj.shape, bf16),
            jax.ShapeDtypeStruct((micro, reach, GROUP * own), f32),
            jax.ShapeDtypeStruct((micro, own, GROUP * own), f32),
        ],
        scratch_shapes=[
            pltpu.SMEM(record_start.shape, jnp.int32),
            pltpu.SMEM(record_pad.shape, jnp.int32),
            pltpu.SemaphoreType.DMA((3,)),
        ],
        compiler_params=PARAMS,
        cost_estimate=cost(signal.size, 2 * head_proj.size),
        name="fixed",
    )(in_hbm(head_proj), in_hbm(record_start), in_hbm(record_pad), chip)
    inputs = (next_far, next_chip)
    kept = (chip, far)
    for tick in range(section_count):
        last = tick + 1 == section_count

        def kernel(*refs, tick=tick, last=last):
            layer_kernel(*refs, tick=tick, stations=stations, last=last)

        out_shape = (
            [jax.ShapeDtypeStruct((1,) + signal.shape, bf16)]
            if last
            else [half_shape, half_shape]
        )
        outputs = pl.pallas_call(
            kernel,
            in_specs=[VMEM] * (8 + len(inputs)),
            out_specs=[VMEM] * len(out_shape),
            out_shape=out_shape,
            scratch_shapes=[
                pltpu.VMEM(shape.shape, bf16)
                for shape, count in zip((half_shape, projected_shape), (4, 4) if tick == 0 else (2, 3))
                for _ in range(count)
            ],
            compiler_params=PARAMS,
            cost_estimate=cost(8 * signal.size * 3 * HEAD, 16 * signal_bytes),
            name="layer",
        )(
            chip, far, squares, time_bias, station_bias, weights, *kept, *inputs,
        )
        if last:
            return outputs[0]
        kept = outputs
        mine = squares_of(*kept)
        chip = moved(kept[0], tick, tick + 1, 0)
        next_far = moved(kept[1], tick, tick + 1, 2)
        squares = moved(mine, tick, tick + 1, 0, other=True)
        (mine_again,) = again(mine)
        far = moved(kept[1], tick, tick + 1, 0)
        far_squares = moved(mine_again, tick, tick + 1, 2, other=True)
        normed_chip = normed(chip, squares, CHIP)
        next_chip = moved(normed_chip, tick + 1, tick + 1, 1)
        far_squares = pl.pallas_call(
            add_kernel,
            in_specs=[VMEM] * 2,
            out_specs=VMEM,
            out_shape=squares_shape,
            compiler_params=PARAMS,
            cost_estimate=BUSY,
            name="add",
        )(squares_of(next_far), far_squares)
        inputs = (next_far, far_squares, next_chip, *project(normed_chip))


def solution(mesh):
    return jax.shard_map(
        body,
        mesh=mesh,
        in_specs=(P(None, "seq", None, "rep"), P("section", "rep", None, None), P(), P()),
        out_specs=P("section", None, "seq", None, "rep"),
        check_vma=False,
    )
```

```python
import math

import jax
import jax.numpy as jnp
from jax import lax
from jax.experimental import pallas as pl
from jax.experimental.pallas import tpu as pltpu
from jax.sharding import PartitionSpec as P

HEADS = 32
HEAD = 128
WIN = 4
GROUP = 4
WEIGHT_PARTS = 4
EPS = 1e-06
BIG = 1e30
CHIP, FAR, NEXT_FAR, NEXT_CHIP = range(4)

HBM = pl.BlockSpec(memory_space=pltpu.HBM)
VMEM = pl.BlockSpec(memory_space=pltpu.VMEM)
BUSY = pl.CostEstimate(flops=2000000000, bytes_accessed=300000, transcendentals=0)
PARAMS = pltpu.CompilerParams(vmem_limit_bytes=16 * 1024 * 1024)


def cost(flops, moved):
    return pl.CostEstimate(flops=flops, bytes_accessed=moved, transcendentals=0)


def odd_device():
    return lax.axis_index("seq") % 2


def first_step(half):
    odd = odd_device()
    return {
        CHIP: WIN * (1 - odd),
        FAR: WIN * odd,
        NEXT_CHIP: 2 * WIN * (1 - odd) - WIN * odd,
        NEXT_FAR: 2 * WIN * odd - WIN * (1 - odd),
    }[half]


def same(count):
    return lax.broadcasted_iota(jnp.int32, (count, count), 0) == lax.broadcasted_iota(
        jnp.int32, (count, count), 1
    )


def squares_row(rows):
    gram = lax.dot_general(
        rows, rows, (((1,), (1,)), ((), ())), preferred_element_type=jnp.float32
    )
    return jnp.sum(jnp.where(same(rows.shape[0]), gram, 0.0), axis=0, keepdims=True)


def fill_masks(first_ref, pad_ref, time_ref, station_ref, stations, total_steps):
    own = 2 * WIN * stations
    keys, columns = 2 * own, GROUP * own
    key = lax.broadcasted_iota(jnp.int32, (keys, columns), 0)
    query = lax.broadcasted_iota(jnp.int32, (keys, columns), 1) % own

    def time_of(row):
        half, step = row // (WIN * stations), (row // stations) % WIN
        start = jnp.where(half == CHIP, first_step(CHIP), first_step(FAR))
        start = jnp.where(half == NEXT_CHIP, first_step(NEXT_CHIP), start)
        return step + jnp.where(half == NEXT_FAR, first_step(NEXT_FAR), start)

    key_station, query_station = key % stations, query % stations
    key_time, query_time = time_of(key), time_of(query)
    same_station = key_station == query_station
    same_time = key_time == query_time
    near = jnp.abs(key_time - query_time) <= WIN
    step = lax.axis_index("seq") * (2 * WIN) + key_time
    for m in range(time_ref.shape[0]):
        first = jnp.zeros((keys, columns), jnp.int32)
        pad = jnp.zeros((keys, columns), jnp.int32)
        for s in range(stations):
            first = jnp.where(key_station == s, first_ref[m, s], first)
            pad = jnp.where(key_station == s, pad_ref[m, s], pad)
        recorded = (step >= first) & (step < total_steps - pad)
        time_ref[m] = jnp.where(same_station & near & (recorded | same_time), 0.0, -BIG)
        station_ref[m] = jnp.where(same_time & (recorded | same_station), 0.0, -BIG)[:own]


def halves_kernel(signal_hbm, chip_ref, far_ref, signal_ref, arrived):
    copy = pltpu.make_async_copy(signal_hbm, signal_ref, arrived)
    copy.start()
    micro, _, stations, _ = signal_ref.shape
    edge = WIN * stations
    copy.wait()
    for half, half_ref in ((FAR, far_ref), (CHIP, chip_ref)):
        start = first_step(half)
        for m in range(micro):
            for t in range(0, WIN, 2):
                pair = [signal_ref[m, start + t + i].astype(jnp.float32) for i in range(2)]
                at = m * edge + t * stations
                half_ref[at : at + 2 * stations, :] = jnp.concatenate(pair, axis=0).astype(
                    jnp.bfloat16
                )


def fixed_kernel(
    weights_hbm, first_hbm, pad_hbm, _, weights_ref, time_ref, station_ref,
    first_ref, pad_ref, arrived, *, stations, total_steps,
):
    part = weights_hbm.shape[1] // WEIGHT_PARTS
    copies = [
        pltpu.make_async_copy(first_hbm, first_ref, arrived.at[0]),
        pltpu.make_async_copy(pad_hbm, pad_ref, arrived.at[1]),
    ]
    for i in range(WEIGHT_PARTS):
        heads = pl.ds(i * part, part)
        copies.append(
            pltpu.make_async_copy(
                weights_hbm.at[:, heads], weights_ref.at[:, heads], arrived.at[2 + i]
            )
        )
    for copy in copies:
        copy.start()
    copies[0].wait()
    copies[1].wait()
    fill_masks(first_ref, pad_ref, time_ref, station_ref, stations, total_steps)
    for copy in copies[2:]:
        copy.wait()


def squares_kernel(*refs):
    out_ref = refs[-1]
    out_ref[...] = jnp.zeros(out_ref.shape, jnp.float32)
    for half, half_ref in enumerate(refs[:-1]):
        out_ref[half : half + 1, 0 : half_ref.shape[0]] = squares_row(half_ref[...])


def scaled(rows, total):
    count = rows.shape[0]
    factor = lax.rsqrt(total / (HEADS * HEAD) + EPS)
    column = jnp.sum(jnp.where(same(count), factor, 0.0), axis=1, keepdims=True)
    return (rows.astype(jnp.float32) * column).astype(jnp.bfloat16)


def norm_kernel(half_ref, mine_ref, squares_ref, normed_ref, *, line):
    rows = half_ref[...]
    count = rows.shape[0]
    normed_ref[...] = scaled(rows, mine_ref[0:1, 0:count] + squares_ref[line : line + 1, 0:count])


def copy_kernel(*refs):
    count = len(refs) // 2
    for source, target in zip(refs[:count], refs[count:]):
        target[...] = source[...]


def add_kernel(mine_ref, other_ref, out_ref):
    out_ref[...] = jnp.zeros(out_ref.shape, jnp.float32)
    out_ref[0:1, :] = mine_ref[0:1, :] + other_ref[FAR : FAR + 1, :]


def project_kernel(weights_ref, *refs):
    count = len(refs) // 2
    halves, outs = refs[:count], refs[count:]
    rows = halves[0].shape[0]
    width = 3 * HEAD
    for head in range(weights_ref.shape[1]):
        lanes = slice(head * HEAD, (head + 1) * HEAD)
        projected = jnp.dot(
            jnp.concatenate([half[:, lanes] for half in halves], axis=0),
            weights_ref[0, head],
            preferred_element_type=jnp.float32,
        ).astype(jnp.bfloat16)
        for i, out in enumerate(outs):
            out[:, head * width : (head + 1) * width] = projected[i * rows : (i + 1) * rows]


def softmax_columns(scores):
    grown = jnp.exp(scores - jnp.max(scores, axis=0, keepdims=True))
    return (grown * (1.0 / jnp.sum(grown, axis=0, keepdims=True))).astype(jnp.bfloat16)


def layer_kernel(
    chip_ref, far_ref, squares_ref, time_ref, station_ref, weights_ref, kept_chip_ref, kept_far_ref,
    *refs, tick, stations, last,
):
    edge = WIN * stations
    micro = chip_ref.shape[0] // edge
    own = 2 * edge
    heads_dev = weights_ref.shape[1]
    width = 3 * HEAD
    bf16, f32 = jnp.bfloat16, jnp.float32
    active = lax.axis_index("section") == tick
    projected = [None] * 4
    if tick == 0:
        next_far_ref, next_chip_ref, *refs = refs
        late = [
            (half, half_ref, squares_ref[half : half + 1, :], True)
            for half, half_ref in enumerate((chip_ref, far_ref, next_far_ref, next_chip_ref))
        ]
    else:
        next_far_ref, far_squares_ref, next_chip_ref, projected[CHIP], *refs = refs
        late = [
            (FAR, far_ref, squares_ref[FAR : FAR + 1, :], False),
            (NEXT_FAR, next_far_ref, far_squares_ref[0:1, :], True),
        ]
    outs, refs = (refs[:1], refs[1:]) if last else (refs[:2], refs[2:])
    normed, refs = refs[: len(late)], refs[len(late) :]
    projecting = [half for half, *_ in late]
    if tick > 0:
        projecting.append(NEXT_CHIP)
    for half, half_ref in zip(projecting, refs):
        projected[half] = half_ref

    def write(m, lanes, values):
        for half in (CHIP, FAR):
            part = values[half * edge : (half + 1) * edge].astype(bf16)
            if last:
                for t in range(WIN):
                    outs[0][0, m, first_step(half) + t, :, lanes] = part[
                        t * stations : (t + 1) * stations
                    ]
            else:
                outs[half][m * edge : (m + 1) * edge, lanes] = part

    def rows_of(halves, m, at):
        return [projected[half][m * edge : (m + 1) * edge, at : at + HEAD] for half in halves]

    @pl.when(active)
    def _():
        lane = lax.broadcasted_iota(jnp.int32, (micro * edge, 128), 1)
        row = lax.broadcasted_iota(jnp.int32, (micro * edge, 128), 0)
        for (_, half_ref, line, complete), normed_ref in zip(late, normed):
            total = jnp.where(lane == row, line, 0.0)
            if not complete:
                for head in range(heads_dev):
                    part = half_ref[:, head * HEAD : (head + 1) * HEAD].astype(f32)
                    total = total + part * part
            factor = lax.rsqrt(jnp.sum(total, axis=1, keepdims=True) / (HEADS * HEAD) + EPS)
            normed_ref[...] = (half_ref[...].astype(f32) * factor).astype(bf16)
        if tick > 0:
            normed.append(next_chip_ref)
        project_kernel(weights_ref, *normed, *[projected[half] for half in projecting])
        pairs = [(g, m) for g in range(heads_dev // GROUP) for m in range(micro)]
        blank = jnp.zeros((own, HEAD), bf16)
        scores = []
        for g, m in pairs:
            at = [(g * GROUP + j) * width for j in range(GROUP)]
            queries = [jnp.concatenate(rows_of((CHIP, FAR), m, a), axis=0) for a in at]
            spread = jnp.concatenate(
                [
                    jnp.concatenate(
                        [queries[j] if i == j else blank for i in range(GROUP)],
                        axis=1,
                    )
                    for j in range(GROUP)
                ],
                axis=0,
            )
            keys = jnp.concatenate(
                [jnp.concatenate(rows_of(range(4), m, a + HEAD), axis=0) for a in at], axis=1
            )
            scores.append(
                lax.dot_general(
                    keys, spread, (((1,), (1,)), ((), ())), preferred_element_type=f32
                )
                * (1.0 / math.sqrt(HEAD))
            )
        mixes = []
        for (g, m), score in zip(pairs, scores):
            time_weights = softmax_columns(score + time_ref[m])
            station_weights = softmax_columns(score[:own] + station_ref[m])
            mixes.append(jnp.concatenate([time_weights, station_weights], axis=0).T)
        for (g, m), mix in zip(pairs, mixes):
            for j in range(GROUP):
                head = g * GROUP + j
                at = head * width + 2 * HEAD
                mixed = jnp.dot(
                    mix[j * own : (j + 1) * own],
                    jnp.concatenate(rows_of((0, 1, 2, 3, CHIP, FAR), m, at), axis=0),
                    preferred_element_type=f32,
                )
                lanes = slice(head * HEAD, (head + 1) * HEAD)
                hidden = jnp.concatenate(
                    [ref[m * edge : (m + 1) * edge, lanes] for ref in (chip_ref, far_ref)], axis=0
                )
                result = hidden.astype(f32) + mixed
                write(m, lanes, result)

    @pl.when(jnp.logical_not(active))
    def _():
        for m in range(micro):
            for head in range(heads_dev):
                lanes = slice(head * HEAD, (head + 1) * HEAD)
                kept = [
                    ref[m * edge : (m + 1) * edge, lanes] for ref in (kept_chip_ref, kept_far_ref)
                ]
                write(m, lanes, jnp.concatenate(kept, axis=0).astype(f32))


def body(signal, head_proj, record_start, record_pad):
    section_count = lax.axis_size("section")
    seq_count = lax.axis_size("seq")
    rep_count = lax.axis_size("rep")
    micro, steps, stations, features = signal.shape
    heads_dev = head_proj.shape[1]
    edge = WIN * stations
    own, reach = 2 * edge, 4 * edge
    bf16, f32 = jnp.bfloat16, jnp.float32
    half_shape = jax.ShapeDtypeStruct((micro * edge, features), bf16)
    squares_shape = jax.ShapeDtypeStruct((8, 128), f32)
    projected_shape = jax.ShapeDtypeStruct((micro * edge, heads_dev * 3 * HEAD), bf16)
    signal_bytes = signal.size * 2

    def in_hbm(block):
        return pltpu.with_memory_space_constraint(block, pltpu.HBM)

    def squares_of(*halves):
        return pl.pallas_call(
            squares_kernel,
            in_specs=[VMEM] * len(halves),
            out_specs=VMEM,
            out_shape=squares_shape,
            compiler_params=PARAMS,
            name="squares",
        )(*halves)

    def normed(rows, squares, line):
        return pl.pallas_call(
            lambda *refs: norm_kernel(*refs, line=line),
            in_specs=[VMEM] * 3,
            out_specs=VMEM,
            out_shape=half_shape,
            compiler_params=PARAMS,
            cost_estimate=BUSY,
            name="norm",
        )(rows, squares_of(rows), squares)

    def again(*blocks):
        return pl.pallas_call(
            copy_kernel,
            in_specs=[VMEM] * len(blocks),
            out_specs=[VMEM] * len(blocks),
            out_shape=[jax.ShapeDtypeStruct(block.shape, block.dtype) for block in blocks],
            compiler_params=PARAMS,
            cost_estimate=BUSY,
            name="copy",
        )(*blocks)

    def project(*halves):
        return pl.pallas_call(
            project_kernel,
            in_specs=[VMEM] * (1 + len(halves)),
            out_specs=[VMEM] * len(halves),
            out_shape=[projected_shape] * len(halves),
            compiler_params=PARAMS,
            cost_estimate=BUSY,
            name="project",
        )(weights, *halves)

    chip, far = pl.pallas_call(
        halves_kernel,
        in_specs=[HBM],
        out_specs=[VMEM] * 2,
        out_shape=[half_shape] * 2,
        scratch_shapes=[pltpu.VMEM(signal.shape, bf16), pltpu.SemaphoreType.DMA],
        compiler_params=PARAMS,
        cost_estimate=cost(signal.size, 2 * signal_bytes),
        name="halves",
    )(in_hbm(signal))
    def moved(block, source, target, hop, other=False):
        route = []
        for i in range(seq_count):
            to = i if hop == 0 else i + 1 - 2 * (i % 2) if hop == 1 else i - 1 + 2 * (i % 2)
            if 0 <= to < seq_count:
                for r in range(rep_count):
                    route.append(
                        (
                            (source * seq_count + i) * rep_count + r,
                            (target * seq_count + to) * rep_count
                            + ((r + 1) % rep_count if other else r),
                        )
                    )
        return lax.ppermute(block, ("section", "seq", "rep"), route)

    next_far = moved(far, 0, 0, 2)
    next_chip = moved(chip, 0, 0, 1)
    squares = lax.psum(squares_of(chip, far, next_far, next_chip), "rep")
    weights, time_bias, station_bias = pl.pallas_call(
        lambda *refs: fixed_kernel(*refs, stations=stations, total_steps=steps * seq_count),
        in_specs=[HBM] * 3 + [VMEM],
        out_specs=[VMEM] * 3,
        out_shape=[
            jax.ShapeDtypeStruct(head_proj.shape, bf16),
            jax.ShapeDtypeStruct((micro, reach, GROUP * own), f32),
            jax.ShapeDtypeStruct((micro, own, GROUP * own), f32),
        ],
        scratch_shapes=[
            pltpu.SMEM(record_start.shape, jnp.int32),
            pltpu.SMEM(record_pad.shape, jnp.int32),
            pltpu.SemaphoreType.DMA((2 + WEIGHT_PARTS,)),
        ],
        compiler_params=PARAMS,
        cost_estimate=cost(signal.size, 2 * head_proj.size),
        name="fixed",
    )(in_hbm(head_proj), in_hbm(record_start), in_hbm(record_pad), chip)
    inputs = (next_far, next_chip)
    kept = (chip, far)
    for tick in range(section_count):
        last = tick + 1 == section_count

        def kernel(*refs, tick=tick, last=last):
            layer_kernel(*refs, tick=tick, stations=stations, last=last)

        out_shape = (
            [jax.ShapeDtypeStruct((1,) + signal.shape, bf16)]
            if last
            else [half_shape, half_shape]
        )
        outputs = pl.pallas_call(
            kernel,
            in_specs=[VMEM] * (8 + len(inputs)),
            out_specs=[VMEM] * len(out_shape),
            out_shape=out_shape,
            scratch_shapes=[
                pltpu.VMEM(shape.shape, bf16)
                for shape, count in zip((half_shape, projected_shape), (4, 4) if tick == 0 else (2, 3))
                for _ in range(count)
            ],
            compiler_params=PARAMS,
            cost_estimate=cost(8 * signal.size * 3 * HEAD, 16 * signal_bytes),
            name="layer",
        )(
            chip, far, squares, time_bias, station_bias, weights, *kept, *inputs,
        )
        if last:
            return outputs[0]
        kept = outputs
        mine = squares_of(*kept)
        chip = moved(kept[0], tick, tick + 1, 0)
        next_far = moved(kept[1], tick, tick + 1, 2)
        squares = moved(mine, tick, tick + 1, 0, other=True)
        (mine_again,) = again(mine)
        far = moved(kept[1], tick, tick + 1, 0)
        far_squares = moved(mine_again, tick, tick + 1, 2, other=True)
        normed_chip = normed(chip, squares, CHIP)
        next_chip = moved(normed_chip, tick + 1, tick + 1, 1)
        far_squares = pl.pallas_call(
            add_kernel,
            in_specs=[VMEM] * 2,
            out_specs=VMEM,
            out_shape=squares_shape,
            compiler_params=PARAMS,
            cost_estimate=BUSY,
            name="add",
        )(squares_of(next_far), far_squares)
        inputs = (next_far, far_squares, next_chip, *project(normed_chip))


def solution(mesh):
    return jax.shard_map(
        body,
        mesh=mesh,
        in_specs=(P(None, "seq", None, "rep"), P("section", "rep", None, None), P(), P()),
        out_specs=P("section", None, "seq", None, "rep"),
        check_vma=False,
    )
```

```python
import math

import jax
import jax.numpy as jnp
from jax import lax
from jax.experimental import pallas as pl
from jax.experimental.pallas import tpu as pltpu
from jax.sharding import PartitionSpec as P

HEADS = 32
HEAD = 128
WIN = 4
GROUP = 4
WEIGHT_PARTS = 4
EPS = 1e-06
BIG = 1e30
CHIP, FAR, NEXT_FAR, NEXT_CHIP = range(4)

HBM = pl.BlockSpec(memory_space=pltpu.HBM)
VMEM = pl.BlockSpec(memory_space=pltpu.VMEM)
BUSY = pl.CostEstimate(flops=2000000000, bytes_accessed=300000, transcendentals=0)
PARAMS = pltpu.CompilerParams(vmem_limit_bytes=16 * 1024 * 1024)


def cost(flops, moved):
    return pl.CostEstimate(flops=flops, bytes_accessed=moved, transcendentals=0)


def odd_device():
    return lax.axis_index("seq") % 2


def first_step(half):
    odd = odd_device()
    return {
        CHIP: WIN * (1 - odd),
        FAR: WIN * odd,
        NEXT_CHIP: 2 * WIN * (1 - odd) - WIN * odd,
        NEXT_FAR: 2 * WIN * odd - WIN * (1 - odd),
    }[half]


def same(count):
    return lax.broadcasted_iota(jnp.int32, (count, count), 0) == lax.broadcasted_iota(
        jnp.int32, (count, count), 1
    )


def squares_row(rows):
    gram = lax.dot_general(
        rows, rows, (((1,), (1,)), ((), ())), preferred_element_type=jnp.float32
    )
    return jnp.sum(jnp.where(same(rows.shape[0]), gram, 0.0), axis=0, keepdims=True)


def mask_parts(stations):
    own = 2 * WIN * stations
    keys, columns = 2 * own, GROUP * own
    key = lax.broadcasted_iota(jnp.int32, (keys, columns), 0)
    query = lax.broadcasted_iota(jnp.int32, (keys, columns), 1) % own

    def time_of(row):
        half, step = row // (WIN * stations), (row // stations) % WIN
        start = jnp.where(half == CHIP, first_step(CHIP), first_step(FAR))
        start = jnp.where(half == NEXT_CHIP, first_step(NEXT_CHIP), start)
        return step + jnp.where(half == NEXT_FAR, first_step(NEXT_FAR), start)

    key_station, query_station = key % stations, query % stations
    key_time, query_time = time_of(key), time_of(query)
    same_station = key_station == query_station
    same_time = key_time == query_time
    near = jnp.abs(key_time - query_time) <= WIN
    step = lax.axis_index("seq") * (2 * WIN) + key_time
    return step, key_station, same_station & near, same_time, same_station & same_time


def fill_masks(parts, first_ref, pad_ref, time_ref, station_ref, total_steps):
    step, key_station, near, same_time, itself = parts
    for m in range(time_ref.shape[0]):
        first = jnp.zeros(step.shape, jnp.int32)
        end = jnp.zeros(step.shape, jnp.int32)
        for s in range(first_ref.shape[1]):
            first = jnp.where(key_station == s, first_ref[m, s], first)
            end = jnp.where(key_station == s, total_steps - pad_ref[m, s], end)
        recorded = (step >= first) & (step < end)
        time_ref[m] = jnp.where((near & recorded) | itself, 0.0, -BIG)
        station_ref[m] = jnp.where((same_time & recorded) | itself, 0.0, -BIG)[
            : station_ref.shape[1]
        ]


def halves_kernel(signal_hbm, chip_ref, far_ref, signal_ref, arrived):
    copy = pltpu.make_async_copy(signal_hbm, signal_ref, arrived)
    copy.start()
    micro, _, stations, _ = signal_ref.shape
    edge = WIN * stations
    copy.wait()
    for half, half_ref in ((FAR, far_ref), (CHIP, chip_ref)):
        start = first_step(half)
        for m in range(micro):
            for t in range(0, WIN, 2):
                pair = [signal_ref[m, start + t + i].astype(jnp.float32) for i in range(2)]
                at = m * edge + t * stations
                half_ref[at : at + 2 * stations, :] = jnp.concatenate(pair, axis=0).astype(
                    jnp.bfloat16
                )


def fixed_kernel(
    weights_hbm, first_hbm, pad_hbm, _, weights_ref, time_ref, station_ref,
    first_ref, pad_ref, arrived, *, stations, total_steps,
):
    part = weights_hbm.shape[1] // WEIGHT_PARTS
    copies = [
        pltpu.make_async_copy(first_hbm, first_ref, arrived.at[0]),
        pltpu.make_async_copy(pad_hbm, pad_ref, arrived.at[1]),
    ]
    for i in range(WEIGHT_PARTS):
        heads = pl.ds(i * part, part)
        copies.append(
            pltpu.make_async_copy(
                weights_hbm.at[:, heads], weights_ref.at[:, heads], arrived.at[2 + i]
            )
        )
    for copy in copies:
        copy.start()
    parts = mask_parts(stations)
    copies[0].wait()
    copies[1].wait()
    fill_masks(parts, first_ref, pad_ref, time_ref, station_ref, total_steps)
    for copy in copies[2:]:
        copy.wait()


def squares_kernel(*refs):
    out_ref = refs[-1]
    out_ref[...] = jnp.zeros(out_ref.shape, jnp.float32)
    for half, half_ref in enumerate(refs[:-1]):
        out_ref[half : half + 1, 0 : half_ref.shape[0]] = squares_row(half_ref[...])


def scaled(rows, total):
    count = rows.shape[0]
    factor = lax.rsqrt(total / (HEADS * HEAD) + EPS)
    column = jnp.sum(jnp.where(same(count), factor, 0.0), axis=1, keepdims=True)
    return (rows.astype(jnp.float32) * column).astype(jnp.bfloat16)


def norm_kernel(half_ref, mine_ref, squares_ref, normed_ref, *, line):
    rows = half_ref[...]
    count = rows.shape[0]
    normed_ref[...] = scaled(rows, mine_ref[0:1, 0:count] + squares_ref[line : line + 1, 0:count])


def copy_kernel(*refs):
    count = len(refs) // 2
    for source, target in zip(refs[:count], refs[count:]):
        target[...] = source[...]


def add_kernel(mine_ref, other_ref, out_ref):
    out_ref[...] = jnp.zeros(out_ref.shape, jnp.float32)
    out_ref[0:1, :] = mine_ref[0:1, :] + other_ref[FAR : FAR + 1, :]


def project_kernel(weights_ref, *refs):
    count = len(refs) // 2
    halves, outs = refs[:count], refs[count:]
    rows = halves[0].shape[0]
    width = 3 * HEAD
    for head in range(weights_ref.shape[1]):
        lanes = slice(head * HEAD, (head + 1) * HEAD)
        projected = jnp.dot(
            jnp.concatenate([half[:, lanes] for half in halves], axis=0),
            weights_ref[0, head],
            preferred_element_type=jnp.float32,
        ).astype(jnp.bfloat16)
        for i, out in enumerate(outs):
            out[:, head * width : (head + 1) * width] = projected[i * rows : (i + 1) * rows]


def softmax_columns(scores):
    grown = jnp.exp(scores - jnp.max(scores, axis=0, keepdims=True))
    return (grown * (1.0 / jnp.sum(grown, axis=0, keepdims=True))).astype(jnp.bfloat16)


def layer_kernel(
    chip_ref, far_ref, squares_ref, time_ref, station_ref, weights_ref, kept_chip_ref, kept_far_ref,
    *refs, tick, stations, last,
):
    edge = WIN * stations
    micro = chip_ref.shape[0] // edge
    own = 2 * edge
    heads_dev = weights_ref.shape[1]
    width = 3 * HEAD
    bf16, f32 = jnp.bfloat16, jnp.float32
    active = lax.axis_index("section") == tick
    projected = [None] * 4
    if tick == 0:
        next_far_ref, next_chip_ref, *refs = refs
        late = [
            (half, half_ref, squares_ref[half : half + 1, :], True)
            for half, half_ref in enumerate((chip_ref, far_ref, next_far_ref, next_chip_ref))
        ]
    else:
        next_far_ref, far_squares_ref, next_chip_ref, projected[CHIP], *refs = refs
        late = [
            (FAR, far_ref, squares_ref[FAR : FAR + 1, :], False),
            (NEXT_FAR, next_far_ref, far_squares_ref[0:1, :], True),
        ]
    outs, refs = (refs[:1], refs[1:]) if last else (refs[:2], refs[2:])
    normed, refs = refs[: len(late)], refs[len(late) :]
    projecting = [half for half, *_ in late]
    if tick > 0:
        projecting.append(NEXT_CHIP)
    for half, half_ref in zip(projecting, refs):
        projected[half] = half_ref

    def write(m, lanes, values):
        for half in (CHIP, FAR):
            part = values[half * edge : (half + 1) * edge].astype(bf16)
            if last:
                for t in range(WIN):
                    outs[0][0, m, first_step(half) + t, :, lanes] = part[
                        t * stations : (t + 1) * stations
                    ]
            else:
                outs[half][m * edge : (m + 1) * edge, lanes] = part

    def rows_of(halves, m, at):
        return [projected[half][m * edge : (m + 1) * edge, at : at + HEAD] for half in halves]

    @pl.when(active)
    def _():
        lane = lax.broadcasted_iota(jnp.int32, (micro * edge, 128), 1)
        row = lax.broadcasted_iota(jnp.int32, (micro * edge, 128), 0)
        for (_, half_ref, line, complete), normed_ref in zip(late, normed):
            total = jnp.where(lane == row, line, 0.0)
            if not complete:
                for head in range(heads_dev):
                    part = half_ref[:, head * HEAD : (head + 1) * HEAD].astype(f32)
                    total = total + part * part
            factor = lax.rsqrt(jnp.sum(total, axis=1, keepdims=True) / (HEADS * HEAD) + EPS)
            normed_ref[...] = (half_ref[...].astype(f32) * factor).astype(bf16)
        if tick > 0:
            normed.append(next_chip_ref)
        project_kernel(weights_ref, *normed, *[projected[half] for half in projecting])
        pairs = [(g, m) for g in range(heads_dev // GROUP) for m in range(micro)]
        blank = jnp.zeros((own, HEAD), bf16)
        scores = []
        for g, m in pairs:
            at = [(g * GROUP + j) * width for j in range(GROUP)]
            queries = [jnp.concatenate(rows_of((CHIP, FAR), m, a), axis=0) for a in at]
            spread = jnp.concatenate(
                [
                    jnp.concatenate(
                        [queries[j] if i == j else blank for i in range(GROUP)],
                        axis=1,
                    )
                    for j in range(GROUP)
                ],
                axis=0,
            )
            keys = jnp.concatenate(
                [jnp.concatenate(rows_of(range(4), m, a + HEAD), axis=0) for a in at], axis=1
            )
            scores.append(
                lax.dot_general(
                    keys, spread, (((1,), (1,)), ((), ())), preferred_element_type=f32
                )
                * (1.0 / math.sqrt(HEAD))
            )
        mixes = []
        for (g, m), score in zip(pairs, scores):
            time_weights = softmax_columns(score + time_ref[m])
            station_weights = softmax_columns(score[:own] + station_ref[m])
            mixes.append(jnp.concatenate([time_weights, station_weights], axis=0).T)
        for (g, m), mix in zip(pairs, mixes):
            for j in range(GROUP):
                head = g * GROUP + j
                at = head * width + 2 * HEAD
                mixed = jnp.dot(
                    mix[j * own : (j + 1) * own],
                    jnp.concatenate(rows_of((0, 1, 2, 3, CHIP, FAR), m, at), axis=0),
                    preferred_element_type=f32,
                )
                lanes = slice(head * HEAD, (head + 1) * HEAD)
                hidden = jnp.concatenate(
                    [ref[m * edge : (m + 1) * edge, lanes] for ref in (chip_ref, far_ref)], axis=0
                )
                result = hidden.astype(f32) + mixed
                write(m, lanes, result)

    @pl.when(jnp.logical_not(active))
    def _():
        for m in range(micro):
            for head in range(heads_dev):
                lanes = slice(head * HEAD, (head + 1) * HEAD)
                kept = [
                    ref[m * edge : (m + 1) * edge, lanes] for ref in (kept_chip_ref, kept_far_ref)
                ]
                write(m, lanes, jnp.concatenate(kept, axis=0).astype(f32))


def body(signal, head_proj, record_start, record_pad):
    section_count = lax.axis_size("section")
    seq_count = lax.axis_size("seq")
    rep_count = lax.axis_size("rep")
    micro, steps, stations, features = signal.shape
    heads_dev = head_proj.shape[1]
    edge = WIN * stations
    own, reach = 2 * edge, 4 * edge
    bf16, f32 = jnp.bfloat16, jnp.float32
    half_shape = jax.ShapeDtypeStruct((micro * edge, features), bf16)
    squares_shape = jax.ShapeDtypeStruct((8, 128), f32)
    projected_shape = jax.ShapeDtypeStruct((micro * edge, heads_dev * 3 * HEAD), bf16)
    signal_bytes = signal.size * 2

    def in_hbm(block):
        return pltpu.with_memory_space_constraint(block, pltpu.HBM)

    def squares_of(*halves):
        return pl.pallas_call(
            squares_kernel,
            in_specs=[VMEM] * len(halves),
            out_specs=VMEM,
            out_shape=squares_shape,
            compiler_params=PARAMS,
            name="squares",
        )(*halves)

    def normed(rows, squares, line):
        return pl.pallas_call(
            lambda *refs: norm_kernel(*refs, line=line),
            in_specs=[VMEM] * 3,
            out_specs=VMEM,
            out_shape=half_shape,
            compiler_params=PARAMS,
            cost_estimate=BUSY,
            name="norm",
        )(rows, squares_of(rows), squares)

    def again(*blocks):
        return pl.pallas_call(
            copy_kernel,
            in_specs=[VMEM] * len(blocks),
            out_specs=[VMEM] * len(blocks),
            out_shape=[jax.ShapeDtypeStruct(block.shape, block.dtype) for block in blocks],
            compiler_params=PARAMS,
            cost_estimate=BUSY,
            name="copy",
        )(*blocks)

    def project(*halves):
        return pl.pallas_call(
            project_kernel,
            in_specs=[VMEM] * (1 + len(halves)),
            out_specs=[VMEM] * len(halves),
            out_shape=[projected_shape] * len(halves),
            compiler_params=PARAMS,
            cost_estimate=BUSY,
            name="project",
        )(weights, *halves)

    chip, far = pl.pallas_call(
        halves_kernel,
        in_specs=[HBM],
        out_specs=[VMEM] * 2,
        out_shape=[half_shape] * 2,
        scratch_shapes=[pltpu.VMEM(signal.shape, bf16), pltpu.SemaphoreType.DMA],
        compiler_params=PARAMS,
        cost_estimate=cost(signal.size, 2 * signal_bytes),
        name="halves",
    )(in_hbm(signal))
    def moved(block, source, target, hop, other=False):
        route = []
        for i in range(seq_count):
            to = i if hop == 0 else i + 1 - 2 * (i % 2) if hop == 1 else i - 1 + 2 * (i % 2)
            if 0 <= to < seq_count:
                for r in range(rep_count):
                    route.append(
                        (
                            (source * seq_count + i) * rep_count + r,
                            (target * seq_count + to) * rep_count
                            + ((r + 1) % rep_count if other else r),
                        )
                    )
        return lax.ppermute(block, ("section", "seq", "rep"), route)

    next_far = moved(far, 0, 0, 2)
    next_chip = moved(chip, 0, 0, 1)
    squares = lax.psum(squares_of(chip, far, next_far, next_chip), "rep")
    weights, time_bias, station_bias = pl.pallas_call(
        lambda *refs: fixed_kernel(*refs, stations=stations, total_steps=steps * seq_count),
        in_specs=[HBM] * 3 + [VMEM],
        out_specs=[VMEM] * 3,
        out_shape=[
            jax.ShapeDtypeStruct(head_proj.shape, bf16),
            jax.ShapeDtypeStruct((micro, reach, GROUP * own), f32),
            jax.ShapeDtypeStruct((micro, own, GROUP * own), f32),
        ],
        scratch_shapes=[
            pltpu.SMEM(record_start.shape, jnp.int32),
            pltpu.SMEM(record_pad.shape, jnp.int32),
            pltpu.SemaphoreType.DMA((2 + WEIGHT_PARTS,)),
        ],
        compiler_params=PARAMS,
        cost_estimate=cost(signal.size, 2 * head_proj.size),
        name="fixed",
    )(in_hbm(head_proj), in_hbm(record_start), in_hbm(record_pad), chip)
    inputs = (next_far, next_chip)
    kept = (chip, far)
    for tick in range(section_count):
        last = tick + 1 == section_count

        def kernel(*refs, tick=tick, last=last):
            layer_kernel(*refs, tick=tick, stations=stations, last=last)

        out_shape = (
            [jax.ShapeDtypeStruct((1,) + signal.shape, bf16)]
            if last
            else [half_shape, half_shape]
        )
        outputs = pl.pallas_call(
            kernel,
            in_specs=[VMEM] * (8 + len(inputs)),
            out_specs=[VMEM] * len(out_shape),
            out_shape=out_shape,
            scratch_shapes=[
                pltpu.VMEM(shape.shape, bf16)
                for shape, count in zip((half_shape, projected_shape), (4, 4) if tick == 0 else (2, 3))
                for _ in range(count)
            ],
            compiler_params=PARAMS,
            cost_estimate=cost(8 * signal.size * 3 * HEAD, 16 * signal_bytes),
            name="layer",
        )(
            chip, far, squares, time_bias, station_bias, weights, *kept, *inputs,
        )
        if last:
            return outputs[0]
        kept = outputs
        mine = squares_of(*kept)
        chip = moved(kept[0], tick, tick + 1, 0)
        next_far = moved(kept[1], tick, tick + 1, 2)
        squares = moved(mine, tick, tick + 1, 0, other=True)
        (mine_again,) = again(mine)
        far = moved(kept[1], tick, tick + 1, 0)
        far_squares = moved(mine_again, tick, tick + 1, 2, other=True)
        normed_chip = normed(chip, squares, CHIP)
        next_chip = moved(normed_chip, tick + 1, tick + 1, 1)
        far_squares = pl.pallas_call(
            add_kernel,
            in_specs=[VMEM] * 2,
            out_specs=VMEM,
            out_shape=squares_shape,
            compiler_params=PARAMS,
            cost_estimate=BUSY,
            name="add",
        )(squares_of(next_far), far_squares)
        inputs = (next_far, far_squares, next_chip, *project(normed_chip))


def solution(mesh):
    return jax.shard_map(
        body,
        mesh=mesh,
        in_specs=(P(None, "seq", None, "rep"), P("section", "rep", None, None), P(), P()),
        out_specs=P("section", None, "seq", None, "rep"),
        check_vma=False,
    )
```

```python
import math

import jax
import jax.numpy as jnp
from jax import lax
from jax.experimental import pallas as pl
from jax.experimental.pallas import tpu as pltpu
from jax.sharding import PartitionSpec as P

HEADS = 32
HEAD = 128
WIN = 4
GROUP = 4
EPS = 1e-06
BIG = 1e30
CHIP, FAR, NEXT_FAR, NEXT_CHIP = range(4)

HBM = pl.BlockSpec(memory_space=pltpu.HBM)
VMEM = pl.BlockSpec(memory_space=pltpu.VMEM)
BUSY = pl.CostEstimate(flops=2000000000, bytes_accessed=300000, transcendentals=0)
PARAMS = pltpu.CompilerParams(vmem_limit_bytes=16 * 1024 * 1024)


def cost(flops, moved):
    return pl.CostEstimate(flops=flops, bytes_accessed=moved, transcendentals=0)


def odd_device():
    return lax.axis_index("seq") % 2


def first_step(half):
    odd = odd_device()
    return {
        CHIP: WIN * (1 - odd),
        FAR: WIN * odd,
        NEXT_CHIP: 2 * WIN * (1 - odd) - WIN * odd,
        NEXT_FAR: 2 * WIN * odd - WIN * (1 - odd),
    }[half]


def same(count):
    return lax.broadcasted_iota(jnp.int32, (count, count), 0) == lax.broadcasted_iota(
        jnp.int32, (count, count), 1
    )


def squares_row(rows):
    gram = lax.dot_general(
        rows, rows, (((1,), (1,)), ((), ())), preferred_element_type=jnp.float32
    )
    return jnp.sum(jnp.where(same(rows.shape[0]), gram, 0.0), axis=0, keepdims=True)


def mask_parts(stations):
    own = 2 * WIN * stations
    keys, columns = 2 * own, GROUP * own
    key = lax.broadcasted_iota(jnp.int32, (keys, columns), 0)
    query = lax.broadcasted_iota(jnp.int32, (keys, columns), 1) % own

    def time_of(row):
        half, step = row // (WIN * stations), (row // stations) % WIN
        start = jnp.where(half == CHIP, first_step(CHIP), first_step(FAR))
        start = jnp.where(half == NEXT_CHIP, first_step(NEXT_CHIP), start)
        return step + jnp.where(half == NEXT_FAR, first_step(NEXT_FAR), start)

    key_station, query_station = key % stations, query % stations
    key_time, query_time = time_of(key), time_of(query)
    same_station = key_station == query_station
    same_time = key_time == query_time
    near = jnp.abs(key_time - query_time) <= WIN
    step = lax.axis_index("seq") * (2 * WIN) + key_time
    return step, key_station, same_station & near, same_time, same_station & same_time


def fill_masks(parts, first_ref, pad_ref, time_ref, station_ref, total_steps):
    step, key_station, near, same_time, itself = parts
    for m in range(time_ref.shape[0]):
        first = jnp.zeros(step.shape, jnp.int32)
        end = jnp.zeros(step.shape, jnp.int32)
        for s in range(first_ref.shape[1]):
            first = jnp.where(key_station == s, first_ref[m, s], first)
            end = jnp.where(key_station == s, total_steps - pad_ref[m, s], end)
        recorded = (step >= first) & (step < end)
        time_ref[m] = jnp.where((near & recorded) | itself, 0.0, -BIG)
        station_ref[m] = jnp.where((same_time & recorded) | itself, 0.0, -BIG)[
            : station_ref.shape[1]
        ]


def weights_part(weights_hbm, weights_ref, part, arrived):
    count = weights_hbm.shape[1] // 2
    heads = pl.ds(part * count, count)
    return pltpu.make_async_copy(weights_hbm.at[:, heads], weights_ref.at[:, heads], arrived)


def halves_kernel(signal_hbm, weights_hbm, chip_ref, far_ref, weights_ref, signal_ref, arrived):
    copy = pltpu.make_async_copy(signal_hbm, signal_ref, arrived.at[0])
    copy.start()
    weights_copy = weights_part(weights_hbm, weights_ref, 0, arrived.at[1])
    weights_copy.start()
    micro, _, stations, _ = signal_ref.shape
    edge = WIN * stations
    copy.wait()
    for half, half_ref in ((FAR, far_ref), (CHIP, chip_ref)):
        start = first_step(half)
        for m in range(micro):
            for t in range(0, WIN, 2):
                pair = [signal_ref[m, start + t + i].astype(jnp.float32) for i in range(2)]
                at = m * edge + t * stations
                half_ref[at : at + 2 * stations, :] = jnp.concatenate(pair, axis=0).astype(
                    jnp.bfloat16
                )
    weights_copy.wait()


def fixed_kernel(
    weights_hbm, first_hbm, pad_hbm, _, __, weights_ref, time_ref, station_ref,
    first_ref, pad_ref, arrived, *, stations, total_steps,
):
    copies = [
        pltpu.make_async_copy(first_hbm, first_ref, arrived.at[0]),
        pltpu.make_async_copy(pad_hbm, pad_ref, arrived.at[1]),
        weights_part(weights_hbm, weights_ref, 1, arrived.at[2]),
    ]
    for copy in copies:
        copy.start()
    parts = mask_parts(stations)
    copies[0].wait()
    copies[1].wait()
    fill_masks(parts, first_ref, pad_ref, time_ref, station_ref, total_steps)
    copies[2].wait()


def squares_kernel(*refs):
    out_ref = refs[-1]
    out_ref[...] = jnp.zeros(out_ref.shape, jnp.float32)
    for half, half_ref in enumerate(refs[:-1]):
        out_ref[half : half + 1, 0 : half_ref.shape[0]] = squares_row(half_ref[...])


def scaled(rows, total):
    count = rows.shape[0]
    factor = lax.rsqrt(total / (HEADS * HEAD) + EPS)
    column = jnp.sum(jnp.where(same(count), factor, 0.0), axis=1, keepdims=True)
    return (rows.astype(jnp.float32) * column).astype(jnp.bfloat16)


def norm_kernel(half_ref, mine_ref, squares_ref, normed_ref, *, line):
    rows = half_ref[...]
    count = rows.shape[0]
    normed_ref[...] = scaled(rows, mine_ref[0:1, 0:count] + squares_ref[line : line + 1, 0:count])


def copy_kernel(*refs):
    count = len(refs) // 2
    for source, target in zip(refs[:count], refs[count:]):
        target[...] = source[...]


def add_kernel(mine_ref, other_ref, out_ref):
    out_ref[...] = jnp.zeros(out_ref.shape, jnp.float32)
    out_ref[0:1, :] = mine_ref[0:1, :] + other_ref[FAR : FAR + 1, :]


def project_kernel(weights_ref, *refs):
    count = len(refs) // 2
    halves, outs = refs[:count], refs[count:]
    rows = halves[0].shape[0]
    width = 3 * HEAD
    for head in range(weights_ref.shape[1]):
        lanes = slice(head * HEAD, (head + 1) * HEAD)
        projected = jnp.dot(
            jnp.concatenate([half[:, lanes] for half in halves], axis=0),
            weights_ref[0, head],
            preferred_element_type=jnp.float32,
        ).astype(jnp.bfloat16)
        for i, out in enumerate(outs):
            out[:, head * width : (head + 1) * width] = projected[i * rows : (i + 1) * rows]


def softmax_columns(scores):
    grown = jnp.exp(scores - jnp.max(scores, axis=0, keepdims=True))
    return (grown * (1.0 / jnp.sum(grown, axis=0, keepdims=True))).astype(jnp.bfloat16)


def layer_kernel(
    chip_ref, far_ref, squares_ref, time_ref, station_ref, weights_ref, kept_chip_ref, kept_far_ref,
    *refs, tick, stations, last,
):
    edge = WIN * stations
    micro = chip_ref.shape[0] // edge
    own = 2 * edge
    heads_dev = weights_ref.shape[1]
    width = 3 * HEAD
    bf16, f32 = jnp.bfloat16, jnp.float32
    active = lax.axis_index("section") == tick
    projected = [None] * 4
    if tick == 0:
        next_far_ref, next_chip_ref, *refs = refs
        late = [
            (half, half_ref, squares_ref[half : half + 1, :], True)
            for half, half_ref in enumerate((chip_ref, far_ref, next_far_ref, next_chip_ref))
        ]
    else:
        next_far_ref, far_squares_ref, next_chip_ref, projected[CHIP], *refs = refs
        late = [
            (FAR, far_ref, squares_ref[FAR : FAR + 1, :], False),
            (NEXT_FAR, next_far_ref, far_squares_ref[0:1, :], True),
        ]
    outs, refs = (refs[:1], refs[1:]) if last else (refs[:2], refs[2:])
    normed, refs = refs[: len(late)], refs[len(late) :]
    projecting = [half for half, *_ in late]
    if tick > 0:
        projecting.append(NEXT_CHIP)
    for half, half_ref in zip(projecting, refs):
        projected[half] = half_ref

    def write(m, lanes, values):
        for half in (CHIP, FAR):
            part = values[half * edge : (half + 1) * edge].astype(bf16)
            if last:
                for t in range(WIN):
                    outs[0][0, m, first_step(half) + t, :, lanes] = part[
                        t * stations : (t + 1) * stations
                    ]
            else:
                outs[half][m * edge : (m + 1) * edge, lanes] = part

    def rows_of(halves, m, at):
        return [projected[half][m * edge : (m + 1) * edge, at : at + HEAD] for half in halves]

    @pl.when(active)
    def _():
        lane = lax.broadcasted_iota(jnp.int32, (micro * edge, 128), 1)
        row = lax.broadcasted_iota(jnp.int32, (micro * edge, 128), 0)
        for (_, half_ref, line, complete), normed_ref in zip(late, normed):
            total = jnp.where(lane == row, line, 0.0)
            if not complete:
                for head in range(heads_dev):
                    part = half_ref[:, head * HEAD : (head + 1) * HEAD].astype(f32)
                    total = total + part * part
            factor = lax.rsqrt(jnp.sum(total, axis=1, keepdims=True) / (HEADS * HEAD) + EPS)
            normed_ref[...] = (half_ref[...].astype(f32) * factor).astype(bf16)
        if tick > 0:
            normed.append(next_chip_ref)
        project_kernel(weights_ref, *normed, *[projected[half] for half in projecting])
        pairs = [(g, m) for g in range(heads_dev // GROUP) for m in range(micro)]
        blank = jnp.zeros((own, HEAD), bf16)
        scores = []
        for g, m in pairs:
            at = [(g * GROUP + j) * width for j in range(GROUP)]
            queries = [jnp.concatenate(rows_of((CHIP, FAR), m, a), axis=0) for a in at]
            spread = jnp.concatenate(
                [
                    jnp.concatenate(
                        [queries[j] if i == j else blank for i in range(GROUP)],
                        axis=1,
                    )
                    for j in range(GROUP)
                ],
                axis=0,
            )
            keys = jnp.concatenate(
                [jnp.concatenate(rows_of(range(4), m, a + HEAD), axis=0) for a in at], axis=1
            )
            scores.append(
                lax.dot_general(
                    keys, spread, (((1,), (1,)), ((), ())), preferred_element_type=f32
                )
                * (1.0 / math.sqrt(HEAD))
            )
        mixes = []
        for (g, m), score in zip(pairs, scores):
            time_weights = softmax_columns(score + time_ref[m])
            station_weights = softmax_columns(score[:own] + station_ref[m])
            mixes.append(jnp.concatenate([time_weights, station_weights], axis=0).T)
        for (g, m), mix in zip(pairs, mixes):
            for j in range(GROUP):
                head = g * GROUP + j
                at = head * width + 2 * HEAD
                mixed = jnp.dot(
                    mix[j * own : (j + 1) * own],
                    jnp.concatenate(rows_of((0, 1, 2, 3, CHIP, FAR), m, at), axis=0),
                    preferred_element_type=f32,
                )
                lanes = slice(head * HEAD, (head + 1) * HEAD)
                hidden = jnp.concatenate(
                    [ref[m * edge : (m + 1) * edge, lanes] for ref in (chip_ref, far_ref)], axis=0
                )
                result = hidden.astype(f32) + mixed
                write(m, lanes, result)

    @pl.when(jnp.logical_not(active))
    def _():
        for m in range(micro):
            for head in range(heads_dev):
                lanes = slice(head * HEAD, (head + 1) * HEAD)
                kept = [
                    ref[m * edge : (m + 1) * edge, lanes] for ref in (kept_chip_ref, kept_far_ref)
                ]
                write(m, lanes, jnp.concatenate(kept, axis=0).astype(f32))


def body(signal, head_proj, record_start, record_pad):
    section_count = lax.axis_size("section")
    seq_count = lax.axis_size("seq")
    rep_count = lax.axis_size("rep")
    micro, steps, stations, features = signal.shape
    heads_dev = head_proj.shape[1]
    edge = WIN * stations
    own, reach = 2 * edge, 4 * edge
    bf16, f32 = jnp.bfloat16, jnp.float32
    half_shape = jax.ShapeDtypeStruct((micro * edge, features), bf16)
    squares_shape = jax.ShapeDtypeStruct((8, 128), f32)
    projected_shape = jax.ShapeDtypeStruct((micro * edge, heads_dev * 3 * HEAD), bf16)
    signal_bytes = signal.size * 2

    def in_hbm(block):
        return pltpu.with_memory_space_constraint(block, pltpu.HBM)

    def squares_of(*halves):
        return pl.pallas_call(
            squares_kernel,
            in_specs=[VMEM] * len(halves),
            out_specs=VMEM,
            out_shape=squares_shape,
            compiler_params=PARAMS,
            name="squares",
        )(*halves)

    def normed(rows, squares, line):
        return pl.pallas_call(
            lambda *refs: norm_kernel(*refs, line=line),
            in_specs=[VMEM] * 3,
            out_specs=VMEM,
            out_shape=half_shape,
            compiler_params=PARAMS,
            cost_estimate=BUSY,
            name="norm",
        )(rows, squares_of(rows), squares)

    def again(*blocks):
        return pl.pallas_call(
            copy_kernel,
            in_specs=[VMEM] * len(blocks),
            out_specs=[VMEM] * len(blocks),
            out_shape=[jax.ShapeDtypeStruct(block.shape, block.dtype) for block in blocks],
            compiler_params=PARAMS,
            cost_estimate=BUSY,
            name="copy",
        )(*blocks)

    def project(*halves):
        return pl.pallas_call(
            project_kernel,
            in_specs=[VMEM] * (1 + len(halves)),
            out_specs=[VMEM] * len(halves),
            out_shape=[projected_shape] * len(halves),
            compiler_params=PARAMS,
            cost_estimate=BUSY,
            name="project",
        )(weights, *halves)

    chip, far, weights = pl.pallas_call(
        halves_kernel,
        in_specs=[HBM] * 2,
        out_specs=[VMEM] * 3,
        out_shape=[half_shape, half_shape, jax.ShapeDtypeStruct(head_proj.shape, bf16)],
        scratch_shapes=[pltpu.VMEM(signal.shape, bf16), pltpu.SemaphoreType.DMA((2,))],
        compiler_params=PARAMS,
        cost_estimate=cost(signal.size, 2 * signal_bytes),
        name="halves",
    )(in_hbm(signal), in_hbm(head_proj))
    def moved(block, source, target, hop, other=False):
        route = []
        for i in range(seq_count):
            to = i if hop == 0 else i + 1 - 2 * (i % 2) if hop == 1 else i - 1 + 2 * (i % 2)
            if 0 <= to < seq_count:
                for r in range(rep_count):
                    route.append(
                        (
                            (source * seq_count + i) * rep_count + r,
                            (target * seq_count + to) * rep_count
                            + ((r + 1) % rep_count if other else r),
                        )
                    )
        return lax.ppermute(block, ("section", "seq", "rep"), route)

    next_far = moved(far, 0, 0, 2)
    next_chip = moved(chip, 0, 0, 1)
    squares = lax.psum(squares_of(chip, far, next_far, next_chip), "rep")
    weights, time_bias, station_bias = pl.pallas_call(
        lambda *refs: fixed_kernel(*refs, stations=stations, total_steps=steps * seq_count),
        in_specs=[HBM] * 3 + [VMEM] * 2,
        input_output_aliases={4: 0},
        out_specs=[VMEM] * 3,
        out_shape=[
            jax.ShapeDtypeStruct(head_proj.shape, bf16),
            jax.ShapeDtypeStruct((micro, reach, GROUP * own), f32),
            jax.ShapeDtypeStruct((micro, own, GROUP * own), f32),
        ],
        scratch_shapes=[
            pltpu.SMEM(record_start.shape, jnp.int32),
            pltpu.SMEM(record_pad.shape, jnp.int32),
            pltpu.SemaphoreType.DMA((3,)),
        ],
        compiler_params=PARAMS,
        cost_estimate=cost(signal.size, 2 * head_proj.size),
        name="fixed",
    )(in_hbm(head_proj), in_hbm(record_start), in_hbm(record_pad), chip, weights)
    inputs = (next_far, next_chip)
    kept = (chip, far)
    for tick in range(section_count):
        last = tick + 1 == section_count

        def kernel(*refs, tick=tick, last=last):
            layer_kernel(*refs, tick=tick, stations=stations, last=last)

        out_shape = (
            [jax.ShapeDtypeStruct((1,) + signal.shape, bf16)]
            if last
            else [half_shape, half_shape]
        )
        outputs = pl.pallas_call(
            kernel,
            in_specs=[VMEM] * (8 + len(inputs)),
            out_specs=[VMEM] * len(out_shape),
            out_shape=out_shape,
            scratch_shapes=[
                pltpu.VMEM(shape.shape, bf16)
                for shape, count in zip((half_shape, projected_shape), (4, 4) if tick == 0 else (2, 3))
                for _ in range(count)
            ],
            compiler_params=PARAMS,
            cost_estimate=cost(8 * signal.size * 3 * HEAD, 16 * signal_bytes),
            name="layer",
        )(
            chip, far, squares, time_bias, station_bias, weights, *kept, *inputs,
        )
        if last:
            return outputs[0]
        kept = outputs
        mine = squares_of(*kept)
        chip = moved(kept[0], tick, tick + 1, 0)
        next_far = moved(kept[1], tick, tick + 1, 2)
        squares = moved(mine, tick, tick + 1, 0, other=True)
        (mine_again,) = again(mine)
        far = moved(kept[1], tick, tick + 1, 0)
        far_squares = moved(mine_again, tick, tick + 1, 2, other=True)
        normed_chip = normed(chip, squares, CHIP)
        next_chip = moved(normed_chip, tick + 1, tick + 1, 1)
        far_squares = pl.pallas_call(
            add_kernel,
            in_specs=[VMEM] * 2,
            out_specs=VMEM,
            out_shape=squares_shape,
            compiler_params=PARAMS,
            cost_estimate=BUSY,
            name="add",
        )(squares_of(next_far), far_squares)
        inputs = (next_far, far_squares, next_chip, *project(normed_chip))


def solution(mesh):
    return jax.shard_map(
        body,
        mesh=mesh,
        in_specs=(P(None, "seq", None, "rep"), P("section", "rep", None, None), P(), P()),
        out_specs=P("section", None, "seq", None, "rep"),
        check_vma=False,
    )
```

```python
import math

import jax
import jax.numpy as jnp
from jax import lax
from jax.experimental import pallas as pl
from jax.experimental.pallas import tpu as pltpu
from jax.sharding import PartitionSpec as P

HEADS = 32
HEAD = 128
WIN = 4
GROUP = 4
EPS = 1e-06
BIG = 1e30
CHIP, FAR, NEXT_FAR, NEXT_CHIP = range(4)

HBM = pl.BlockSpec(memory_space=pltpu.HBM)
VMEM = pl.BlockSpec(memory_space=pltpu.VMEM)
BUSY = pl.CostEstimate(flops=2000000000, bytes_accessed=300000, transcendentals=0)
PARAMS = pltpu.CompilerParams(vmem_limit_bytes=16 * 1024 * 1024)


def cost(flops, moved):
    return pl.CostEstimate(flops=flops, bytes_accessed=moved, transcendentals=0)


def odd_device():
    return lax.axis_index("seq") % 2


def first_step(half):
    odd = odd_device()
    return {
        CHIP: WIN * (1 - odd),
        FAR: WIN * odd,
        NEXT_CHIP: 2 * WIN * (1 - odd) - WIN * odd,
        NEXT_FAR: 2 * WIN * odd - WIN * (1 - odd),
    }[half]


def same(count):
    return lax.broadcasted_iota(jnp.int32, (count, count), 0) == lax.broadcasted_iota(
        jnp.int32, (count, count), 1
    )


def squares_row(rows):
    gram = lax.dot_general(
        rows, rows, (((1,), (1,)), ((), ())), preferred_element_type=jnp.float32
    )
    return jnp.sum(jnp.where(same(rows.shape[0]), gram, 0.0), axis=0, keepdims=True)


def fill_masks(first_ref, pad_ref, time_ref, station_ref, stations, total_steps):
    own = 2 * WIN * stations
    keys, columns = 2 * own, GROUP * own
    key = lax.broadcasted_iota(jnp.int32, (keys, columns), 0)
    query = lax.broadcasted_iota(jnp.int32, (keys, columns), 1) % own

    def time_of(row):
        half, step = row // (WIN * stations), (row // stations) % WIN
        start = jnp.where(half == CHIP, first_step(CHIP), first_step(FAR))
        start = jnp.where(half == NEXT_CHIP, first_step(NEXT_CHIP), start)
        return step + jnp.where(half == NEXT_FAR, first_step(NEXT_FAR), start)

    key_station, query_station = key % stations, query % stations
    key_time, query_time = time_of(key), time_of(query)
    same_station = key_station == query_station
    same_time = key_time == query_time
    near = jnp.abs(key_time - query_time) <= WIN
    step = lax.axis_index("seq") * (2 * WIN) + key_time
    for m in range(time_ref.shape[0]):
        first = jnp.zeros((keys, columns), jnp.int32)
        pad = jnp.zeros((keys, columns), jnp.int32)
        for s in range(stations):
            first = jnp.where(key_station == s, first_ref[m, s], first)
            pad = jnp.where(key_station == s, pad_ref[m, s], pad)
        recorded = (step >= first) & (step < total_steps - pad)
        time_ref[m] = jnp.where(same_station & near & (recorded | same_time), 0.0, -BIG)
        station_ref[m] = jnp.where(same_time & (recorded | same_station), 0.0, -BIG)[:own]


def halves_kernel(signal_hbm, chip_ref, far_ref, signal_ref, arrived):
    copy = pltpu.make_async_copy(signal_hbm, signal_ref, arrived)
    copy.start()
    micro, _, stations, _ = signal_ref.shape
    edge = WIN * stations
    copy.wait()
    for half, half_ref in ((FAR, far_ref), (CHIP, chip_ref)):
        start = first_step(half)
        for m in range(micro):
            for t in range(0, WIN, 2):
                pair = [signal_ref[m, start + t + i].astype(jnp.float32) for i in range(2)]
                at = m * edge + t * stations
                half_ref[at : at + 2 * stations, :] = jnp.concatenate(pair, axis=0).astype(
                    jnp.bfloat16
                )


def fixed_kernel(
    weights_hbm, first_hbm, pad_hbm, _, weights_ref, time_ref, station_ref,
    first_ref, pad_ref, arrived, *, stations, total_steps,
):
    copies = [
        pltpu.make_async_copy(first_hbm, first_ref, arrived.at[0]),
        pltpu.make_async_copy(pad_hbm, pad_ref, arrived.at[1]),
        pltpu.make_async_copy(weights_hbm, weights_ref, arrived.at[2]),
    ]
    for copy in copies:
        copy.start()
    copies[0].wait()
    copies[1].wait()
    fill_masks(first_ref, pad_ref, time_ref, station_ref, stations, total_steps)
    copies[2].wait()


def squares_kernel(*refs):
    out_ref = refs[-1]
    out_ref[...] = jnp.zeros(out_ref.shape, jnp.float32)
    for half, half_ref in enumerate(refs[:-1]):
        out_ref[half : half + 1, 0 : half_ref.shape[0]] = squares_row(half_ref[...])


def scaled(rows, total):
    count = rows.shape[0]
    factor = lax.rsqrt(total / (HEADS * HEAD) + EPS)
    column = jnp.sum(jnp.where(same(count), factor, 0.0), axis=1, keepdims=True)
    return (rows.astype(jnp.float32) * column).astype(jnp.bfloat16)


def norm_kernel(half_ref, mine_ref, squares_ref, normed_ref, *, line):
    rows = half_ref[...]
    count = rows.shape[0]
    normed_ref[...] = scaled(rows, mine_ref[0:1, 0:count] + squares_ref[line : line + 1, 0:count])


def copy_kernel(*refs):
    count = len(refs) // 2
    for source, target in zip(refs[:count], refs[count:]):
        target[...] = source[...]


def add_kernel(mine_ref, other_ref, out_ref):
    out_ref[...] = jnp.zeros(out_ref.shape, jnp.float32)
    out_ref[0:1, :] = mine_ref[0:1, :] + other_ref[FAR : FAR + 1, :]


def project_kernel(weights_ref, *refs):
    count = len(refs) // 2
    halves, outs = refs[:count], refs[count:]
    rows = halves[0].shape[0]
    width = 3 * HEAD
    for head in range(weights_ref.shape[1]):
        lanes = slice(head * HEAD, (head + 1) * HEAD)
        projected = jnp.dot(
            jnp.concatenate([half[:, lanes] for half in halves], axis=0),
            weights_ref[0, head],
            preferred_element_type=jnp.float32,
        ).astype(jnp.bfloat16)
        for i, out in enumerate(outs):
            out[:, head * width : (head + 1) * width] = projected[i * rows : (i + 1) * rows]


def softmax_columns(scores):
    grown = jnp.exp(scores - jnp.max(scores, axis=0, keepdims=True))
    return (grown * (1.0 / jnp.sum(grown, axis=0, keepdims=True))).astype(jnp.bfloat16)


def layer_kernel(
    chip_ref, far_ref, squares_ref, time_ref, station_ref, weights_ref, kept_chip_ref, kept_far_ref,
    *refs, tick, stations, last,
):
    edge = WIN * stations
    micro = chip_ref.shape[0] // edge
    own = 2 * edge
    heads_dev = weights_ref.shape[1]
    width = 3 * HEAD
    bf16, f32 = jnp.bfloat16, jnp.float32
    active = lax.axis_index("section") == tick
    projected = [None] * 4
    if tick == 0:
        next_far_ref, next_chip_ref, *refs = refs
        late = [
            (
                half,
                half_ref,
                sum(squares_ref[i + half : i + half + 1, :] for i in range(0, squares_ref.shape[0], 8)),
                True,
            )
            for half, half_ref in enumerate((chip_ref, far_ref, next_far_ref, next_chip_ref))
        ]
    else:
        next_far_ref, far_squares_ref, next_chip_ref, projected[CHIP], *refs = refs
        late = [
            (FAR, far_ref, squares_ref[FAR : FAR + 1, :], False),
            (NEXT_FAR, next_far_ref, far_squares_ref[0:1, :], True),
        ]
    outs, refs = (refs[:1], refs[1:]) if last else (refs[:2], refs[2:])
    normed, refs = refs[: len(late)], refs[len(late) :]
    projecting = [half for half, *_ in late]
    if tick > 0:
        projecting.append(NEXT_CHIP)
    for half, half_ref in zip(projecting, refs):
        projected[half] = half_ref

    def write(m, lanes, values):
        for half in (CHIP, FAR):
            part = values[half * edge : (half + 1) * edge].astype(bf16)
            if last:
                for t in range(WIN):
                    outs[0][0, m, first_step(half) + t, :, lanes] = part[
                        t * stations : (t + 1) * stations
                    ]
            else:
                outs[half][m * edge : (m + 1) * edge, lanes] = part

    def rows_of(halves, m, at):
        return [projected[half][m * edge : (m + 1) * edge, at : at + HEAD] for half in halves]

    @pl.when(active)
    def _():
        lane = lax.broadcasted_iota(jnp.int32, (micro * edge, 128), 1)
        row = lax.broadcasted_iota(jnp.int32, (micro * edge, 128), 0)
        for (_, half_ref, line, complete), normed_ref in zip(late, normed):
            total = jnp.where(lane == row, line, 0.0)
            if not complete:
                for head in range(heads_dev):
                    part = half_ref[:, head * HEAD : (head + 1) * HEAD].astype(f32)
                    total = total + part * part
            factor = lax.rsqrt(jnp.sum(total, axis=1, keepdims=True) / (HEADS * HEAD) + EPS)
            normed_ref[...] = (half_ref[...].astype(f32) * factor).astype(bf16)
        if tick > 0:
            normed.append(next_chip_ref)
        project_kernel(weights_ref, *normed, *[projected[half] for half in projecting])
        pairs = [(g, m) for g in range(heads_dev // GROUP) for m in range(micro)]
        blank = jnp.zeros((own, HEAD), bf16)
        scores = []
        for g, m in pairs:
            at = [(g * GROUP + j) * width for j in range(GROUP)]
            queries = [jnp.concatenate(rows_of((CHIP, FAR), m, a), axis=0) for a in at]
            spread = jnp.concatenate(
                [
                    jnp.concatenate(
                        [queries[j] if i == j else blank for i in range(GROUP)],
                        axis=1,
                    )
                    for j in range(GROUP)
                ],
                axis=0,
            )
            keys = jnp.concatenate(
                [jnp.concatenate(rows_of(range(4), m, a + HEAD), axis=0) for a in at], axis=1
            )
            scores.append(
                lax.dot_general(
                    keys, spread, (((1,), (1,)), ((), ())), preferred_element_type=f32
                )
                * (1.0 / math.sqrt(HEAD))
            )
        mixes = []
        for (g, m), score in zip(pairs, scores):
            time_weights = softmax_columns(score + time_ref[m])
            station_weights = softmax_columns(score[:own] + station_ref[m])
            mixes.append(jnp.concatenate([time_weights, station_weights], axis=0).T)
        for (g, m), mix in zip(pairs, mixes):
            for j in range(GROUP):
                head = g * GROUP + j
                at = head * width + 2 * HEAD
                mixed = jnp.dot(
                    mix[j * own : (j + 1) * own],
                    jnp.concatenate(rows_of((0, 1, 2, 3, CHIP, FAR), m, at), axis=0),
                    preferred_element_type=f32,
                )
                lanes = slice(head * HEAD, (head + 1) * HEAD)
                hidden = jnp.concatenate(
                    [ref[m * edge : (m + 1) * edge, lanes] for ref in (chip_ref, far_ref)], axis=0
                )
                result = hidden.astype(f32) + mixed
                write(m, lanes, result)

    @pl.when(jnp.logical_not(active))
    def _():
        for m in range(micro):
            for head in range(heads_dev):
                lanes = slice(head * HEAD, (head + 1) * HEAD)
                kept = [
                    ref[m * edge : (m + 1) * edge, lanes] for ref in (kept_chip_ref, kept_far_ref)
                ]
                write(m, lanes, jnp.concatenate(kept, axis=0).astype(f32))


def body(signal, head_proj, record_start, record_pad):
    section_count = lax.axis_size("section")
    seq_count = lax.axis_size("seq")
    rep_count = lax.axis_size("rep")
    micro, steps, stations, features = signal.shape
    heads_dev = head_proj.shape[1]
    edge = WIN * stations
    own, reach = 2 * edge, 4 * edge
    bf16, f32 = jnp.bfloat16, jnp.float32
    half_shape = jax.ShapeDtypeStruct((micro * edge, features), bf16)
    squares_shape = jax.ShapeDtypeStruct((8, 128), f32)
    projected_shape = jax.ShapeDtypeStruct((micro * edge, heads_dev * 3 * HEAD), bf16)
    signal_bytes = signal.size * 2

    def in_hbm(block):
        return pltpu.with_memory_space_constraint(block, pltpu.HBM)

    def squares_of(*halves):
        return pl.pallas_call(
            squares_kernel,
            in_specs=[VMEM] * len(halves),
            out_specs=VMEM,
            out_shape=squares_shape,
            compiler_params=PARAMS,
            name="squares",
        )(*halves)

    def normed(rows, squares, line):
        return pl.pallas_call(
            lambda *refs: norm_kernel(*refs, line=line),
            in_specs=[VMEM] * 3,
            out_specs=VMEM,
            out_shape=half_shape,
            compiler_params=PARAMS,
            cost_estimate=BUSY,
            name="norm",
        )(rows, squares_of(rows), squares)

    def again(*blocks):
        return pl.pallas_call(
            copy_kernel,
            in_specs=[VMEM] * len(blocks),
            out_specs=[VMEM] * len(blocks),
            out_shape=[jax.ShapeDtypeStruct(block.shape, block.dtype) for block in blocks],
            compiler_params=PARAMS,
            cost_estimate=BUSY,
            name="copy",
        )(*blocks)

    def project(*halves):
        return pl.pallas_call(
            project_kernel,
            in_specs=[VMEM] * (1 + len(halves)),
            out_specs=[VMEM] * len(halves),
            out_shape=[projected_shape] * len(halves),
            compiler_params=PARAMS,
            cost_estimate=BUSY,
            name="project",
        )(weights, *halves)

    chip, far = pl.pallas_call(
        halves_kernel,
        in_specs=[HBM],
        out_specs=[VMEM] * 2,
        out_shape=[half_shape] * 2,
        scratch_shapes=[pltpu.VMEM(signal.shape, bf16), pltpu.SemaphoreType.DMA],
        compiler_params=PARAMS,
        cost_estimate=cost(signal.size, 2 * signal_bytes),
        name="halves",
    )(in_hbm(signal))
    def moved(block, source, target, hop, other=False):
        route = []
        for i in range(seq_count):
            to = i if hop == 0 else i + 1 - 2 * (i % 2) if hop == 1 else i - 1 + 2 * (i % 2)
            if 0 <= to < seq_count:
                for r in range(rep_count):
                    route.append(
                        (
                            (source * seq_count + i) * rep_count + r,
                            (target * seq_count + to) * rep_count
                            + ((r + 1) % rep_count if other else r),
                        )
                    )
        return lax.ppermute(block, ("section", "seq", "rep"), route)

    next_far = moved(far, 0, 0, 2)
    next_chip = moved(chip, 0, 0, 1)
    squares = lax.all_gather(squares_of(chip, far, next_far, next_chip), "rep", tiled=True)
    weights, time_bias, station_bias = pl.pallas_call(
        lambda *refs: fixed_kernel(*refs, stations=stations, total_steps=steps * seq_count),
        in_specs=[HBM] * 3 + [VMEM],
        out_specs=[VMEM] * 3,
        out_shape=[
            jax.ShapeDtypeStruct(head_proj.shape, bf16),
            jax.ShapeDtypeStruct((micro, reach, GROUP * own), f32),
            jax.ShapeDtypeStruct((micro, own, GROUP * own), f32),
        ],
        scratch_shapes=[
            pltpu.SMEM(record_start.shape, jnp.int32),
            pltpu.SMEM(record_pad.shape, jnp.int32),
            pltpu.SemaphoreType.DMA((3,)),
        ],
        compiler_params=PARAMS,
        cost_estimate=cost(signal.size, 2 * head_proj.size),
        name="fixed",
    )(in_hbm(head_proj), in_hbm(record_start), in_hbm(record_pad), chip)
    inputs = (next_far, next_chip)
    kept = (chip, far)
    for tick in range(section_count):
        last = tick + 1 == section_count

        def kernel(*refs, tick=tick, last=last):
            layer_kernel(*refs, tick=tick, stations=stations, last=last)

        out_shape = (
            [jax.ShapeDtypeStruct((1,) + signal.shape, bf16)]
            if last
            else [half_shape, half_shape]
        )
        outputs = pl.pallas_call(
            kernel,
            in_specs=[VMEM] * (8 + len(inputs)),
            out_specs=[VMEM] * len(out_shape),
            out_shape=out_shape,
            scratch_shapes=[
                pltpu.VMEM(shape.shape, bf16)
                for shape, count in zip((half_shape, projected_shape), (4, 4) if tick == 0 else (2, 3))
                for _ in range(count)
            ],
            compiler_params=PARAMS,
            cost_estimate=cost(8 * signal.size * 3 * HEAD, 16 * signal_bytes),
            name="layer",
        )(
            chip, far, squares, time_bias, station_bias, weights, *kept, *inputs,
        )
        if last:
            return outputs[0]
        kept = outputs
        mine = squares_of(*kept)
        chip = moved(kept[0], tick, tick + 1, 0)
        next_far = moved(kept[1], tick, tick + 1, 2)
        squares = moved(mine, tick, tick + 1, 0, other=True)
        (mine_again,) = again(mine)
        far = moved(kept[1], tick, tick + 1, 0)
        far_squares = moved(mine_again, tick, tick + 1, 2, other=True)
        normed_chip = normed(chip, squares, CHIP)
        next_chip = moved(normed_chip, tick + 1, tick + 1, 1)
        far_squares = pl.pallas_call(
            add_kernel,
            in_specs=[VMEM] * 2,
            out_specs=VMEM,
            out_shape=squares_shape,
            compiler_params=PARAMS,
            cost_estimate=BUSY,
            name="add",
        )(squares_of(next_far), far_squares)
        inputs = (next_far, far_squares, next_chip, *project(normed_chip))


def solution(mesh):
    return jax.shard_map(
        body,
        mesh=mesh,
        in_specs=(P(None, "seq", None, "rep"), P("section", "rep", None, None), P(), P()),
        out_specs=P("section", None, "seq", None, "rep"),
        check_vma=False,
    )
```

```python
import math

import jax
import jax.numpy as jnp
from jax import lax
from jax.experimental import pallas as pl
from jax.experimental.pallas import tpu as pltpu
from jax.sharding import PartitionSpec as P

HEADS = 32
HEAD = 128
WIN = 4
GROUP = 4
EPS = 1e-06
BIG = 1e30
CHIP, FAR, NEXT_FAR, NEXT_CHIP = range(4)

HBM = pl.BlockSpec(memory_space=pltpu.HBM)
VMEM = pl.BlockSpec(memory_space=pltpu.VMEM)
BUSY = pl.CostEstimate(flops=2000000000, bytes_accessed=300000, transcendentals=0)
PARAMS = pltpu.CompilerParams(vmem_limit_bytes=16 * 1024 * 1024)


def cost(flops, moved):
    return pl.CostEstimate(flops=flops, bytes_accessed=moved, transcendentals=0)


def odd_device():
    return lax.axis_index("seq") % 2


def first_step(half):
    odd = odd_device()
    return {
        CHIP: WIN * (1 - odd),
        FAR: WIN * odd,
        NEXT_CHIP: 2 * WIN * (1 - odd) - WIN * odd,
        NEXT_FAR: 2 * WIN * odd - WIN * (1 - odd),
    }[half]


def same(count):
    return lax.broadcasted_iota(jnp.int32, (count, count), 0) == lax.broadcasted_iota(
        jnp.int32, (count, count), 1
    )


def squares_row(rows):
    gram = lax.dot_general(
        rows, rows, (((1,), (1,)), ((), ())), preferred_element_type=jnp.float32
    )
    return jnp.sum(jnp.where(same(rows.shape[0]), gram, 0.0), axis=0, keepdims=True)


def fill_masks(first_ref, pad_ref, time_ref, station_ref, stations, total_steps):
    own = 2 * WIN * stations
    keys, columns = 2 * own, GROUP * own
    key = lax.broadcasted_iota(jnp.int32, (keys, columns), 0)
    query = lax.broadcasted_iota(jnp.int32, (keys, columns), 1) % own

    def time_of(row):
        half, step = row // (WIN * stations), (row // stations) % WIN
        start = jnp.where(half == CHIP, first_step(CHIP), first_step(FAR))
        start = jnp.where(half == NEXT_CHIP, first_step(NEXT_CHIP), start)
        return step + jnp.where(half == NEXT_FAR, first_step(NEXT_FAR), start)

    key_station, query_station = key % stations, query % stations
    key_time, query_time = time_of(key), time_of(query)
    same_station = key_station == query_station
    same_time = key_time == query_time
    near = jnp.abs(key_time - query_time) <= WIN
    step = lax.axis_index("seq") * (2 * WIN) + key_time
    for m in range(time_ref.shape[0]):
        first = jnp.zeros((keys, columns), jnp.int32)
        pad = jnp.zeros((keys, columns), jnp.int32)
        for s in range(stations):
            first = jnp.where(key_station == s, first_ref[m, s], first)
            pad = jnp.where(key_station == s, pad_ref[m, s], pad)
        recorded = (step >= first) & (step < total_steps - pad)
        time_ref[m] = jnp.where(same_station & near & (recorded | same_time), 0.0, -BIG)
        station_ref[m] = jnp.where(same_time & (recorded | same_station), 0.0, -BIG)[:own]


def halves_kernel(signal_hbm, chip_ref, far_ref, signal_ref, arrived):
    copy = pltpu.make_async_copy(signal_hbm, signal_ref, arrived)
    copy.start()
    micro, _, stations, _ = signal_ref.shape
    edge = WIN * stations
    copy.wait()
    for half, half_ref in ((FAR, far_ref), (CHIP, chip_ref)):
        start = first_step(half)
        for m in range(micro):
            for t in range(0, WIN, 2):
                pair = [signal_ref[m, start + t + i].astype(jnp.float32) for i in range(2)]
                at = m * edge + t * stations
                half_ref[at : at + 2 * stations, :] = jnp.concatenate(pair, axis=0).astype(
                    jnp.bfloat16
                )


def fixed_kernel(
    weights_hbm, first_hbm, pad_hbm, _, weights_ref, time_ref, station_ref,
    first_ref, pad_ref, arrived, *, stations, total_steps,
):
    copies = [
        pltpu.make_async_copy(first_hbm, first_ref, arrived.at[0]),
        pltpu.make_async_copy(pad_hbm, pad_ref, arrived.at[1]),
        pltpu.make_async_copy(weights_hbm, weights_ref, arrived.at[2]),
    ]
    for copy in copies:
        copy.start()
    copies[0].wait()
    copies[1].wait()
    fill_masks(first_ref, pad_ref, time_ref, station_ref, stations, total_steps)
    copies[2].wait()


def squares_kernel(*refs):
    out_ref = refs[-1]
    out_ref[...] = jnp.zeros(out_ref.shape, jnp.float32)
    for half, half_ref in enumerate(refs[:-1]):
        out_ref[half : half + 1, 0 : half_ref.shape[0]] = squares_row(half_ref[...])


def scaled(rows, total):
    count = rows.shape[0]
    factor = lax.rsqrt(total / (HEADS * HEAD) + EPS)
    column = jnp.sum(jnp.where(same(count), factor, 0.0), axis=1, keepdims=True)
    return (rows.astype(jnp.float32) * column).astype(jnp.bfloat16)


def norm_kernel(half_ref, mine_ref, squares_ref, normed_ref, *, line):
    rows = half_ref[...]
    count = rows.shape[0]
    normed_ref[...] = scaled(rows, mine_ref[0:1, 0:count] + squares_ref[line : line + 1, 0:count])


def copy_kernel(*refs):
    count = len(refs) // 2
    for source, target in zip(refs[:count], refs[count:]):
        target[...] = source[...]


def add_kernel(mine_ref, other_ref, out_ref):
    out_ref[...] = jnp.zeros(out_ref.shape, jnp.float32)
    out_ref[0:1, :] = mine_ref[0:1, :] + other_ref[FAR : FAR + 1, :]


def project_kernel(weights_ref, *refs):
    count = len(refs) // 2
    halves, outs = refs[:count], refs[count:]
    rows = halves[0].shape[0]
    width = 3 * HEAD
    for head in range(weights_ref.shape[1]):
        lanes = slice(head * HEAD, (head + 1) * HEAD)
        projected = jnp.dot(
            jnp.concatenate([half[:, lanes] for half in halves], axis=0),
            weights_ref[0, head],
            preferred_element_type=jnp.float32,
        ).astype(jnp.bfloat16)
        for i, out in enumerate(outs):
            out[:, head * width : (head + 1) * width] = projected[i * rows : (i + 1) * rows]


def softmax_columns(scores):
    grown = jnp.exp(scores - jnp.max(scores, axis=0, keepdims=True))
    return (grown * (1.0 / jnp.sum(grown, axis=0, keepdims=True))).astype(jnp.bfloat16)


def layer_kernel(
    chip_ref, far_ref, squares_ref, time_ref, station_ref, weights_ref, kept_chip_ref, kept_far_ref,
    *refs, tick, stations, last,
):
    edge = WIN * stations
    micro = chip_ref.shape[0] // edge
    own = 2 * edge
    heads_dev = weights_ref.shape[1]
    width = 3 * HEAD
    bf16, f32 = jnp.bfloat16, jnp.float32
    active = lax.axis_index("section") == tick
    projected = [None] * 4
    if tick == 0:
        next_far_ref, next_chip_ref, *refs = refs
        late = [
            (
                half,
                half_ref,
                sum(squares_ref[i + half : i + half + 1, :] for i in range(0, squares_ref.shape[0], 8)),
                True,
            )
            for half, half_ref in enumerate((chip_ref, far_ref, next_far_ref, next_chip_ref))
        ]
    else:
        next_far_ref, far_squares_ref, next_chip_ref, projected[CHIP], *refs = refs
        late = [
            (FAR, far_ref, squares_ref[FAR : FAR + 1, :], False),
            (NEXT_FAR, next_far_ref, far_squares_ref[0:1, :], True),
        ]
    outs, refs = (refs[:1], refs[1:]) if last else (refs[:2], refs[2:])
    normed, refs = refs[: len(late)], refs[len(late) :]
    projecting = [half for half, *_ in late]
    if tick > 0:
        projecting.append(NEXT_CHIP)
    for half, half_ref in zip(projecting, refs):
        projected[half] = half_ref

    def write(m, lanes, values):
        for half in (CHIP, FAR):
            part = values[half * edge : (half + 1) * edge].astype(bf16)
            if last:
                for t in range(WIN):
                    outs[0][0, m, first_step(half) + t, :, lanes] = part[
                        t * stations : (t + 1) * stations
                    ]
            else:
                outs[half][m * edge : (m + 1) * edge, lanes] = part

    def rows_of(halves, m, at):
        return [projected[half][m * edge : (m + 1) * edge, at : at + HEAD] for half in halves]

    @pl.when(active)
    def _():
        lane = lax.broadcasted_iota(jnp.int32, (micro * edge, 128), 1)
        row = lax.broadcasted_iota(jnp.int32, (micro * edge, 128), 0)
        for (_, half_ref, line, complete), normed_ref in zip(late, normed):
            total = jnp.where(lane == row, line, 0.0)
            if not complete:
                for head in range(heads_dev):
                    part = half_ref[:, head * HEAD : (head + 1) * HEAD].astype(f32)
                    total = total + part * part
            factor = lax.rsqrt(jnp.sum(total, axis=1, keepdims=True) / (HEADS * HEAD) + EPS)
            normed_ref[...] = (half_ref[...].astype(f32) * factor).astype(bf16)
        if tick > 0:
            rows = micro * edge
            other = pl.multiple_of((1 - odd_device()) * rows, rows)
            normed.append(next_chip_ref.at[pl.ds(other, rows)])
        project_kernel(weights_ref, *normed, *[projected[half] for half in projecting])
        pairs = [(g, m) for g in range(heads_dev // GROUP) for m in range(micro)]
        blank = jnp.zeros((own, HEAD), bf16)
        scores = []
        for g, m in pairs:
            at = [(g * GROUP + j) * width for j in range(GROUP)]
            queries = [jnp.concatenate(rows_of((CHIP, FAR), m, a), axis=0) for a in at]
            spread = jnp.concatenate(
                [
                    jnp.concatenate(
                        [queries[j] if i == j else blank for i in range(GROUP)],
                        axis=1,
                    )
                    for j in range(GROUP)
                ],
                axis=0,
            )
            keys = jnp.concatenate(
                [jnp.concatenate(rows_of(range(4), m, a + HEAD), axis=0) for a in at], axis=1
            )
            scores.append(
                lax.dot_general(
                    keys, spread, (((1,), (1,)), ((), ())), preferred_element_type=f32
                )
                * (1.0 / math.sqrt(HEAD))
            )
        mixes = []
        for (g, m), score in zip(pairs, scores):
            time_weights = softmax_columns(score + time_ref[m])
            station_weights = softmax_columns(score[:own] + station_ref[m])
            mixes.append(jnp.concatenate([time_weights, station_weights], axis=0).T)
        for (g, m), mix in zip(pairs, mixes):
            for j in range(GROUP):
                head = g * GROUP + j
                at = head * width + 2 * HEAD
                mixed = jnp.dot(
                    mix[j * own : (j + 1) * own],
                    jnp.concatenate(rows_of((0, 1, 2, 3, CHIP, FAR), m, at), axis=0),
                    preferred_element_type=f32,
                )
                lanes = slice(head * HEAD, (head + 1) * HEAD)
                hidden = jnp.concatenate(
                    [ref[m * edge : (m + 1) * edge, lanes] for ref in (chip_ref, far_ref)], axis=0
                )
                result = hidden.astype(f32) + mixed
                write(m, lanes, result)

    @pl.when(jnp.logical_not(active))
    def _():
        for m in range(micro):
            for head in range(heads_dev):
                lanes = slice(head * HEAD, (head + 1) * HEAD)
                kept = [
                    ref[m * edge : (m + 1) * edge, lanes] for ref in (kept_chip_ref, kept_far_ref)
                ]
                write(m, lanes, jnp.concatenate(kept, axis=0).astype(f32))


def body(signal, head_proj, record_start, record_pad):
    section_count = lax.axis_size("section")
    seq_count = lax.axis_size("seq")
    rep_count = lax.axis_size("rep")
    micro, steps, stations, features = signal.shape
    heads_dev = head_proj.shape[1]
    edge = WIN * stations
    own, reach = 2 * edge, 4 * edge
    bf16, f32 = jnp.bfloat16, jnp.float32
    half_shape = jax.ShapeDtypeStruct((micro * edge, features), bf16)
    squares_shape = jax.ShapeDtypeStruct((8, 128), f32)
    projected_shape = jax.ShapeDtypeStruct((micro * edge, heads_dev * 3 * HEAD), bf16)
    signal_bytes = signal.size * 2

    def in_hbm(block):
        return pltpu.with_memory_space_constraint(block, pltpu.HBM)

    def squares_of(*halves):
        return pl.pallas_call(
            squares_kernel,
            in_specs=[VMEM] * len(halves),
            out_specs=VMEM,
            out_shape=squares_shape,
            compiler_params=PARAMS,
            name="squares",
        )(*halves)

    def normed(rows, squares, line):
        return pl.pallas_call(
            lambda *refs: norm_kernel(*refs, line=line),
            in_specs=[VMEM] * 3,
            out_specs=VMEM,
            out_shape=half_shape,
            compiler_params=PARAMS,
            cost_estimate=BUSY,
            name="norm",
        )(rows, squares_of(rows), squares)

    def again(*blocks):
        return pl.pallas_call(
            copy_kernel,
            in_specs=[VMEM] * len(blocks),
            out_specs=[VMEM] * len(blocks),
            out_shape=[jax.ShapeDtypeStruct(block.shape, block.dtype) for block in blocks],
            compiler_params=PARAMS,
            cost_estimate=BUSY,
            name="copy",
        )(*blocks)

    def project(*halves):
        return pl.pallas_call(
            project_kernel,
            in_specs=[VMEM] * (1 + len(halves)),
            out_specs=[VMEM] * len(halves),
            out_shape=[projected_shape] * len(halves),
            compiler_params=PARAMS,
            cost_estimate=BUSY,
            name="project",
        )(weights, *halves)

    chip, far = pl.pallas_call(
        halves_kernel,
        in_specs=[HBM],
        out_specs=[VMEM] * 2,
        out_shape=[half_shape] * 2,
        scratch_shapes=[pltpu.VMEM(signal.shape, bf16), pltpu.SemaphoreType.DMA],
        compiler_params=PARAMS,
        cost_estimate=cost(signal.size, 2 * signal_bytes),
        name="halves",
    )(in_hbm(signal))
    def moved(block, source, target, hop, other=False):
        route = []
        for i in range(seq_count):
            to = i if hop == 0 else i + 1 - 2 * (i % 2) if hop == 1 else i - 1 + 2 * (i % 2)
            if 0 <= to < seq_count:
                for r in range(rep_count):
                    route.append(
                        (
                            (source * seq_count + i) * rep_count + r,
                            (target * seq_count + to) * rep_count
                            + ((r + 1) % rep_count if other else r),
                        )
                    )
        return lax.ppermute(block, ("section", "seq", "rep"), route)

    next_far = moved(far, 0, 0, 2)
    next_chip = moved(chip, 0, 0, 1)
    squares = lax.all_gather(squares_of(chip, far, next_far, next_chip), "rep", tiled=True)
    weights, time_bias, station_bias = pl.pallas_call(
        lambda *refs: fixed_kernel(*refs, stations=stations, total_steps=steps * seq_count),
        in_specs=[HBM] * 3 + [VMEM],
        out_specs=[VMEM] * 3,
        out_shape=[
            jax.ShapeDtypeStruct(head_proj.shape, bf16),
            jax.ShapeDtypeStruct((micro, reach, GROUP * own), f32),
            jax.ShapeDtypeStruct((micro, own, GROUP * own), f32),
        ],
        scratch_shapes=[
            pltpu.SMEM(record_start.shape, jnp.int32),
            pltpu.SMEM(record_pad.shape, jnp.int32),
            pltpu.SemaphoreType.DMA((3,)),
        ],
        compiler_params=PARAMS,
        cost_estimate=cost(signal.size, 2 * head_proj.size),
        name="fixed",
    )(in_hbm(head_proj), in_hbm(record_start), in_hbm(record_pad), chip)
    inputs = (next_far, next_chip)
    kept = (chip, far)
    for tick in range(section_count):
        last = tick + 1 == section_count

        def kernel(*refs, tick=tick, last=last):
            layer_kernel(*refs, tick=tick, stations=stations, last=last)

        out_shape = (
            [jax.ShapeDtypeStruct((1,) + signal.shape, bf16)]
            if last
            else [half_shape, half_shape]
        )
        outputs = pl.pallas_call(
            kernel,
            in_specs=[VMEM] * (8 + len(inputs)),
            out_specs=[VMEM] * len(out_shape),
            out_shape=out_shape,
            scratch_shapes=[
                pltpu.VMEM(shape.shape, bf16)
                for shape, count in zip((half_shape, projected_shape), (4, 4) if tick == 0 else (2, 3))
                for _ in range(count)
            ],
            compiler_params=PARAMS,
            cost_estimate=cost(8 * signal.size * 3 * HEAD, 16 * signal_bytes),
            name="layer",
        )(
            chip, far, squares, time_bias, station_bias, weights, *kept, *inputs,
        )
        if last:
            return outputs[0]
        kept = outputs
        mine = squares_of(*kept)
        chip = moved(kept[0], tick, tick + 1, 0)
        next_far = moved(kept[1], tick, tick + 1, 2)
        squares = moved(mine, tick, tick + 1, 0, other=True)
        (mine_again,) = again(mine)
        far = moved(kept[1], tick, tick + 1, 0)
        far_squares = moved(mine_again, tick, tick + 1, 2, other=True)
        normed_chip = normed(chip, squares, CHIP)
        next_chip = lax.all_gather(
            normed_chip,
            "seq",
            axis_index_groups=[[i, i + 1] for i in range(0, seq_count, 2)],
            tiled=True,
        )
        far_squares = pl.pallas_call(
            add_kernel,
            in_specs=[VMEM] * 2,
            out_specs=VMEM,
            out_shape=squares_shape,
            compiler_params=PARAMS,
            cost_estimate=BUSY,
            name="add",
        )(squares_of(next_far), far_squares)
        inputs = (next_far, far_squares, next_chip, *project(normed_chip))


def solution(mesh):
    return jax.shard_map(
        body,
        mesh=mesh,
        in_specs=(P(None, "seq", None, "rep"), P("section", "rep", None, None), P(), P()),
        out_specs=P("section", None, "seq", None, "rep"),
        check_vma=False,
    )
```

```python
import math

import jax
import jax.numpy as jnp
from jax import lax
from jax.experimental import pallas as pl
from jax.experimental.pallas import tpu as pltpu
from jax.sharding import PartitionSpec as P

HEADS = 32
HEAD = 128
WIN = 4
GROUP = 4
EPS = 1e-06
BIG = 1e30
CHIP, FAR, NEXT_FAR, NEXT_CHIP = range(4)

HBM = pl.BlockSpec(memory_space=pltpu.HBM)
VMEM = pl.BlockSpec(memory_space=pltpu.VMEM)
BUSY = pl.CostEstimate(flops=2000000000, bytes_accessed=300000, transcendentals=0)
PARAMS = pltpu.CompilerParams(vmem_limit_bytes=16 * 1024 * 1024)


def cost(flops, moved):
    return pl.CostEstimate(flops=flops, bytes_accessed=moved, transcendentals=0)


def odd_device():
    return lax.axis_index("seq") % 2


def first_step(half):
    odd = odd_device()
    return {
        CHIP: WIN * (1 - odd),
        FAR: WIN * odd,
        NEXT_CHIP: 2 * WIN * (1 - odd) - WIN * odd,
        NEXT_FAR: 2 * WIN * odd - WIN * (1 - odd),
    }[half]


def same(count):
    return lax.broadcasted_iota(jnp.int32, (count, count), 0) == lax.broadcasted_iota(
        jnp.int32, (count, count), 1
    )


def squares_row(rows):
    gram = lax.dot_general(
        rows, rows, (((1,), (1,)), ((), ())), preferred_element_type=jnp.float32
    )
    return jnp.sum(jnp.where(same(rows.shape[0]), gram, 0.0), axis=0, keepdims=True)


def fill_masks(first_ref, pad_ref, time_ref, station_ref, stations, total_steps):
    own = 2 * WIN * stations
    keys, columns = 2 * own, GROUP * own
    key = lax.broadcasted_iota(jnp.int32, (keys, columns), 0)
    query = lax.broadcasted_iota(jnp.int32, (keys, columns), 1) % own

    def time_of(row):
        half, step = row // (WIN * stations), (row // stations) % WIN
        start = jnp.where(half == CHIP, first_step(CHIP), first_step(FAR))
        start = jnp.where(half == NEXT_CHIP, first_step(NEXT_CHIP), start)
        return step + jnp.where(half == NEXT_FAR, first_step(NEXT_FAR), start)

    key_station, query_station = key % stations, query % stations
    key_time, query_time = time_of(key), time_of(query)
    same_station = key_station == query_station
    same_time = key_time == query_time
    near = jnp.abs(key_time - query_time) <= WIN
    step = lax.axis_index("seq") * (2 * WIN) + key_time
    for m in range(time_ref.shape[0]):
        first = jnp.zeros((keys, columns), jnp.int32)
        pad = jnp.zeros((keys, columns), jnp.int32)
        for s in range(stations):
            first = jnp.where(key_station == s, first_ref[m, s], first)
            pad = jnp.where(key_station == s, pad_ref[m, s], pad)
        recorded = (step >= first) & (step < total_steps - pad)
        time_ref[m] = jnp.where(same_station & near & (recorded | same_time), 0.0, -BIG)
        station_ref[m] = jnp.where(same_time & (recorded | same_station), 0.0, -BIG)[:own]


def halves_kernel(signal_hbm, chip_ref, far_ref, signal_ref, arrived):
    copy = pltpu.make_async_copy(signal_hbm, signal_ref, arrived)
    copy.start()
    micro, _, stations, _ = signal_ref.shape
    edge = WIN * stations
    copy.wait()
    for half, half_ref in ((FAR, far_ref), (CHIP, chip_ref)):
        start = first_step(half)
        for m in range(micro):
            for t in range(0, WIN, 2):
                pair = [signal_ref[m, start + t + i].astype(jnp.float32) for i in range(2)]
                at = m * edge + t * stations
                half_ref[at : at + 2 * stations, :] = jnp.concatenate(pair, axis=0).astype(
                    jnp.bfloat16
                )


def fixed_kernel(
    weights_hbm, first_hbm, pad_hbm, _, weights_ref, time_ref, station_ref,
    first_ref, pad_ref, arrived, *, stations, total_steps,
):
    copies = [
        pltpu.make_async_copy(first_hbm, first_ref, arrived.at[0]),
        pltpu.make_async_copy(pad_hbm, pad_ref, arrived.at[1]),
        pltpu.make_async_copy(weights_hbm, weights_ref, arrived.at[2]),
    ]
    for copy in copies:
        copy.start()
    copies[0].wait()
    copies[1].wait()
    fill_masks(first_ref, pad_ref, time_ref, station_ref, stations, total_steps)
    copies[2].wait()


def squares_kernel(*refs):
    out_ref = refs[-1]
    out_ref[...] = jnp.zeros(out_ref.shape, jnp.float32)
    for half, half_ref in enumerate(refs[:-1]):
        out_ref[half : half + 1, 0 : half_ref.shape[0]] = squares_row(half_ref[...])


def scaled(rows, total):
    count = rows.shape[0]
    factor = lax.rsqrt(total / (HEADS * HEAD) + EPS)
    column = jnp.sum(jnp.where(same(count), factor, 0.0), axis=1, keepdims=True)
    return (rows.astype(jnp.float32) * column).astype(jnp.bfloat16)


def norm_kernel(half_ref, mine_ref, squares_ref, normed_ref, *, line):
    rows = half_ref[...]
    count = rows.shape[0]
    normed_ref[...] = scaled(rows, mine_ref[0:1, 0:count] + squares_ref[line : line + 1, 0:count])


def copy_kernel(*refs):
    count = len(refs) // 2
    for source, target in zip(refs[:count], refs[count:]):
        target[...] = source[...]


def add_kernel(mine_ref, other_ref, out_ref):
    out_ref[...] = jnp.zeros(out_ref.shape, jnp.float32)
    out_ref[0:1, :] = mine_ref[0:1, :] + other_ref[FAR : FAR + 1, :]


def project_kernel(weights_ref, *refs):
    count = len(refs) // 2
    halves, outs = refs[:count], refs[count:]
    rows = halves[0].shape[0]
    width = 3 * HEAD
    for head in range(weights_ref.shape[1]):
        lanes = slice(head * HEAD, (head + 1) * HEAD)
        projected = jnp.dot(
            jnp.concatenate([half[:, lanes] for half in halves], axis=0),
            weights_ref[0, head],
            preferred_element_type=jnp.float32,
        ).astype(jnp.bfloat16)
        for i, out in enumerate(outs):
            out[:, head * width : (head + 1) * width] = projected[i * rows : (i + 1) * rows]


def softmax_columns(scores):
    grown = jnp.exp(scores - jnp.max(scores, axis=0, keepdims=True))
    return (grown * (1.0 / jnp.sum(grown, axis=0, keepdims=True))).astype(jnp.bfloat16)


def layer_kernel(
    chip_ref, far_ref, squares_ref, time_ref, station_ref, weights_ref, kept_chip_ref, kept_far_ref,
    *refs, tick, stations, last,
):
    edge = WIN * stations
    micro = chip_ref.shape[0] // edge
    own = 2 * edge
    heads_dev = weights_ref.shape[1]
    width = 3 * HEAD
    bf16, f32 = jnp.bfloat16, jnp.float32
    active = lax.axis_index("section") == tick
    projected = [None] * 4
    if tick == 0:
        next_far_ref, next_chip_ref, *refs = refs
        late = [
            (
                half,
                half_ref,
                sum(squares_ref[i + half : i + half + 1, :] for i in range(0, squares_ref.shape[0], 8)),
                True,
            )
            for half, half_ref in enumerate((chip_ref, far_ref, next_far_ref, next_chip_ref))
        ]
    else:
        next_far_ref, far_squares_ref, next_chip_ref, projected[CHIP], *refs = refs
        late = [
            (FAR, far_ref, squares_ref[FAR : FAR + 1, :], False),
            (NEXT_FAR, next_far_ref, far_squares_ref[0:1, :], True),
        ]
    outs, refs = (refs[:1], refs[1:]) if last else (refs[:2], refs[2:])
    normed, refs = refs[: len(late)], refs[len(late) :]
    projecting = [half for half, *_ in late]
    if tick > 0:
        projecting.append(NEXT_CHIP)
    for half, half_ref in zip(projecting, refs):
        projected[half] = half_ref

    def write(m, lanes, values):
        for half in (CHIP, FAR):
            part = values[half * edge : (half + 1) * edge].astype(bf16)
            if last:
                for t in range(WIN):
                    outs[0][0, m, first_step(half) + t, :, lanes] = part[
                        t * stations : (t + 1) * stations
                    ]
            else:
                outs[half][m * edge : (m + 1) * edge, lanes] = part

    def rows_of(halves, m, at):
        return [projected[half][m * edge : (m + 1) * edge, at : at + HEAD] for half in halves]

    @pl.when(active)
    def _():
        lane = lax.broadcasted_iota(jnp.int32, (micro * edge, 128), 1)
        row = lax.broadcasted_iota(jnp.int32, (micro * edge, 128), 0)
        for (_, half_ref, line, complete), normed_ref in zip(late, normed):
            total = jnp.where(lane == row, line, 0.0)
            if not complete:
                for head in range(heads_dev):
                    part = half_ref[:, head * HEAD : (head + 1) * HEAD].astype(f32)
                    total = total + part * part
            factor = lax.rsqrt(jnp.sum(total, axis=1, keepdims=True) / (HEADS * HEAD) + EPS)
            normed_ref[...] = (half_ref[...].astype(f32) * factor).astype(bf16)
        if tick > 0:
            rows = micro * edge
            other = pl.multiple_of((1 - odd_device()) * rows, rows)
            normed.append(next_chip_ref.at[pl.ds(other, rows)])
        project_kernel(weights_ref, *normed, *[projected[half] for half in projecting])
        pairs = [(g, m) for g in range(heads_dev // GROUP) for m in range(micro)]
        blank = jnp.zeros((own, HEAD), bf16)
        scores = []
        for g, m in pairs:
            at = [(g * GROUP + j) * width for j in range(GROUP)]
            queries = [jnp.concatenate(rows_of((CHIP, FAR), m, a), axis=0) for a in at]
            spread = jnp.concatenate(
                [
                    jnp.concatenate(
                        [queries[j] if i == j else blank for i in range(GROUP)],
                        axis=1,
                    )
                    for j in range(GROUP)
                ],
                axis=0,
            )
            keys = jnp.concatenate(
                [jnp.concatenate(rows_of(range(4), m, a + HEAD), axis=0) for a in at], axis=1
            )
            scores.append(
                lax.dot_general(
                    keys, spread, (((1,), (1,)), ((), ())), preferred_element_type=f32
                )
                * (1.0 / math.sqrt(HEAD))
            )
        mixes = []
        for (g, m), score in zip(pairs, scores):
            time_weights = softmax_columns(score + time_ref[m])
            station_weights = softmax_columns(score[:own] + station_ref[m])
            mixes.append(jnp.concatenate([time_weights, station_weights], axis=0).T)
        for (g, m), mix in zip(pairs, mixes):
            for j in range(GROUP):
                head = g * GROUP + j
                at = head * width + 2 * HEAD
                mixed = jnp.dot(
                    mix[j * own : (j + 1) * own],
                    jnp.concatenate(rows_of((0, 1, 2, 3, CHIP, FAR), m, at), axis=0),
                    preferred_element_type=f32,
                )
                lanes = slice(head * HEAD, (head + 1) * HEAD)
                hidden = jnp.concatenate(
                    [ref[m * edge : (m + 1) * edge, lanes] for ref in (chip_ref, far_ref)], axis=0
                )
                result = hidden.astype(f32) + mixed
                write(m, lanes, result)

    @pl.when(jnp.logical_not(active))
    def _():
        for m in range(micro):
            for head in range(heads_dev):
                lanes = slice(head * HEAD, (head + 1) * HEAD)
                kept = [
                    ref[m * edge : (m + 1) * edge, lanes] for ref in (kept_chip_ref, kept_far_ref)
                ]
                write(m, lanes, jnp.concatenate(kept, axis=0).astype(f32))


def body(signal, head_proj, record_start, record_pad):
    section_count = lax.axis_size("section")
    seq_count = lax.axis_size("seq")
    rep_count = lax.axis_size("rep")
    micro, steps, stations, features = signal.shape
    heads_dev = head_proj.shape[1]
    edge = WIN * stations
    own, reach = 2 * edge, 4 * edge
    bf16, f32 = jnp.bfloat16, jnp.float32
    half_shape = jax.ShapeDtypeStruct((micro * edge, features), bf16)
    squares_shape = jax.ShapeDtypeStruct((8, 128), f32)
    projected_shape = jax.ShapeDtypeStruct((micro * edge, heads_dev * 3 * HEAD), bf16)
    signal_bytes = signal.size * 2

    def in_hbm(block):
        return pltpu.with_memory_space_constraint(block, pltpu.HBM)

    def squares_of(*halves):
        return pl.pallas_call(
            squares_kernel,
            in_specs=[VMEM] * len(halves),
            out_specs=VMEM,
            out_shape=squares_shape,
            compiler_params=PARAMS,
            name="squares",
        )(*halves)

    def normed(rows, squares, line):
        return pl.pallas_call(
            lambda *refs: norm_kernel(*refs, line=line),
            in_specs=[VMEM] * 3,
            out_specs=VMEM,
            out_shape=half_shape,
            compiler_params=PARAMS,
            cost_estimate=BUSY,
            name="norm",
        )(rows, squares_of(rows), squares)

    def again(*blocks):
        return pl.pallas_call(
            copy_kernel,
            in_specs=[VMEM] * len(blocks),
            out_specs=[VMEM] * len(blocks),
            out_shape=[jax.ShapeDtypeStruct(block.shape, block.dtype) for block in blocks],
            compiler_params=PARAMS,
            cost_estimate=BUSY,
            name="copy",
        )(*blocks)

    def project(half, after):
        return pl.pallas_call(
            lambda weights_ref, half_ref, _, out_ref: project_kernel(weights_ref, half_ref, out_ref),
            in_specs=[VMEM] * 3,
            out_specs=VMEM,
            out_shape=projected_shape,
            compiler_params=PARAMS,
            cost_estimate=BUSY,
            name="project",
        )(weights, half, after)

    chip, far = pl.pallas_call(
        halves_kernel,
        in_specs=[HBM],
        out_specs=[VMEM] * 2,
        out_shape=[half_shape] * 2,
        scratch_shapes=[pltpu.VMEM(signal.shape, bf16), pltpu.SemaphoreType.DMA],
        compiler_params=PARAMS,
        cost_estimate=cost(signal.size, 2 * signal_bytes),
        name="halves",
    )(in_hbm(signal))
    def moved(block, source, target, hop, other=False):
        route = []
        for i in range(seq_count):
            to = i if hop == 0 else i + 1 - 2 * (i % 2) if hop == 1 else i - 1 + 2 * (i % 2)
            if 0 <= to < seq_count:
                for r in range(rep_count):
                    route.append(
                        (
                            (source * seq_count + i) * rep_count + r,
                            (target * seq_count + to) * rep_count
                            + ((r + 1) % rep_count if other else r),
                        )
                    )
        return lax.ppermute(block, ("section", "seq", "rep"), route)

    next_far = moved(far, 0, 0, 2)
    next_chip = moved(chip, 0, 0, 1)
    squares = lax.all_gather(squares_of(chip, far, next_far, next_chip), "rep", tiled=True)
    weights, time_bias, station_bias = pl.pallas_call(
        lambda *refs: fixed_kernel(*refs, stations=stations, total_steps=steps * seq_count),
        in_specs=[HBM] * 3 + [VMEM],
        out_specs=[VMEM] * 3,
        out_shape=[
            jax.ShapeDtypeStruct(head_proj.shape, bf16),
            jax.ShapeDtypeStruct((micro, reach, GROUP * own), f32),
            jax.ShapeDtypeStruct((micro, own, GROUP * own), f32),
        ],
        scratch_shapes=[
            pltpu.SMEM(record_start.shape, jnp.int32),
            pltpu.SMEM(record_pad.shape, jnp.int32),
            pltpu.SemaphoreType.DMA((3,)),
        ],
        compiler_params=PARAMS,
        cost_estimate=cost(signal.size, 2 * head_proj.size),
        name="fixed",
    )(in_hbm(head_proj), in_hbm(record_start), in_hbm(record_pad), chip)
    inputs = (next_far, next_chip)
    kept = (chip, far)
    for tick in range(section_count):
        last = tick + 1 == section_count

        def kernel(*refs, tick=tick, last=last):
            layer_kernel(*refs, tick=tick, stations=stations, last=last)

        out_shape = (
            [jax.ShapeDtypeStruct((1,) + signal.shape, bf16)]
            if last
            else [half_shape, half_shape]
        )
        outputs = pl.pallas_call(
            kernel,
            in_specs=[VMEM] * (8 + len(inputs)),
            out_specs=[VMEM] * len(out_shape),
            out_shape=out_shape,
            scratch_shapes=[
                pltpu.VMEM(shape.shape, bf16)
                for shape, count in zip((half_shape, projected_shape), (4, 4) if tick == 0 else (2, 3))
                for _ in range(count)
            ],
            compiler_params=PARAMS,
            cost_estimate=cost(8 * signal.size * 3 * HEAD, 16 * signal_bytes),
            name="layer",
        )(
            chip, far, squares, time_bias, station_bias, weights, *kept, *inputs,
        )
        if last:
            return outputs[0]
        kept = outputs
        mine = squares_of(*kept)
        chip = moved(kept[0], tick, tick + 1, 0)
        next_far = moved(kept[1], tick, tick + 1, 2)
        squares = moved(mine, tick, tick + 1, 0, other=True)
        (mine_again,) = again(mine)
        far = moved(kept[1], tick, tick + 1, 0)
        far_squares = moved(mine_again, tick, tick + 1, 2, other=True)
        normed_chip = normed(chip, squares, CHIP)
        next_chip = lax.all_gather(
            normed_chip,
            "seq",
            axis_index_groups=[[i, i + 1] for i in range(0, seq_count, 2)],
            tiled=True,
        )
        far_squares = pl.pallas_call(
            add_kernel,
            in_specs=[VMEM] * 2,
            out_specs=VMEM,
            out_shape=squares_shape,
            compiler_params=PARAMS,
            cost_estimate=BUSY,
            name="add",
        )(squares_of(next_far), far_squares)
        inputs = (next_far, far_squares, next_chip, project(normed_chip, next_chip))


def solution(mesh):
    return jax.shard_map(
        body,
        mesh=mesh,
        in_specs=(P(None, "seq", None, "rep"), P("section", "rep", None, None), P(), P()),
        out_specs=P("section", None, "seq", None, "rep"),
        check_vma=False,
    )
```

```python
import math

import jax
import jax.numpy as jnp
from jax import lax
from jax.experimental import pallas as pl
from jax.experimental.pallas import tpu as pltpu
from jax.sharding import PartitionSpec as P

HEADS = 32
HEAD = 128
WIN = 4
GROUP = 4
EPS = 1e-06
BIG = 1e30
CHIP, FAR, NEXT_FAR, NEXT_CHIP = range(4)

HBM = pl.BlockSpec(memory_space=pltpu.HBM)
VMEM = pl.BlockSpec(memory_space=pltpu.VMEM)
BUSY = pl.CostEstimate(flops=2000000000, bytes_accessed=300000, transcendentals=0)
PARAMS = pltpu.CompilerParams(vmem_limit_bytes=16 * 1024 * 1024)


def cost(flops, moved):
    return pl.CostEstimate(flops=flops, bytes_accessed=moved, transcendentals=0)


def odd_device():
    return lax.axis_index("seq") % 2


def first_step(half):
    odd = odd_device()
    return {
        CHIP: WIN * (1 - odd),
        FAR: WIN * odd,
        NEXT_CHIP: 2 * WIN * (1 - odd) - WIN * odd,
        NEXT_FAR: 2 * WIN * odd - WIN * (1 - odd),
    }[half]


def same(count):
    return lax.broadcasted_iota(jnp.int32, (count, count), 0) == lax.broadcasted_iota(
        jnp.int32, (count, count), 1
    )


def squares_row(rows):
    gram = lax.dot_general(
        rows, rows, (((1,), (1,)), ((), ())), preferred_element_type=jnp.float32
    )
    return jnp.sum(jnp.where(same(rows.shape[0]), gram, 0.0), axis=0, keepdims=True)


def fill_masks(first_ref, pad_ref, time_ref, station_ref, stations, total_steps):
    own = 2 * WIN * stations
    keys, columns = 2 * own, GROUP * own
    key = lax.broadcasted_iota(jnp.int32, (keys, columns), 0)
    query = lax.broadcasted_iota(jnp.int32, (keys, columns), 1) % own

    def time_of(row):
        half, step = row // (WIN * stations), (row // stations) % WIN
        start = jnp.where(half == CHIP, first_step(CHIP), first_step(FAR))
        start = jnp.where(half == NEXT_CHIP, first_step(NEXT_CHIP), start)
        return step + jnp.where(half == NEXT_FAR, first_step(NEXT_FAR), start)

    key_station, query_station = key % stations, query % stations
    key_time, query_time = time_of(key), time_of(query)
    same_station = key_station == query_station
    same_time = key_time == query_time
    near = jnp.abs(key_time - query_time) <= WIN
    step = lax.axis_index("seq") * (2 * WIN) + key_time
    for m in range(time_ref.shape[0]):
        first = jnp.zeros((keys, columns), jnp.int32)
        pad = jnp.zeros((keys, columns), jnp.int32)
        for s in range(stations):
            first = jnp.where(key_station == s, first_ref[m, s], first)
            pad = jnp.where(key_station == s, pad_ref[m, s], pad)
        recorded = (step >= first) & (step < total_steps - pad)
        time_ref[m] = jnp.where(same_station & near & (recorded | same_time), 0.0, -BIG)
        station_ref[m] = jnp.where(same_time & (recorded | same_station), 0.0, -BIG)[:own]


def halves_kernel(signal_hbm, chip_ref, far_ref, signal_ref, arrived):
    copy = pltpu.make_async_copy(signal_hbm, signal_ref, arrived)
    copy.start()
    micro, _, stations, _ = signal_ref.shape
    edge = WIN * stations
    copy.wait()
    for half, half_ref in ((FAR, far_ref), (CHIP, chip_ref)):
        start = first_step(half)
        for m in range(micro):
            for t in range(0, WIN, 2):
                pair = [signal_ref[m, start + t + i].astype(jnp.float32) for i in range(2)]
                at = m * edge + t * stations
                half_ref[at : at + 2 * stations, :] = jnp.concatenate(pair, axis=0).astype(
                    jnp.bfloat16
                )


def fixed_kernel(
    weights_hbm, first_hbm, pad_hbm, _, weights_ref, time_ref, station_ref,
    first_ref, pad_ref, arrived, *, stations, total_steps,
):
    copies = [
        pltpu.make_async_copy(first_hbm, first_ref, arrived.at[0]),
        pltpu.make_async_copy(pad_hbm, pad_ref, arrived.at[1]),
        pltpu.make_async_copy(weights_hbm, weights_ref, arrived.at[2]),
    ]
    for copy in copies:
        copy.start()
    copies[0].wait()
    copies[1].wait()
    fill_masks(first_ref, pad_ref, time_ref, station_ref, stations, total_steps)
    copies[2].wait()


def squares_kernel(*refs):
    out_ref = refs[-1]
    out_ref[...] = jnp.zeros(out_ref.shape, jnp.float32)
    for half, half_ref in enumerate(refs[:-1]):
        out_ref[half : half + 1, 0 : half_ref.shape[0]] = squares_row(half_ref[...])


def scaled(rows, total):
    count = rows.shape[0]
    factor = lax.rsqrt(total / (HEADS * HEAD) + EPS)
    column = jnp.sum(jnp.where(same(count), factor, 0.0), axis=1, keepdims=True)
    return (rows.astype(jnp.float32) * column).astype(jnp.bfloat16)


def norm_kernel(half_ref, mine_ref, squares_ref, normed_ref, *, line):
    rows = half_ref[...]
    count = rows.shape[0]
    normed_ref[...] = scaled(rows, mine_ref[0:1, 0:count] + squares_ref[line : line + 1, 0:count])


def copy_kernel(*refs):
    count = len(refs) // 2
    for source, target in zip(refs[:count], refs[count:]):
        target[...] = source[...]


def add_kernel(mine_ref, other_ref, out_ref):
    out_ref[...] = jnp.zeros(out_ref.shape, jnp.float32)
    out_ref[0:1, :] = mine_ref[0:1, :] + other_ref[FAR : FAR + 1, :]


def project_kernel(weights_ref, *refs, start=0):
    count = len(refs) // 2
    halves, outs = refs[:count], refs[count:]
    rows = halves[0].shape[0]
    width = 3 * HEAD
    for head in range(weights_ref.shape[1]):
        lanes = slice(head * HEAD, (head + 1) * HEAD)
        projected = jnp.dot(
            jnp.concatenate([half[:, lanes] for half in halves], axis=0),
            weights_ref[0, head, :, start:],
            preferred_element_type=jnp.float32,
        ).astype(jnp.bfloat16)
        for i, out in enumerate(outs):
            out[:, head * width + start : (head + 1) * width] = projected[i * rows : (i + 1) * rows]


def softmax_columns(scores):
    grown = jnp.exp(scores - jnp.max(scores, axis=0, keepdims=True))
    return (grown * (1.0 / jnp.sum(grown, axis=0, keepdims=True))).astype(jnp.bfloat16)


def layer_kernel(
    chip_ref, far_ref, squares_ref, time_ref, station_ref, weights_ref, kept_chip_ref, kept_far_ref,
    *refs, tick, stations, last,
):
    edge = WIN * stations
    micro = chip_ref.shape[0] // edge
    own = 2 * edge
    heads_dev = weights_ref.shape[1]
    width = 3 * HEAD
    bf16, f32 = jnp.bfloat16, jnp.float32
    active = lax.axis_index("section") == tick
    projected = [None] * 4
    if tick == 0:
        next_far_ref, next_chip_ref, *refs = refs
        late = [
            (
                half,
                half_ref,
                sum(squares_ref[i + half : i + half + 1, :] for i in range(0, squares_ref.shape[0], 8)),
                True,
            )
            for half, half_ref in enumerate((chip_ref, far_ref, next_far_ref, next_chip_ref))
        ]
    else:
        next_far_ref, far_squares_ref, next_chip_ref, projected[CHIP], *refs = refs
        late = [
            (FAR, far_ref, squares_ref[FAR : FAR + 1, :], False),
            (NEXT_FAR, next_far_ref, far_squares_ref[0:1, :], True),
        ]
    outs, refs = (refs[:1], refs[1:]) if last else (refs[:2], refs[2:])
    normed, refs = refs[: len(late)], refs[len(late) :]
    projecting = [half for half, *_ in late]
    if tick > 0:
        projecting.append(NEXT_CHIP)
    for half, half_ref in zip(projecting, refs):
        projected[half] = half_ref

    def write(m, lanes, values):
        for half in (CHIP, FAR):
            part = values[half * edge : (half + 1) * edge].astype(bf16)
            if last:
                for t in range(WIN):
                    outs[0][0, m, first_step(half) + t, :, lanes] = part[
                        t * stations : (t + 1) * stations
                    ]
            else:
                outs[half][m * edge : (m + 1) * edge, lanes] = part

    def rows_of(halves, m, at):
        return [projected[half][m * edge : (m + 1) * edge, at : at + HEAD] for half in halves]

    @pl.when(active)
    def _():
        lane = lax.broadcasted_iota(jnp.int32, (micro * edge, 128), 1)
        row = lax.broadcasted_iota(jnp.int32, (micro * edge, 128), 0)
        for (_, half_ref, line, complete), normed_ref in zip(late, normed):
            total = jnp.where(lane == row, line, 0.0)
            if not complete:
                for head in range(heads_dev):
                    part = half_ref[:, head * HEAD : (head + 1) * HEAD].astype(f32)
                    total = total + part * part
            factor = lax.rsqrt(jnp.sum(total, axis=1, keepdims=True) / (HEADS * HEAD) + EPS)
            normed_ref[...] = (half_ref[...].astype(f32) * factor).astype(bf16)
        if tick > 0:
            rows = micro * edge
            other = pl.multiple_of((1 - odd_device()) * rows, rows)
            normed.append(next_chip_ref.at[pl.ds(other, rows)])
        for mine, start in ((True, 0), (False, HEAD)):
            chosen = [
                (normed_half, projected[half])
                for half, normed_half in zip(projecting, normed)
                if (half in (CHIP, FAR)) == mine
            ]
            project_kernel(
                weights_ref, *[a for a, _ in chosen], *[b for _, b in chosen], start=start
            )
        pairs = [(g, m) for g in range(heads_dev // GROUP) for m in range(micro)]
        blank = jnp.zeros((own, HEAD), bf16)
        scores = []
        for g, m in pairs:
            at = [(g * GROUP + j) * width for j in range(GROUP)]
            queries = [jnp.concatenate(rows_of((CHIP, FAR), m, a), axis=0) for a in at]
            spread = jnp.concatenate(
                [
                    jnp.concatenate(
                        [queries[j] if i == j else blank for i in range(GROUP)],
                        axis=1,
                    )
                    for j in range(GROUP)
                ],
                axis=0,
            )
            keys = jnp.concatenate(
                [jnp.concatenate(rows_of(range(4), m, a + HEAD), axis=0) for a in at], axis=1
            )
            scores.append(
                lax.dot_general(
                    keys, spread, (((1,), (1,)), ((), ())), preferred_element_type=f32
                )
                * (1.0 / math.sqrt(HEAD))
            )
        mixes = []
        for (g, m), score in zip(pairs, scores):
            time_weights = softmax_columns(score + time_ref[m])
            station_weights = softmax_columns(score[:own] + station_ref[m])
            mixes.append(jnp.concatenate([time_weights, station_weights], axis=0).T)
        for (g, m), mix in zip(pairs, mixes):
            for j in range(GROUP):
                head = g * GROUP + j
                at = head * width + 2 * HEAD
                mixed = jnp.dot(
                    mix[j * own : (j + 1) * own],
                    jnp.concatenate(rows_of((0, 1, 2, 3, CHIP, FAR), m, at), axis=0),
                    preferred_element_type=f32,
                )
                lanes = slice(head * HEAD, (head + 1) * HEAD)
                hidden = jnp.concatenate(
                    [ref[m * edge : (m + 1) * edge, lanes] for ref in (chip_ref, far_ref)], axis=0
                )
                result = hidden.astype(f32) + mixed
                write(m, lanes, result)

    @pl.when(jnp.logical_not(active))
    def _():
        for m in range(micro):
            for head in range(heads_dev):
                lanes = slice(head * HEAD, (head + 1) * HEAD)
                kept = [
                    ref[m * edge : (m + 1) * edge, lanes] for ref in (kept_chip_ref, kept_far_ref)
                ]
                write(m, lanes, jnp.concatenate(kept, axis=0).astype(f32))


def body(signal, head_proj, record_start, record_pad):
    section_count = lax.axis_size("section")
    seq_count = lax.axis_size("seq")
    rep_count = lax.axis_size("rep")
    micro, steps, stations, features = signal.shape
    heads_dev = head_proj.shape[1]
    edge = WIN * stations
    own, reach = 2 * edge, 4 * edge
    bf16, f32 = jnp.bfloat16, jnp.float32
    half_shape = jax.ShapeDtypeStruct((micro * edge, features), bf16)
    squares_shape = jax.ShapeDtypeStruct((8, 128), f32)
    projected_shape = jax.ShapeDtypeStruct((micro * edge, heads_dev * 3 * HEAD), bf16)
    signal_bytes = signal.size * 2

    def in_hbm(block):
        return pltpu.with_memory_space_constraint(block, pltpu.HBM)

    def squares_of(*halves):
        return pl.pallas_call(
            squares_kernel,
            in_specs=[VMEM] * len(halves),
            out_specs=VMEM,
            out_shape=squares_shape,
            compiler_params=PARAMS,
            name="squares",
        )(*halves)

    def normed(rows, squares, line):
        return pl.pallas_call(
            lambda *refs: norm_kernel(*refs, line=line),
            in_specs=[VMEM] * 3,
            out_specs=VMEM,
            out_shape=half_shape,
            compiler_params=PARAMS,
            cost_estimate=BUSY,
            name="norm",
        )(rows, squares_of(rows), squares)

    def again(*blocks):
        return pl.pallas_call(
            copy_kernel,
            in_specs=[VMEM] * len(blocks),
            out_specs=[VMEM] * len(blocks),
            out_shape=[jax.ShapeDtypeStruct(block.shape, block.dtype) for block in blocks],
            compiler_params=PARAMS,
            cost_estimate=BUSY,
            name="copy",
        )(*blocks)

    def project(half, after):
        return pl.pallas_call(
            lambda weights_ref, half_ref, _, out_ref: project_kernel(weights_ref, half_ref, out_ref),
            in_specs=[VMEM] * 3,
            out_specs=VMEM,
            out_shape=projected_shape,
            compiler_params=PARAMS,
            cost_estimate=BUSY,
            name="project",
        )(weights, half, after)

    chip, far = pl.pallas_call(
        halves_kernel,
        in_specs=[HBM],
        out_specs=[VMEM] * 2,
        out_shape=[half_shape] * 2,
        scratch_shapes=[pltpu.VMEM(signal.shape, bf16), pltpu.SemaphoreType.DMA],
        compiler_params=PARAMS,
        cost_estimate=cost(signal.size, 2 * signal_bytes),
        name="halves",
    )(in_hbm(signal))
    def moved(block, source, target, hop, other=False):
        route = []
        for i in range(seq_count):
            to = i if hop == 0 else i + 1 - 2 * (i % 2) if hop == 1 else i - 1 + 2 * (i % 2)
            if 0 <= to < seq_count:
                for r in range(rep_count):
                    route.append(
                        (
                            (source * seq_count + i) * rep_count + r,
                            (target * seq_count + to) * rep_count
                            + ((r + 1) % rep_count if other else r),
                        )
                    )
        return lax.ppermute(block, ("section", "seq", "rep"), route)

    next_far = moved(far, 0, 0, 2)
    next_chip = moved(chip, 0, 0, 1)
    squares = lax.all_gather(squares_of(chip, far, next_far, next_chip), "rep", tiled=True)
    weights, time_bias, station_bias = pl.pallas_call(
        lambda *refs: fixed_kernel(*refs, stations=stations, total_steps=steps * seq_count),
        in_specs=[HBM] * 3 + [VMEM],
        out_specs=[VMEM] * 3,
        out_shape=[
            jax.ShapeDtypeStruct(head_proj.shape, bf16),
            jax.ShapeDtypeStruct((micro, reach, GROUP * own), f32),
            jax.ShapeDtypeStruct((micro, own, GROUP * own), f32),
        ],
        scratch_shapes=[
            pltpu.SMEM(record_start.shape, jnp.int32),
            pltpu.SMEM(record_pad.shape, jnp.int32),
            pltpu.SemaphoreType.DMA((3,)),
        ],
        compiler_params=PARAMS,
        cost_estimate=cost(signal.size, 2 * head_proj.size),
        name="fixed",
    )(in_hbm(head_proj), in_hbm(record_start), in_hbm(record_pad), chip)
    inputs = (next_far, next_chip)
    kept = (chip, far)
    for tick in range(section_count):
        last = tick + 1 == section_count

        def kernel(*refs, tick=tick, last=last):
            layer_kernel(*refs, tick=tick, stations=stations, last=last)

        out_shape = (
            [jax.ShapeDtypeStruct((1,) + signal.shape, bf16)]
            if last
            else [half_shape, half_shape]
        )
        outputs = pl.pallas_call(
            kernel,
            in_specs=[VMEM] * (8 + len(inputs)),
            out_specs=[VMEM] * len(out_shape),
            out_shape=out_shape,
            scratch_shapes=[
                pltpu.VMEM(shape.shape, bf16)
                for shape, count in zip((half_shape, projected_shape), (4, 4) if tick == 0 else (2, 3))
                for _ in range(count)
            ],
            compiler_params=PARAMS,
            cost_estimate=cost(8 * signal.size * 3 * HEAD, 16 * signal_bytes),
            name="layer",
        )(
            chip, far, squares, time_bias, station_bias, weights, *kept, *inputs,
        )
        if last:
            return outputs[0]
        kept = outputs
        mine = squares_of(*kept)
        chip = moved(kept[0], tick, tick + 1, 0)
        next_far = moved(kept[1], tick, tick + 1, 2)
        squares = moved(mine, tick, tick + 1, 0, other=True)
        (mine_again,) = again(mine)
        far = moved(kept[1], tick, tick + 1, 0)
        far_squares = moved(mine_again, tick, tick + 1, 2, other=True)
        normed_chip = normed(chip, squares, CHIP)
        next_chip = lax.all_gather(
            normed_chip,
            "seq",
            axis_index_groups=[[i, i + 1] for i in range(0, seq_count, 2)],
            tiled=True,
        )
        far_squares = pl.pallas_call(
            add_kernel,
            in_specs=[VMEM] * 2,
            out_specs=VMEM,
            out_shape=squares_shape,
            compiler_params=PARAMS,
            cost_estimate=BUSY,
            name="add",
        )(squares_of(next_far), far_squares)
        inputs = (next_far, far_squares, next_chip, project(normed_chip, next_chip))


def solution(mesh):
    return jax.shard_map(
        body,
        mesh=mesh,
        in_specs=(P(None, "seq", None, "rep"), P("section", "rep", None, None), P(), P()),
        out_specs=P("section", None, "seq", None, "rep"),
        check_vma=False,
    )
```
